32 devices in a mesh: wide: 8 (over z, x), narrow: 4 (over y, core).
Axes of the slice: x: 2, y: 2, z: 4, core: 2. Of those that a mesh axis runs over, the one named last changes fastest.
Arguments:
- object_field: float32 [2, 2048, 2048], P(None, 'narrow', 'wide'), may hold values from -6 to 6
- probe: float32 [4, 2, 256, 256], replicated, may hold values from -3 to 3
- amplitudes: float32 [256, 256, 256], P(('wide', 'narrow')), may hold values from 0.5 to 4
- offsets: int32 [256, 2], P(('wide', 'narrow')), may hold values from 0 to 1792, as said below
- live: int32 [32], P(('wide', 'narrow')), may hold values from 1 to 8, as said below
Outputs:
- object_grad: float32 [2, 2048, 2048], P(None, 'narrow', 'wide')
- probe_grad: float32 [4, 2, 256, 256], replicated
The draws below stay inside these ranges and needn't reach their ends.
Inputs may be any that keep to these rules, and one draw needn't show every extreme that they name: `offsets`: the patch of every slot (used or not) lies wholly inside the object, and starts inside the object tile of 512 rows and 256 columns that holds the same mesh place as the slot: slot p with b = p // 8, row tile b % (2048 / 512) and column tile b // (2048 / 512). Block b of 8 slots uses its first live[b] slots; in every draw some block uses all 8.
All inputs are finite; a program needn't handle non-finite values.
Results may differ from the reference program's by a relative error of at most 0.005.
Values sent between devices are 32-bit elements; how exact they have to be, the bound alone decides.
No kernel may reach another device: no remote copies, remote signals or barrier semaphores. Data moves between devices by JAX's collectives and lax.ppermute only.
A program may use at most 128 MiB of HBM per device.

```python
import math
import jax
import jax.numpy as jnp
from jax import lax

M = 256
MODES = 4
TR = 512
TC = 256
CAP = 8
POSITIONS = 256
NR = 2048
NC = 2048


def draw_offsets(key, part):
    key = jax.random.fold_in(key, 11)
    number = jnp.arange(POSITIONS, dtype=jnp.int32)
    device = number // CAP
    narrow_count = NR // TR
    band = device % narrow_count
    column = device // narrow_count
    row_span = jnp.minimum(TR, NR - M - band * TR + 1)
    col_span = jnp.minimum(TC, NC - M - column * TC + 1)
    row_key, col_key = jax.random.split(key)
    rows = band * TR + jax.random.randint(row_key, (POSITIONS,), 0, row_span)
    cols = column * TC + jax.random.randint(col_key, (POSITIONS,), 0, col_span)
    return jnp.stack([rows, cols], 1).astype(jnp.int32)


def draw_live(key, part):
    key = jax.random.fold_in(key, 23)
    blocks = POSITIONS // CAP
    busy_key, count_key = jax.random.split(key)
    busiest = jax.random.randint(busy_key, (), 0, blocks)
    counts = jax.random.randint(count_key, (blocks,), 1, CAP // 2 + 1)
    return jnp.where(jnp.arange(blocks) == busiest, CAP, counts).astype(jnp.int32)


def block_scale(own_key, shape, cuts, smallest, high):
    factor_of, own = 1.0, jax.random.fold_in(own_key, 6)
    for axis_at, shards_of in cuts:
        heights = jnp.exp(jax.random.uniform(jax.random.fold_in(own, axis_at), (shards_of,), jnp.float32, smallest / len(cuts), high / len(cuts)))
        factor_of = factor_of * jnp.repeat(heights, shape[axis_at] // shards_of).reshape([-1 if axis == axis_at else 1 for axis in range(len(shape))])
    return factor_of


def normal_values(own_key, dims, deviation, most, pieces=(), kind=jnp.bfloat16):
    values = deviation * jax.random.normal(own_key, dims, jnp.float32)
    if pieces:
        values = values * block_scale(own_key, dims, pieces, -0.22, 0.18)
    return jnp.clip(values, -most, most).astype(kind)


def setup_inputs(seed: int = 0) -> dict:
    key_list = jax.random.split(jax.random.key(seed), 6)
    object_field = normal_values(key_list[0], (2, NR, NC), 1.0, 6.0, ((1, 4), (2, 8)), jnp.float32)
    probe = normal_values(key_list[1], (MODES, 2, M, M), 0.5, 3.0, (), jnp.float32)
    amplitudes = jnp.clip(jnp.exp(math.log(4.0) - 2.0794415 * jax.random.uniform(key_list[2], (POSITIONS, M, M), jnp.float32) ** block_scale(key_list[2], (POSITIONS, M, M), ((0, 32),), -0.2, 0.2)), 0.5, 4.0)
    offsets = draw_offsets(jax.random.fold_in(key_list[5], 71), 0)
    live = draw_live(jax.random.fold_in(key_list[5], 71), 0)
    return {"object_field": object_field, "probe": probe, "amplitudes": amplitudes, "offsets": offsets, "live": live}


def dft_blocks(extent):
    freq = jnp.arange(extent, dtype=jnp.int32)
    phases = freq[:, None] * freq[None, :] % extent
    angles = phases.astype(jnp.float32) * (2.0 * math.pi / extent)
    scale = 1.0 / math.sqrt(extent)
    cosine = jnp.cos(angles) * scale
    sine = jnp.sin(angles) * scale
    forward = jnp.concatenate([jnp.concatenate([cosine, sine], 1), jnp.concatenate([-sine, cosine], 1)], 0)
    backward = jnp.concatenate([jnp.concatenate([cosine, -sine], 1), jnp.concatenate([sine, cosine], 1)], 0)
    return (forward.astype(jnp.bfloat16), backward.astype(jnp.bfloat16))

def left_apply(block, waves):
    modes = waves.shape[0]
    extent = waves.shape[2]
    stacked = waves.reshape(modes, 2 * extent, waves.shape[3]).astype(jnp.float32)
    result = jnp.einsum('ab,kbc->kac', block.astype(jnp.float32), stacked, precision=lax.Precision.HIGHEST)
    return result.reshape(modes, 2, extent, waves.shape[3])

def slot_gradients(window, probe, amplitude, forward, backward):
    probe_re = probe[:, 0]
    probe_im = probe[:, 1]
    object_re = window[0]
    object_im = window[1]
    waves = jnp.stack([probe_re * object_re - probe_im * object_im, probe_re * object_im + probe_im * object_re], 1).astype(jnp.bfloat16)
    inner = left_apply(forward, waves).astype(jnp.bfloat16)
    far_turned = left_apply(forward, jnp.swapaxes(inner, 2, 3))
    intensity = lax.optimization_barrier(jnp.sum(far_turned * far_turned, axis=(0, 1)))
    factor = 2.0 * (1.0 - amplitude.T / jnp.sqrt(intensity + 0.5))
    grad_turned = (factor * far_turned).astype(jnp.bfloat16)
    across = left_apply(backward, grad_turned).astype(jnp.bfloat16)
    wave_grad = left_apply(backward, jnp.swapaxes(across, 2, 3))
    grad_re = wave_grad[:, 0]
    grad_im = wave_grad[:, 1]
    object_part = jnp.stack([lax.optimization_barrier(jnp.sum(probe_re * grad_re + probe_im * grad_im, 0)), lax.optimization_barrier(jnp.sum(probe_re * grad_im - probe_im * grad_re, 0))], 0)
    probe_part = jnp.stack([object_re * grad_re + object_im * grad_im, object_re * grad_im - object_im * grad_re], 1)
    return (object_part, probe_part)

def reference(object_field, probe, amplitudes, offsets, live):
    forward, backward = dft_blocks(M)
    anchor = jnp.zeros((), jnp.int32)

    def visit(number, carry):

        def active(state):
            gradient, probe_sum = state
            row_at = offsets[number, 0].astype(jnp.int32)
            col_at = offsets[number, 1].astype(jnp.int32)
            window = lax.dynamic_slice(object_field, (anchor, row_at, col_at), (2, M, M))
            object_part, probe_part = slot_gradients(window, probe, amplitudes[number], forward, backward)
            before = lax.dynamic_slice(gradient, (anchor, row_at, col_at), (2, M, M))
            gradient = lax.dynamic_update_slice(gradient, before + object_part, (anchor, row_at, col_at))
            return (gradient, probe_sum + probe_part)

        def passive(state):
            return state
        return lax.cond(number % CAP < live[number // CAP], active, passive, carry)
    start = (jnp.zeros(object_field.shape, jnp.float32), jnp.zeros(probe.shape, jnp.float32))
    gradient, probe_sum = lax.fori_loop(0, POSITIONS, visit, start)
    return (gradient, probe_sum / math.sqrt(POSITIONS))
```

```python
import functools
import math

import jax
import jax.numpy as jnp
import ml_dtypes
import numpy as np
from jax import lax
from jax.experimental import pallas as pl
from jax.experimental.pallas import tpu as pltpu
from jax.sharding import PartitionSpec as P

F32 = jnp.float32
BF16 = jnp.bfloat16
LANES = 128


def half_dft(extent):
    half = extent // 2
    blocks = []
    for parity in range(2):
        freq = 2 * np.arange(half)[:, None] + parity
        angles = (freq * np.arange(half)[None, :] % extent) * (2.0 * math.pi / extent)
        cosine = np.cos(angles) / math.sqrt(extent)
        sine = np.sin(angles) / math.sqrt(extent)
        blocks.append(np.block([[cosine, sine], [-sine, cosine]]))
    both = np.stack(blocks)
    return np.stack([both, np.swapaxes(both, 1, 2)]).astype(ml_dtypes.bfloat16)


def parity_order(extent):
    order = np.concatenate([np.arange(0, extent, 2), np.arange(1, extent, 2)])
    matrix = np.zeros((extent, extent), np.float32)
    matrix[order, np.arange(extent)] = 1.0
    return matrix


def dot(a, b):
    return jnp.dot(a, b, preferred_element_type=F32)


def slots_kernel(
    tile_rows, tile_cols, offsets, live, own, below, right, corner, probe, amps, mats,
    grad_own, grad_below, grad_right, grad_corner, probe_sum,
    ext, grad, window, part, amp, waves, inner, far, power, across, in_sems, amp_sems, out_sems,
):
    modes = probe.shape[0]
    extent = probe.shape[2]
    half = extent // 2
    rows_step = 32
    count = live[0]

    pieces = [
        (own, grad_own, slice(0, tile_rows), slice(0, tile_cols)),
        (below, grad_below, slice(tile_rows, tile_rows + extent), slice(0, tile_cols)),
        (right, grad_right, slice(0, tile_rows), slice(tile_cols, tile_cols + extent)),
        (corner, grad_corner, slice(tile_rows, tile_rows + extent), slice(tile_cols, tile_cols + extent)),
    ]
    loads = [
        pltpu.make_async_copy(src, ext.at[:, rows, cols], in_sems.at[n])
        for n, (src, _, rows, cols) in enumerate(pieces)
    ]
    for load in loads:
        load.start()

    def amp_copy(number, place):
        return pltpu.make_async_copy(amps.at[number], amp.at[place], amp_sems.at[place])

    amp_copy(0, 0).start()
    grad[...] = jnp.zeros_like(grad)
    probe_sum[...] = jnp.zeros_like(probe_sum)
    for load in loads:
        load.wait()
    groups = rows_step // 8
    lane = lax.broadcasted_iota(jnp.int32, (rows_step, LANES), 1)
    lane3 = lax.broadcasted_iota(jnp.int32, (groups + 1, 8, LANES), 2)
    sublane = lax.broadcasted_iota(jnp.int32, (groups, 8, LANES), 1)
    sublane_tall = lax.broadcasted_iota(jnp.int32, (groups + 1, 8, LANES), 1)

    @pl.loop(0, count)
    def _(number):
        place = lax.rem(number, 2)

        @pl.when(number + 1 < count)
        def _():
            amp_copy(number + 1, 1 - place).start()

        row_at = lax.rem(offsets[number, 0], tile_rows)
        col_at = lax.rem(offsets[number, 1], tile_cols)
        shift = lax.rem(col_at, LANES)
        col_base = pl.multiple_of(col_at - shift, LANES)
        back = lax.rem(LANES - shift, LANES)
        wide_cols = extent // LANES + 1
        row_shift = lax.rem(row_at, 8)
        row_base = pl.multiple_of(row_at - row_shift, 8)
        row_back = lax.rem(8 - row_shift, 8)

        for plane in range(2):
            for row in range(0, extent, rows_step):
                turned = []
                for c in range(wide_cols):
                    tall = ext[plane, pl.ds(row_base + row, rows_step + 8), pl.ds(col_base + LANES * c, LANES)]
                    tall = pltpu.roll(tall.reshape(groups + 1, 8, LANES), row_back, 1)
                    flat = jnp.where(sublane < 8 - row_shift, tall[:-1], tall[1:]).reshape(rows_step, LANES)
                    turned.append(pltpu.roll(flat, back, 1))
                for c in range(wide_cols - 1):
                    window[plane, row : row + rows_step, c * LANES : (c + 1) * LANES] = jnp.where(
                        lane < LANES - shift, turned[c], turned[c + 1]
                    )

        for k in range(modes):
            for row in range(0, half, rows_step):
                waves_at = []
                for base in (row, half + row):
                    rows = slice(base, base + rows_step)
                    pr, pi = probe[k, 0, rows, :], probe[k, 1, rows, :]
                    o_re, o_im = window[0, rows, :], window[1, rows, :]
                    waves_at.append((pr * o_re - pi * o_im, pr * o_im + pi * o_re))
                for c in range(2):
                    rows = slice(c * half + row, c * half + row + rows_step)
                    waves[k, 0, rows, :] = (waves_at[0][c] + waves_at[1][c]).astype(BF16)
                    waves[k, 1, rows, :] = (waves_at[0][c] - waves_at[1][c]).astype(BF16)
            for a in range(2):
                z = dot(mats[0, a], waves[k, a])
                left, right_half = z[:, :half], z[:, half:]
                for b, value in enumerate((left + right_half, left - right_half)):
                    value = value.astype(BF16)
                    inner[k, b, a * half : (a + 1) * half, :half] = value[:half]
                    inner[k, b, a * half : (a + 1) * half, half:] = value[half:]
            for b in range(2):
                f = dot(inner[k, b], mats[1, b])
                far[k, b] = f
                own_power = f[:, :half] * f[:, :half] + f[:, half:] * f[:, half:]
                power[b] = own_power if k == 0 else power[b] + own_power

        amp_copy(number, place).wait()
        for b in range(2):
            power[b] = 2.0 - 2.0 * amp[place, :, b * half : (b + 1) * half] * lax.rsqrt(power[b] + 0.5)

        for k in range(modes):
            ys = []
            for b in range(2):
                factor = power[b]
                g = jnp.concatenate([far[k, b, :, :half] * factor, far[k, b, :, half:] * factor], 1)
                ys.append(dot(g.astype(BF16), mats[0, b]))
            for side, y in enumerate((ys[0] + ys[1], ys[0] - ys[1])):
                y = y.astype(BF16)
                cols = slice(side * half, (side + 1) * half)
                for a in range(2):
                    rows = slice(a * half, (a + 1) * half)
                    across[k, a, :half, cols] = y[rows, :half]
                    across[k, a, half:, cols] = y[rows, half:]
            v0 = dot(mats[1, 0], across[k, 0])
            v1 = dot(mats[1, 1], across[k, 1])
            for side, v in enumerate((v0 + v1, v0 - v1)):
                rows = slice(side * half, (side + 1) * half)
                g_re, g_im = v[:half], v[half:]
                pr, pi = probe[k, 0, rows, :], probe[k, 1, rows, :]
                o_re, o_im = window[0, rows, :], window[1, rows, :]
                add_re = pr * g_re + pi * g_im
                add_im = pr * g_im - pi * g_re
                part[0, rows, :] = add_re if k == 0 else part[0, rows, :] + add_re
                part[1, rows, :] = add_im if k == 0 else part[1, rows, :] + add_im
                probe_sum[k, 0, rows, :] += o_re * g_re + o_im * g_im
                probe_sum[k, 1, rows, :] += o_re * g_im - o_im * g_re

        zero = jnp.zeros((groups + 1, 8, LANES), F32)
        edge = jnp.zeros((1, 8, LANES), F32)
        for plane in range(2):
            for row in range(0, extent, rows_step):
                turned = []
                for c in range(wide_cols - 1):
                    flat = part[plane, row : row + rows_step, c * LANES : (c + 1) * LANES]
                    flat = pltpu.roll(flat, shift, 1).reshape(groups, 8, LANES)
                    flat = pltpu.roll(flat, row_shift, 1)
                    low = jnp.concatenate([flat, edge], 0)
                    high = jnp.concatenate([edge, flat], 0)
                    turned.append(jnp.where(sublane_tall >= row_shift, low, high))
                turned = [zero] + turned + [zero]
                for c in range(wide_cols):
                    at = (plane, pl.ds(row_base + row, rows_step + 8), pl.ds(col_base + LANES * c, LANES))
                    value = jnp.where(lane3 >= shift, turned[c + 1], turned[c])
                    grad[at] += value.reshape(rows_step + 8, LANES)

    stores = [
        pltpu.make_async_copy(grad.at[:, rows, cols], dst, out_sems.at[n])
        for n, (_, dst, rows, cols) in enumerate(pieces)
    ]
    for store in stores:
        store.start()
    for store in stores:
        store.wait()


def run_slots(offsets, live, own, below, right, corner, probe, amps):
    extent = probe.shape[2]
    modes = probe.shape[0]
    tile_rows, tile_cols = own.shape[1:]
    mats = jnp.asarray(half_dft(extent))
    smem = pl.BlockSpec(memory_space=pltpu.SMEM)
    vmem = pl.BlockSpec(memory_space=pltpu.VMEM)
    hbm = pl.BlockSpec(memory_space=pl.ANY)
    shape = jax.ShapeDtypeStruct
    return pl.pallas_call(
        functools.partial(slots_kernel, tile_rows, tile_cols),
        out_shape=[shape(v.shape, F32) for v in (own, below, right, corner, probe)],
        in_specs=[smem, smem, hbm, hbm, hbm, hbm, vmem, hbm, vmem],
        out_specs=[hbm, hbm, hbm, hbm, vmem],
        scratch_shapes=[
            pltpu.VMEM((2, tile_rows + extent, tile_cols + extent), F32),
            pltpu.VMEM((2, tile_rows + extent, tile_cols + extent), F32),
            pltpu.VMEM((2, extent, extent), F32),
            pltpu.VMEM((2, extent, extent), F32),
            pltpu.VMEM((2, extent, extent), F32),
            pltpu.VMEM((modes, 2, extent, extent), BF16),
            pltpu.VMEM((modes, 2, extent, extent), BF16),
            pltpu.VMEM((modes, 2, extent, extent), F32),
            pltpu.VMEM((2, extent, extent // 2), F32),
            pltpu.VMEM((modes, 2, extent, extent), BF16),
            pltpu.SemaphoreType.DMA((4,)),
            pltpu.SemaphoreType.DMA((2,)),
            pltpu.SemaphoreType.DMA((4,)),
        ],
        compiler_params=pltpu.CompilerParams(vmem_limit_bytes=48 * 1024 * 1024),
        name="slots",
    )(offsets, live, own, below, right, corner, probe, amps, mats)


def shifted(value, axis, steps):
    count = lax.axis_size(axis)
    first, last = (max(0, -steps), min(count, count - steps))
    return lax.ppermute(value, axis, [(source, source + steps) for source in range(first, last)])


def swapped(value, axis, bit):
    count = lax.axis_size(axis)
    return lax.ppermute(value, axis, [(source, source ^ bit) for source in range(count)])


def halve(value, axis, bit):
    upper = (lax.axis_index(axis) & bit) != 0
    low, high = jnp.split(value, 2, 0)
    came = swapped(jnp.where(upper, low, high), axis, bit)
    return jnp.where(upper, high, low) + came


def double(value, axis, bit):
    upper = (lax.axis_index(axis) & bit) != 0
    came = swapped(value, axis, bit)
    return jnp.concatenate([jnp.where(upper, came, value), jnp.where(upper, value, came)], 0)


def sum_everywhere(value):
    narrow = [("narrow", 1 << n) for n in range(lax.axis_size("narrow").bit_length() - 1)]
    wide = [("wide", 1 << n) for n in range(lax.axis_size("wide").bit_length() - 1)]
    first, rest = narrow[0], narrow[1:] + wide
    turning, last = rest[:3], rest[3:]
    value = halve(value, *first)
    unit = value.shape[0] // 8
    parts = jnp.split(value, [3 * unit, 6 * unit], 0)
    orders = [turning[n:] + turning[:n] + last for n in range(3)]
    for step in range(len(rest)):
        parts = [halve(part, *order[step]) for part, order in zip(parts, orders)]
    for step in reversed(range(len(rest))):
        parts = [double(part, *order[step]) for part, order in zip(parts, orders)]
    return double(jnp.concatenate(parts, 0), *first)


def on_device(object_field, probe, amplitudes, offsets, live):
    extent = probe.shape[2]
    order = jnp.asarray(parity_order(extent))
    amps = jnp.einsum("rq,prc,cd->pqd", order, amplitudes, order, precision=lax.Precision.HIGHEST)
    right = shifted(object_field[:, :, :extent], "wide", -1)
    below = shifted(object_field[:, :extent, :], "narrow", -1)
    corner = shifted(right[:, :extent, :], "narrow", -1)
    grad_own, grad_below, grad_right, grad_corner, probe_sum = run_slots(
        offsets, live, object_field, below, right, corner, probe, amps
    )
    total_slots = lax.axis_size("wide") * lax.axis_size("narrow") * offsets.shape[0]
    scaled = (probe_sum / math.sqrt(total_slots)).reshape(-1, extent)
    probe_grad = sum_everywhere(scaled).reshape(probe.shape)
    came_below = shifted(grad_below, "narrow", 1)
    came_corner = shifted(grad_corner, "narrow", 1)
    came_right = shifted(grad_right.at[:, :extent, :].add(came_corner), "wide", 1)
    object_grad = grad_own.at[:, :extent, :].add(came_below).at[:, :, :extent].add(came_right)
    return (object_grad, probe_grad)


def solution(mesh):
    return jax.shard_map(
        on_device,
        mesh=mesh,
        in_specs=(
            P(None, "narrow", "wide"),
            P(),
            P(("wide", "narrow"), None, None),
            P(("wide", "narrow"), None),
            P(("wide", "narrow")),
        ),
        out_specs=(P(None, "narrow", "wide"), P()),
        check_vma=False,
    )
```

```python
import functools
import math

import jax
import jax.numpy as jnp
import ml_dtypes
import numpy as np
from jax import lax
from jax.experimental import pallas as pl
from jax.experimental.pallas import tpu as pltpu
from jax.sharding import PartitionSpec as P

F32 = jnp.float32
BF16 = jnp.bfloat16
LANES = 128


def half_dft(extent):
    half = extent // 2
    blocks = []
    for parity in range(2):
        freq = 2 * np.arange(half)[:, None] + parity
        angles = (freq * np.arange(half)[None, :] % extent) * (2.0 * math.pi / extent)
        cosine = np.cos(angles) / math.sqrt(extent)
        sine = np.sin(angles) / math.sqrt(extent)
        blocks.append(np.block([[cosine, sine], [-sine, cosine]]))
    both = np.stack(blocks)
    return np.stack([both, np.swapaxes(both, 1, 2)]).astype(ml_dtypes.bfloat16)


def parity_order(extent):
    order = np.concatenate([np.arange(0, extent, 2), np.arange(1, extent, 2)])
    matrix = np.zeros((extent, extent), np.float32)
    matrix[order, np.arange(extent)] = 1.0
    return matrix


def dot(a, b):
    return jnp.dot(a, b, preferred_element_type=F32)


def slots_kernel(
    late, tile_rows, tile_cols, offsets, live, *refs,
):
    pieces = refs[: 8 if late else 5]
    refs = refs[len(pieces) :]
    if late:
        grad_so_far, probe_so_far, probe, amps, mats, order = refs[:6]
        grad_own, grad_below, grad_right, grad_right_low, grad_corner, probe_keep, probe_send = refs[6:13]
        refs = refs[13:]
    else:
        probe, amps, mats, order, grad_out, probe_out = refs[:6]
        refs = refs[6:]
    ext, grad, probe_sum, window, part, amp, sorted_amp, waves, inner, far, power, across, in_sems, amp_sem, out_sems = refs
    modes = probe.shape[0]
    extent = probe.shape[2]
    half = extent // 2
    rows_step = 32
    groups = rows_step // 8
    count = live[0]

    low_rows = slice(tile_rows, tile_rows + extent)
    first = slice(tile_cols, tile_cols + LANES)
    second = slice(tile_cols + LANES, tile_cols + extent)
    places = [(slice(0, tile_rows), slice(0, tile_cols)), (low_rows, slice(0, tile_cols))]
    for cols in (first, second):
        places += [(slice(0, extent), cols), (slice(extent, tile_rows), cols), (low_rows, cols)]
    loads = [
        pltpu.make_async_copy(src, ext.at[:, rows, cols], in_sems.at[n])
        for n, (src, (rows, cols)) in enumerate(zip(pieces, places))
    ]
    if late:
        loads.append(pltpu.make_async_copy(grad_so_far, grad, in_sems.at[len(pieces)]))
        loads.append(pltpu.make_async_copy(probe_so_far, probe_sum, in_sems.at[len(pieces) + 1]))
    for load in loads:
        load.start()
    if not late:
        grad[...] = jnp.zeros_like(grad)
        probe_sum[...] = jnp.zeros_like(probe_sum)
    for load in loads:
        load.wait()
    lane = lax.broadcasted_iota(jnp.int32, (rows_step, LANES), 1)
    lane3 = lax.broadcasted_iota(jnp.int32, (groups + 1, 8, LANES), 2)
    sublane = lax.broadcasted_iota(jnp.int32, (groups, 8, LANES), 1)
    sublane_tall = lax.broadcasted_iota(jnp.int32, (groups + 1, 8, LANES), 1)

    def rows_of(k, c, rows):
        start = (k * 2 + c) * extent
        return slice(start + rows.start, start + rows.stop)

    def visit(number, row_at, col_at):
        amp_load = pltpu.make_async_copy(amps.at[number], amp, amp_sem)
        amp_load.start()
        shift = lax.rem(col_at, LANES)
        col_base = pl.multiple_of(col_at - shift, LANES)
        back = lax.rem(LANES - shift, LANES)
        wide_cols = extent // LANES + 1
        row_shift = lax.rem(row_at, 8)
        row_base = pl.multiple_of(row_at - row_shift, 8)
        row_back = lax.rem(8 - row_shift, 8)

        for plane in range(2):
            for row in range(0, extent, rows_step):
                turned = []
                for c in range(wide_cols):
                    tall = ext[plane, pl.ds(row_base + row, rows_step + 8), pl.ds(col_base + LANES * c, LANES)]
                    tall = pltpu.roll(tall.reshape(groups + 1, 8, LANES), row_back, 1)
                    flat = jnp.where(sublane < 8 - row_shift, tall[:-1], tall[1:]).reshape(rows_step, LANES)
                    turned.append(pltpu.roll(flat, back, 1))
                for c in range(wide_cols - 1):
                    window[plane, row : row + rows_step, c * LANES : (c + 1) * LANES] = jnp.where(
                        lane < LANES - shift, turned[c], turned[c + 1]
                    )


        def psi(k, step=rows_step):
            for row in range(0, half, step):
                waves_at = []
                for base in (row, half + row):
                    rows = slice(base, base + step)
                    pr, pi = probe[k, 0, rows, :], probe[k, 1, rows, :]
                    o_re, o_im = window[0, rows, :], window[1, rows, :]
                    waves_at.append((pr * o_re - pi * o_im, pr * o_im + pi * o_re))
                for c in range(2):
                    rows = slice(c * half + row, c * half + row + step)
                    waves[k, 0, rows, :] = (waves_at[0][c] + waves_at[1][c]).astype(BF16)
                    waves[k, 1, rows, :] = (waves_at[0][c] - waves_at[1][c]).astype(BF16)

        def left(k):
            for a in range(2):
                z = dot(mats[0, a], waves[k, a])
                left, right_half = z[:, :half], z[:, half:]
                for b, value in enumerate((left + right_half, left - right_half)):
                    value = value.astype(BF16)
                    inner[k, b, a * half : (a + 1) * half, :half] = value[:half]
                    inner[k, b, a * half : (a + 1) * half, half:] = value[half:]

        def right(k):
            for b in range(2):
                f = dot(inner[k, b], mats[1, b])
                far[k, b] = f
                own_power = f[:, :half] * f[:, :half] + f[:, half:] * f[:, half:]
                power[b] = own_power if k == 0 else power[b] + own_power

        def factors():
            amp_load.wait()
            high = amp[...].astype(BF16)
            low = (amp[...] - high.astype(F32)).astype(BF16)
            turned = dot(high, order[...]) + dot(low, order[...])
            for b in range(2):
                sorted_amp[b] = turned[:, b * half : (b + 1) * half]
            for b in range(2):
                for a in range(2):
                    rows = slice(a * half, (a + 1) * half)
                    for_rows = sorted_amp[b, pl.ds(a, half, 2), :]
                    power[b, rows] = 2.0 - 2.0 * for_rows * lax.rsqrt(power[b, rows] + 0.5)

        def back_right(k):
            ys = []
            for b in range(2):
                factor = power[b]
                g = jnp.concatenate([far[k, b, :, :half] * factor, far[k, b, :, half:] * factor], 1)
                ys.append(dot(g.astype(BF16), mats[0, b]))
            for side, y in enumerate((ys[0] + ys[1], ys[0] - ys[1])):
                y = y.astype(BF16)
                cols = slice(side * half, (side + 1) * half)
                for a in range(2):
                    rows = slice(a * half, (a + 1) * half)
                    across[k, a, :half, cols] = y[rows, :half]
                    across[k, a, half:, cols] = y[rows, half:]

        def back_left(k):
            v0 = dot(mats[1, 0], across[k, 0])
            v1 = dot(mats[1, 1], across[k, 1])
            for side, v in enumerate((v0 + v1, v0 - v1)):
                rows = slice(side * half, (side + 1) * half)
                g_re, g_im = v[:half], v[half:]
                pr, pi = probe[k, 0, rows, :], probe[k, 1, rows, :]
                o_re, o_im = window[0, rows, :], window[1, rows, :]
                add_re = pr * g_re + pi * g_im
                add_im = pr * g_im - pi * g_re
                part[0, rows, :] = add_re if k == 0 else part[0, rows, :] + add_re
                part[1, rows, :] = add_im if k == 0 else part[1, rows, :] + add_im
                probe_sum[rows_of(k, 0, rows), :] += o_re * g_re + o_im * g_im
                probe_sum[rows_of(k, 1, rows), :] += o_re * g_im - o_im * g_re

        for stage in (psi, left, right):
            for k in range(modes):
                stage(k)
        factors()
        for stage in (back_right, back_left):
            for k in range(modes):
                stage(k)

        zero = jnp.zeros((groups + 1, 8, LANES), F32)
        edge = jnp.zeros((1, 8, LANES), F32)
        for plane in range(2):
            for row in range(0, extent, rows_step):
                turned = []
                for c in range(wide_cols - 1):
                    flat = part[plane, row : row + rows_step, c * LANES : (c + 1) * LANES]
                    flat = pltpu.roll(flat, shift, 1).reshape(groups, 8, LANES)
                    flat = pltpu.roll(flat, row_shift, 1)
                    low = jnp.concatenate([flat, edge], 0)
                    high = jnp.concatenate([edge, flat], 0)
                    turned.append(jnp.where(sublane_tall >= row_shift, low, high))
                turned = [zero] + turned + [zero]
                for c in range(wide_cols):
                    at = (plane, pl.ds(row_base + row, rows_step + 8), pl.ds(col_base + LANES * c, LANES))
                    value = jnp.where(lane3 >= shift, turned[c + 1], turned[c])
                    grad[at] += value.reshape(rows_step + 8, LANES)

    @pl.loop(0, count)
    def _(number):
        row_at = lax.rem(offsets[number, 0], tile_rows)
        col_at = lax.rem(offsets[number, 1], tile_cols)

        @pl.when((col_at > LANES) == late)
        def _():
            visit(number, row_at, col_at)

    if late:
        own_half = (lax.axis_index("narrow") & 1) * (probe_sum.shape[0] // 2)
        other_half = probe_sum.shape[0] // 2 - own_half
        whole = slice(0, tile_cols)
        rim = slice(tile_cols, tile_cols + extent)
        pairs = [
            (probe_sum.at[pl.ds(pl.multiple_of(start, 8), probe_sum.shape[0] // 2), :], dst)
            for start, dst in ((other_half, probe_send), (own_half, probe_keep))
        ] + [
            (grad.at[:, low_rows, rim], grad_corner),
            (grad.at[:, low_rows, whole], grad_below),
            (grad.at[:, 0:extent, rim], grad_right),
            (grad.at[:, extent:tile_rows, rim], grad_right_low),
            (grad.at[:, 0:tile_rows, whole], grad_own),
        ]
    else:
        pairs = [(grad, grad_out), (probe_sum, probe_out)]
    stores = [pltpu.make_async_copy(src, dst, out_sems.at[n]) for n, (src, dst) in enumerate(pairs)]
    for store in stores:
        store.start()
    for store in stores:
        store.wait()


def run_slots(late, offsets, live, pieces, sums, probe, amps):
    extent = probe.shape[2]
    modes = probe.shape[0]
    tile_rows, tile_cols = pieces[0].shape[1:]
    mats = jnp.asarray(half_dft(extent))
    order = jnp.asarray(parity_order(extent)).astype(BF16)
    smem = pl.BlockSpec(memory_space=pltpu.SMEM)
    vmem = pl.BlockSpec(memory_space=pltpu.VMEM)
    hbm = pl.BlockSpec(memory_space=pl.ANY)
    grad_shape = (2, tile_rows + extent, tile_cols + extent)
    sum_shape = (modes * 2 * extent, extent)
    half_sum = (sum_shape[0] // 2, extent)
    if late:
        outs = [(2, tile_rows, tile_cols), (2, extent, tile_cols), (2, extent, extent), (2, tile_rows - extent, extent)]
        outs += [(2, extent, extent), half_sum, half_sum]
    else:
        outs = [grad_shape, sum_shape]
    return pl.pallas_call(
        functools.partial(slots_kernel, late, tile_rows, tile_cols),
        out_shape=[jax.ShapeDtypeStruct(shape, F32) for shape in outs],
        in_specs=[smem, smem] + [hbm] * (len(pieces) + len(sums)) + [vmem, hbm, vmem, vmem],
        out_specs=[hbm] * len(outs),
        scratch_shapes=[
            pltpu.VMEM(grad_shape, F32),
            pltpu.VMEM(grad_shape, F32),
            pltpu.VMEM(sum_shape, F32),
            pltpu.VMEM((2, extent, extent), F32),
            pltpu.VMEM((2, extent, extent), F32),
            pltpu.VMEM((extent, extent), F32),
            pltpu.VMEM((2, extent, extent // 2), F32),
            pltpu.VMEM((modes, 2, extent, extent), BF16),
            pltpu.VMEM((modes, 2, extent, extent), BF16),
            pltpu.VMEM((modes, 2, extent, extent), F32),
            pltpu.VMEM((2, extent, extent // 2), F32),
            pltpu.VMEM((modes, 2, extent, extent), BF16),
            pltpu.SemaphoreType.DMA((10,)),
            pltpu.SemaphoreType.DMA(()),
            pltpu.SemaphoreType.DMA((7,)),
        ],
        compiler_params=pltpu.CompilerParams(vmem_limit_bytes=40 * 1024 * 1024),
        name="late_slots" if late else "early_slots",
    )(offsets, live, *pieces, *sums, probe, amps, mats, order)


def split_kernel(extent, tile_rows, tile, *refs):
    outs, sems = refs[:-1], refs[-1]
    spans = []
    for cols in (slice(0, LANES), slice(LANES, extent)):
        spans += [(slice(0, extent), cols), (slice(extent, tile_rows), cols)]
    spans.append((slice(0, extent), slice(0, tile.shape[2])))
    copies = [
        pltpu.make_async_copy(tile.at[:, rows, cols], out, sems.at[n]) for n, ((rows, cols), out) in enumerate(zip(spans, outs))
    ]
    for copy in copies:
        copy.start()
    for copy in copies:
        copy.wait()


def split_tile(tile, extent):
    rows, cols = tile.shape[1:]
    shapes = [(2, extent, LANES), (2, rows - extent, LANES), (2, extent, extent - LANES), (2, rows - extent, extent - LANES)]
    shapes.append((2, extent, cols))
    hbm = pl.BlockSpec(memory_space=pl.ANY)
    return pl.pallas_call(
        functools.partial(split_kernel, extent, rows),
        out_shape=[jax.ShapeDtypeStruct(shape, F32) for shape in shapes],
        in_specs=[hbm],
        out_specs=[hbm] * len(shapes),
        scratch_shapes=[pltpu.SemaphoreType.DMA((len(shapes),))],
        name="split_tile",
    )(tile)


def shifted(value, axis, steps):
    count = lax.axis_size(axis)
    first, last = (max(0, -steps), min(count, count - steps))
    return lax.ppermute(value, axis, [(source, source + steps) for source in range(first, last)])


def place_in(bits):
    linear = lax.axis_index("wide") * lax.axis_size("narrow") + lax.axis_index("narrow")
    place = 0
    for n, bit in enumerate(bits):
        place = place + ((linear // bit) % 2) * (1 << n)
    return place


def partners(bits):
    return [sum(bit for n, bit in enumerate(bits) if step >> n & 1) for step in range(1 << len(bits))]


def swapped(value, mask):
    count = lax.axis_size("wide") * lax.axis_size("narrow")
    return lax.ppermute(value, ("wide", "narrow"), [(source, source ^ mask) for source in range(count)])


def add_kernel(bits, count, *refs):
    ins, outs = refs[:count], refs[count:]
    rows = outs[0].shape[0]
    place = place_in(bits)
    for step, out in enumerate(outs):
        at = pl.ds(pl.multiple_of((place ^ step) * rows, 8), rows)
        out[...] = sum(ref[at, :] for ref in ins)


def add_parts(parts, bits):
    count = 1 << len(bits)
    rows, cols = parts[0].shape
    vmem = pl.BlockSpec(memory_space=pltpu.VMEM)
    return pl.pallas_call(
        functools.partial(add_kernel, bits, len(parts)),
        out_shape=[jax.ShapeDtypeStruct((rows // count, cols), F32)] * count,
        in_specs=[vmem] * len(parts),
        out_specs=[vmem] * count,
        compiler_params=pltpu.CompilerParams(vmem_limit_bytes=8 * 1024 * 1024),
        name="add_parts",
    )(*parts)


def join_kernel(bits, scale, *refs):
    ins, out = refs[:-1], refs[-1]
    rows = ins[0].shape[0]
    place = place_in(bits)
    for step, ref in enumerate(ins):
        at = pl.ds(pl.multiple_of((place ^ step) * rows, 8), rows)
        out[at, :] = ref[...] if scale is None else ref[...] * scale


def join_parts(parts, bits, scale=None):
    rows, cols = parts[0].shape
    vmem = pl.BlockSpec(memory_space=pltpu.VMEM)
    return pl.pallas_call(
        functools.partial(join_kernel, bits, scale),
        out_shape=jax.ShapeDtypeStruct((rows * len(parts), cols), F32),
        in_specs=[vmem] * len(parts),
        out_specs=vmem,
        compiler_params=pltpu.CompilerParams(vmem_limit_bytes=8 * 1024 * 1024),
        name="join_parts",
    )(*parts)


def sum_everywhere(keep, send, scale):
    narrow, wide = lax.axis_size("narrow"), lax.axis_size("wide")
    bits = [1 << n for n in range((narrow * wide).bit_length() - 1)]
    groups = [tuple(bits[n : n + 2]) for n in range(1, len(bits), 2)]
    parts = [keep, swapped(send, bits[0])]
    for group in groups:
        pieces = add_parts(parts, group)
        parts = [pieces[0]] + [swapped(piece, mask) for piece, mask in zip(pieces[1:], partners(group)[1:])]
    value = add_parts(parts, ())[0]
    for group in reversed(groups):
        parts = [value] + [swapped(value, mask) for mask in partners(group)[1:]]
        if group != groups[0]:
            value = join_parts(parts, group)
    parts = parts + [swapped(part, bits[0]) for part in parts]
    return join_parts(parts, groups[0] + (bits[0],), scale)


def on_device(object_field, probe, amplitudes, offsets, live):
    extent = probe.shape[2]
    first_top, first_low, second_top, second_low, top = split_tile(object_field, extent)
    strips = [shifted(part, "wide", -1) for part in (first_top, first_low, second_top, second_low)]
    below = shifted(top, "narrow", -1)
    corner = shifted(strips[0], "narrow", -1)
    early = [object_field, below, strips[0], strips[1], corner]
    grad_so_far, probe_so_far = run_slots(False, offsets, live, early, [], probe, amplitudes)
    second, probe_so_far = lax.optimization_barrier((strips[2], probe_so_far))
    late = early + [second, strips[3], shifted(second, "narrow", -1)]
    grad_own, grad_below, grad_right, grad_right_low, grad_corner, keep, send = run_slots(
        True, offsets, live, late, [grad_so_far, probe_so_far], probe, amplitudes
    )
    came_corner = shifted(grad_corner, "narrow", 1)
    came_below = shifted(grad_below, "narrow", 1)
    came_right = shifted(grad_right + came_corner, "wide", 1)
    came_right_low = shifted(grad_right_low, "wide", 1)
    total_slots = lax.axis_size("wide") * lax.axis_size("narrow") * offsets.shape[0]
    probe_grad = sum_everywhere(keep, send, 1.0 / math.sqrt(total_slots)).reshape(probe.shape)
    rims = jnp.concatenate([came_right, came_right_low], 1)
    object_grad = grad_own.at[:, :extent, :].add(came_below).at[:, :, :extent].add(rims)
    return (object_grad, probe_grad)


def solution(mesh):
    return jax.shard_map(
        on_device,
        mesh=mesh,
        in_specs=(
            P(None, "narrow", "wide"),
            P(),
            P(("wide", "narrow"), None, None),
            P(("wide", "narrow"), None),
            P(("wide", "narrow")),
        ),
        out_specs=(P(None, "narrow", "wide"), P()),
        check_vma=False,
    )
```

```python
import functools
import math

import jax
import jax.numpy as jnp
import ml_dtypes
import numpy as np
from jax import lax
from jax.experimental import pallas as pl
from jax.experimental.pallas import tpu as pltpu
from jax.sharding import PartitionSpec as P

F32 = jnp.float32
BF16 = jnp.bfloat16
LANES = 128


def half_dft(extent):
    half = extent // 2
    blocks = []
    for parity in range(2):
        freq = 2 * np.arange(half)[:, None] + parity
        angles = (freq * np.arange(half)[None, :] % extent) * (2.0 * math.pi / extent)
        cosine = np.cos(angles) / math.sqrt(extent)
        sine = np.sin(angles) / math.sqrt(extent)
        blocks.append(np.block([[cosine, sine], [-sine, cosine]]))
    both = np.stack(blocks)
    return np.stack([both, np.swapaxes(both, 1, 2)]).astype(ml_dtypes.bfloat16)


def parity_order(extent):
    order = np.concatenate([np.arange(0, extent, 2), np.arange(1, extent, 2)])
    matrix = np.zeros((extent, extent), np.float32)
    matrix[order, np.arange(extent)] = 1.0
    return matrix


def dot(a, b):
    return jnp.dot(a, b, preferred_element_type=F32)


def slots_kernel(
    late, tile_rows, tile_cols, offsets, live, *refs,
):
    pieces = refs[: 8 if late else 5]
    refs = refs[len(pieces) :]
    if late:
        grad_so_far, probe_so_far, probe, amps, mats, order = refs[:6]
        grad_own, grad_below, grad_right, grad_right_low, grad_corner, probe_keep, probe_send = refs[6:13]
        refs = refs[13:]
    else:
        probe, amps, mats, order, grad_out, probe_out = refs[:6]
        refs = refs[6:]
    ext, grad, probe_sum, window, part, amp, sorted_amp, waves, inner, far, power, across, in_sems, amp_sem, out_sems = refs
    modes = probe.shape[0]
    extent = probe.shape[2]
    half = extent // 2
    rows_step = 32
    groups = rows_step // 8
    count = live[0]

    low_rows = slice(tile_rows, tile_rows + extent)
    first = slice(tile_cols, tile_cols + LANES)
    second = slice(tile_cols + LANES, tile_cols + extent)
    places = [(slice(0, tile_rows), slice(0, tile_cols)), (low_rows, slice(0, tile_cols))]
    for cols in (first, second):
        places += [(slice(0, extent), cols), (slice(extent, tile_rows), cols), (low_rows, cols)]
    loads = [
        pltpu.make_async_copy(src, ext.at[:, rows, cols], in_sems.at[n])
        for n, (src, (rows, cols)) in enumerate(zip(pieces, places))
    ]
    if late:
        loads.append(pltpu.make_async_copy(grad_so_far, grad, in_sems.at[len(pieces)]))
        loads.append(pltpu.make_async_copy(probe_so_far, probe_sum, in_sems.at[len(pieces) + 1]))
    for load in loads:
        load.start()
    if not late:
        grad[...] = jnp.zeros_like(grad)
        probe_sum[...] = jnp.zeros_like(probe_sum)
    for load in loads:
        load.wait()
    lane = lax.broadcasted_iota(jnp.int32, (rows_step, LANES), 1)
    lane3 = lax.broadcasted_iota(jnp.int32, (groups + 1, 8, LANES), 2)
    sublane = lax.broadcasted_iota(jnp.int32, (groups, 8, LANES), 1)
    sublane_tall = lax.broadcasted_iota(jnp.int32, (groups + 1, 8, LANES), 1)

    def rows_of(k, c, rows):
        start = (k * 2 + c) * extent
        return slice(start + rows.start, start + rows.stop)

    def visit(number, row_at, col_at):
        amp_load = pltpu.make_async_copy(amps.at[number], amp, amp_sem)
        amp_load.start()
        shift = lax.rem(col_at, LANES)
        col_base = pl.multiple_of(col_at - shift, LANES)
        back = lax.rem(LANES - shift, LANES)
        wide_cols = extent // LANES + 1
        row_shift = lax.rem(row_at, 8)
        row_base = pl.multiple_of(row_at - row_shift, 8)
        row_back = lax.rem(8 - row_shift, 8)

        for plane in range(2):
            for row in range(0, extent, rows_step):
                turned = []
                for c in range(wide_cols):
                    tall = ext[plane, pl.ds(row_base + row, rows_step + 8), pl.ds(col_base + LANES * c, LANES)]
                    tall = pltpu.roll(tall.reshape(groups + 1, 8, LANES), row_back, 1)
                    flat = jnp.where(sublane < 8 - row_shift, tall[:-1], tall[1:]).reshape(rows_step, LANES)
                    turned.append(pltpu.roll(flat, back, 1))
                for c in range(wide_cols - 1):
                    window[plane, row : row + rows_step, c * LANES : (c + 1) * LANES] = jnp.where(
                        lane < LANES - shift, turned[c], turned[c + 1]
                    )


        def psi(k, step=rows_step):
            for row in range(0, half, step):
                waves_at = []
                for base in (row, half + row):
                    rows = slice(base, base + step)
                    pr, pi = probe[k, 0, rows, :], probe[k, 1, rows, :]
                    o_re, o_im = window[0, rows, :], window[1, rows, :]
                    waves_at.append((pr * o_re - pi * o_im, pr * o_im + pi * o_re))
                for c in range(2):
                    rows = slice(c * half + row, c * half + row + step)
                    waves[k, 0, rows, :] = (waves_at[0][c] + waves_at[1][c]).astype(BF16)
                    waves[k, 1, rows, :] = (waves_at[0][c] - waves_at[1][c]).astype(BF16)

        def left(k):
            for a in range(2):
                z = dot(mats[0, a], waves[k, a])
                left, right_half = z[:, :half], z[:, half:]
                for b, value in enumerate((left + right_half, left - right_half)):
                    value = value.astype(BF16)
                    inner[k, b, a * half : (a + 1) * half, :half] = value[:half]
                    inner[k, b, a * half : (a + 1) * half, half:] = value[half:]

        def right(k):
            for b in range(2):
                f = dot(inner[k, b], mats[1, b])
                far[k, b] = f
                own_power = f[:, :half] * f[:, :half] + f[:, half:] * f[:, half:]
                power[b] = own_power if k == 0 else power[b] + own_power

        def factors():
            amp_load.wait()
            high = amp[...].astype(BF16)
            low = (amp[...] - high.astype(F32)).astype(BF16)
            turned = dot(high, order[...]) + dot(low, order[...])
            for b in range(2):
                sorted_amp[b] = turned[:, b * half : (b + 1) * half]
            for b in range(2):
                for a in range(2):
                    rows = slice(a * half, (a + 1) * half)
                    for_rows = sorted_amp[b, pl.ds(a, half, 2), :]
                    power[b, rows] = 2.0 - 2.0 * for_rows * lax.rsqrt(power[b, rows] + 0.5)

        def back_right(k):
            ys = []
            for b in range(2):
                factor = power[b]
                g = jnp.concatenate([far[k, b, :, :half] * factor, far[k, b, :, half:] * factor], 1)
                ys.append(dot(g.astype(BF16), mats[0, b]))
            for side, y in enumerate((ys[0] + ys[1], ys[0] - ys[1])):
                y = y.astype(BF16)
                cols = slice(side * half, (side + 1) * half)
                for a in range(2):
                    rows = slice(a * half, (a + 1) * half)
                    across[k, a, :half, cols] = y[rows, :half]
                    across[k, a, half:, cols] = y[rows, half:]

        def back_left(k):
            v0 = dot(mats[1, 0], across[k, 0])
            v1 = dot(mats[1, 1], across[k, 1])
            for side, v in enumerate((v0 + v1, v0 - v1)):
                rows = slice(side * half, (side + 1) * half)
                g_re, g_im = v[:half], v[half:]
                pr, pi = probe[k, 0, rows, :], probe[k, 1, rows, :]
                o_re, o_im = window[0, rows, :], window[1, rows, :]
                add_re = pr * g_re + pi * g_im
                add_im = pr * g_im - pi * g_re
                part[0, rows, :] = add_re if k == 0 else part[0, rows, :] + add_re
                part[1, rows, :] = add_im if k == 0 else part[1, rows, :] + add_im
                probe_sum[rows_of(k, 0, rows), :] += o_re * g_re + o_im * g_im
                probe_sum[rows_of(k, 1, rows), :] += o_re * g_im - o_im * g_re

        for stage in (psi, left, right):
            for k in range(modes):
                stage(k)
        factors()
        for stage in (back_right, back_left):
            for k in range(modes):
                stage(k)

        zero = jnp.zeros((groups + 1, 8, LANES), F32)
        edge = jnp.zeros((1, 8, LANES), F32)
        for plane in range(2):
            for row in range(0, extent, rows_step):
                turned = []
                for c in range(wide_cols - 1):
                    flat = part[plane, row : row + rows_step, c * LANES : (c + 1) * LANES]
                    flat = pltpu.roll(flat, shift, 1).reshape(groups, 8, LANES)
                    flat = pltpu.roll(flat, row_shift, 1)
                    low = jnp.concatenate([flat, edge], 0)
                    high = jnp.concatenate([edge, flat], 0)
                    turned.append(jnp.where(sublane_tall >= row_shift, low, high))
                turned = [zero] + turned + [zero]
                for c in range(wide_cols):
                    at = (plane, pl.ds(row_base + row, rows_step + 8), pl.ds(col_base + LANES * c, LANES))
                    value = jnp.where(lane3 >= shift, turned[c + 1], turned[c])
                    grad[at] += value.reshape(rows_step + 8, LANES)

    @pl.loop(0, count)
    def _(number):
        row_at = lax.rem(offsets[number, 0], tile_rows)
        col_at = lax.rem(offsets[number, 1], tile_cols)

        @pl.when((col_at > LANES) == late)
        def _():
            visit(number, row_at, col_at)

    if late:
        own_half = (lax.axis_index("narrow") & 1) * (probe_sum.shape[0] // 2)
        other_half = probe_sum.shape[0] // 2 - own_half
        whole = slice(0, tile_cols)
        rim = slice(tile_cols, tile_cols + extent)
        pairs = [
            (probe_sum.at[pl.ds(pl.multiple_of(start, 8), probe_sum.shape[0] // 2), :], dst)
            for start, dst in ((other_half, probe_send), (own_half, probe_keep))
        ] + [
            (grad.at[:, low_rows, rim], grad_corner),
            (grad.at[:, low_rows, whole], grad_below),
            (grad.at[:, 0:extent, rim], grad_right),
            (grad.at[:, extent:tile_rows, rim], grad_right_low),
            (grad.at[:, 0:tile_rows, whole], grad_own),
        ]
    else:
        pairs = [(grad, grad_out), (probe_sum, probe_out)]
    stores = [pltpu.make_async_copy(src, dst, out_sems.at[n]) for n, (src, dst) in enumerate(pairs)]
    for store in stores:
        store.start()
    for store in stores:
        store.wait()


def run_slots(late, offsets, live, pieces, sums, probe, amps):
    extent = probe.shape[2]
    modes = probe.shape[0]
    tile_rows, tile_cols = pieces[0].shape[1:]
    mats = jnp.asarray(half_dft(extent))
    order = jnp.asarray(parity_order(extent)).astype(BF16)
    smem = pl.BlockSpec(memory_space=pltpu.SMEM)
    vmem = pl.BlockSpec(memory_space=pltpu.VMEM)
    hbm = pl.BlockSpec(memory_space=pl.ANY)
    grad_shape = (2, tile_rows + extent, tile_cols + extent)
    sum_shape = (modes * 2 * extent, extent)
    half_sum = (sum_shape[0] // 2, extent)
    if late:
        outs = [(2, tile_rows, tile_cols), (2, extent, tile_cols), (2, extent, extent), (2, tile_rows - extent, extent)]
        outs += [(2, extent, extent), half_sum, half_sum]
    else:
        outs = [grad_shape, sum_shape]
    return pl.pallas_call(
        functools.partial(slots_kernel, late, tile_rows, tile_cols),
        out_shape=[jax.ShapeDtypeStruct(shape, F32) for shape in outs],
        in_specs=[smem, smem] + [hbm] * (len(pieces) + len(sums)) + [vmem, hbm, vmem, vmem],
        out_specs=[hbm] * len(outs),
        scratch_shapes=[
            pltpu.VMEM(grad_shape, F32),
            pltpu.VMEM(grad_shape, F32),
            pltpu.VMEM(sum_shape, F32),
            pltpu.VMEM((2, extent, extent), F32),
            pltpu.VMEM((2, extent, extent), F32),
            pltpu.VMEM((extent, extent), F32),
            pltpu.VMEM((2, extent, extent // 2), F32),
            pltpu.VMEM((modes, 2, extent, extent), BF16),
            pltpu.VMEM((modes, 2, extent, extent), BF16),
            pltpu.VMEM((modes, 2, extent, extent), F32),
            pltpu.VMEM((2, extent, extent // 2), F32),
            pltpu.VMEM((modes, 2, extent, extent), BF16),
            pltpu.SemaphoreType.DMA((10,)),
            pltpu.SemaphoreType.DMA(()),
            pltpu.SemaphoreType.DMA((7,)),
        ],
        compiler_params=pltpu.CompilerParams(vmem_limit_bytes=60 * 1024 * 1024),
        name="late_slots" if late else "early_slots",
    )(offsets, live, *pieces, *sums, probe, amps, mats, order)


def split_kernel(tile, *outs):
    strips, top = outs[:-1], outs[-1]
    extent = top.shape[1]
    rows = tile.shape[1]
    for n, out in enumerate(strips):
        at = slice(0, extent) if n % 2 == 0 else slice(extent, rows)
        first = n // 2 * LANES
        out[...] = tile[:, at, first : first + out.shape[2]]
    top[...] = tile[:, :extent, :]


def split_tile(tile, extent):
    rows, cols = tile.shape[1:]
    shapes = [(2, extent, LANES), (2, rows - extent, LANES), (2, extent, extent - LANES), (2, rows - extent, extent - LANES)]
    shapes.append((2, extent, cols))
    vmem = pl.BlockSpec(memory_space=pltpu.VMEM)
    return pl.pallas_call(
        split_kernel,
        out_shape=[jax.ShapeDtypeStruct(shape, F32) for shape in shapes],
        in_specs=[vmem],
        out_specs=[vmem] * len(shapes),
        compiler_params=pltpu.CompilerParams(vmem_limit_bytes=8 * 1024 * 1024),
        name="split_tile",
    )(tile)


def shifted(value, axis, steps):
    count = lax.axis_size(axis)
    first, last = (max(0, -steps), min(count, count - steps))
    return lax.ppermute(value, axis, [(source, source + steps) for source in range(first, last)])


def place_in(bits):
    linear = lax.axis_index("wide") * lax.axis_size("narrow") + lax.axis_index("narrow")
    place = 0
    for n, bit in enumerate(bits):
        place = place + ((linear // bit) % 2) * (1 << n)
    return place


def partners(bits):
    return [sum(bit for n, bit in enumerate(bits) if step >> n & 1) for step in range(1 << len(bits))]


def swapped(value, mask):
    count = lax.axis_size("wide") * lax.axis_size("narrow")
    return lax.ppermute(value, ("wide", "narrow"), [(source, source ^ mask) for source in range(count)])


def add_kernel(bits, count, *refs):
    ins, outs = refs[:count], refs[count:]
    rows = outs[0].shape[0]
    place = place_in(bits)
    for step, out in enumerate(outs):
        at = pl.ds(pl.multiple_of((place ^ step) * rows, 8), rows)
        out[...] = sum(ref[at, :] for ref in ins)


def add_parts(parts, bits):
    count = 1 << len(bits)
    rows, cols = parts[0].shape
    vmem = pl.BlockSpec(memory_space=pltpu.VMEM)
    return pl.pallas_call(
        functools.partial(add_kernel, bits, len(parts)),
        out_shape=[jax.ShapeDtypeStruct((rows // count, cols), F32)] * count,
        in_specs=[vmem] * len(parts),
        out_specs=[vmem] * count,
        compiler_params=pltpu.CompilerParams(vmem_limit_bytes=8 * 1024 * 1024),
        name="add_parts",
    )(*parts)


def join_kernel(bits, scale, *refs):
    ins, out = refs[:-1], refs[-1]
    rows = ins[0].shape[0]
    place = place_in(bits)
    for step, ref in enumerate(ins):
        at = pl.ds(pl.multiple_of((place ^ step) * rows, 8), rows)
        out[at, :] = ref[...] if scale is None else ref[...] * scale


def join_parts(parts, bits, scale=None):
    rows, cols = parts[0].shape
    vmem = pl.BlockSpec(memory_space=pltpu.VMEM)
    return pl.pallas_call(
        functools.partial(join_kernel, bits, scale),
        out_shape=jax.ShapeDtypeStruct((rows * len(parts), cols), F32),
        in_specs=[vmem] * len(parts),
        out_specs=vmem,
        compiler_params=pltpu.CompilerParams(vmem_limit_bytes=8 * 1024 * 1024),
        name="join_parts",
    )(*parts)


def sum_everywhere(keep, send, scale, beside):
    narrow, wide = lax.axis_size("narrow"), lax.axis_size("wide")
    bits = [1 << n for n in range((narrow * wide).bit_length() - 1)]
    groups = [tuple(bits[n : n + 2]) for n in range(1, len(bits), 2)]
    parts = [keep, swapped(send, bits[0])]
    for group in groups:
        pieces = add_parts(parts, group)
        parts = [pieces[0]] + [swapped(piece, mask) for piece, mask in zip(pieces[1:], partners(group)[1:])]
        if group == groups[0]:
            parts, beside = lax.optimization_barrier((parts, beside))
    value = add_parts(parts, ())[0]
    for group in reversed(groups):
        parts = [value] + [swapped(value, mask) for mask in partners(group)[1:]]
        if group != groups[0]:
            value = join_parts(parts, group)
    parts = parts + [swapped(part, bits[0]) for part in parts]
    return join_parts(parts, groups[0] + (bits[0],), scale), beside


def on_device(object_field, probe, amplitudes, offsets, live):
    extent = probe.shape[2]
    first_top, first_low, second_top, second_low, top = split_tile(object_field, extent)
    strips = [shifted(part, "wide", -1) for part in (first_top, first_low, second_top, second_low)]
    below = shifted(top, "narrow", -1)
    corner = shifted(strips[0], "narrow", -1)
    early = [object_field, below, strips[0], strips[1], corner]
    grad_so_far, probe_so_far = run_slots(False, offsets, live, early, [], probe, amplitudes)
    second, probe_so_far = lax.optimization_barrier((strips[2], probe_so_far))
    late = early + [second, strips[3], shifted(second, "narrow", -1)]
    grad_own, grad_below, grad_right, grad_right_low, grad_corner, keep, send = run_slots(
        True, offsets, live, late, [grad_so_far, probe_so_far], probe, amplitudes
    )
    grad_right, keep, send = lax.optimization_barrier((grad_right + shifted(grad_corner, "narrow", 1), keep, send))
    beside = [shifted(grad_below, "narrow", 1), shifted(grad_right, "wide", 1), shifted(grad_right_low, "wide", 1)]
    total_slots = lax.axis_size("wide") * lax.axis_size("narrow") * offsets.shape[0]
    probe_grad, beside = sum_everywhere(keep, send, 1.0 / math.sqrt(total_slots), beside)
    came_below, came_right, came_right_low = beside
    rims = jnp.concatenate([came_right, came_right_low], 1)
    object_grad = grad_own.at[:, :extent, :].add(came_below).at[:, :, :extent].add(rims)
    return (object_grad, probe_grad.reshape(probe.shape))


def solution(mesh):
    return jax.shard_map(
        on_device,
        mesh=mesh,
        in_specs=(
            P(None, "narrow", "wide"),
            P(),
            P(("wide", "narrow"), None, None),
            P(("wide", "narrow"), None),
            P(("wide", "narrow")),
        ),
        out_specs=(P(None, "narrow", "wide"), P()),
        check_vma=False,
    )
```

```python
import functools
import math

import jax
import jax.numpy as jnp
import ml_dtypes
import numpy as np
from jax import lax
from jax.experimental import pallas as pl
from jax.experimental.pallas import tpu as pltpu
from jax.sharding import PartitionSpec as P

F32 = jnp.float32
BF16 = jnp.bfloat16
LANES = 128


def half_dft(extent):
    half = extent // 2
    blocks = []
    for parity in range(2):
        freq = 2 * np.arange(half)[:, None] + parity
        angles = (freq * np.arange(half)[None, :] % extent) * (2.0 * math.pi / extent)
        cosine = np.cos(angles) / math.sqrt(extent)
        sine = np.sin(angles) / math.sqrt(extent)
        blocks.append(np.block([[cosine, sine], [-sine, cosine]]))
    both = np.stack(blocks)
    return np.stack([both, np.swapaxes(both, 1, 2)]).astype(ml_dtypes.bfloat16)


def parity_order(extent):
    order = np.concatenate([np.arange(0, extent, 2), np.arange(1, extent, 2)])
    matrix = np.zeros((extent, extent), np.float32)
    matrix[order, np.arange(extent)] = 1.0
    return matrix


def dot(a, b):
    return jnp.dot(a, b, preferred_element_type=F32)


def slots_kernel(
    tile_rows, tile_cols, offsets, live, own, below, right, right_low, corner, probe_in, amps, mats, order,
    grad_own, grad_below, grad_right, grad_right_low, grad_corner, probe_keep, probe_send,
    ext, grad, probe, probe_sum, window, part, amp, sorted_amp, waves, inner, far, power, across,
    in_sems, amp_sem, out_sems,
):
    modes = probe.shape[0]
    extent = probe.shape[2]
    half = extent // 2
    rows_step = 32
    groups = rows_step // 8
    count = live[0]

    low_rows = slice(tile_rows, tile_rows + extent)
    whole = slice(0, tile_cols)
    rim = slice(tile_cols, tile_cols + extent)
    places = [
        (own, slice(0, tile_rows), whole),
        (below, low_rows, whole),
        (right, slice(0, extent), rim),
        (right_low, slice(extent, tile_rows), rim),
        (corner, low_rows, rim),
    ]
    loads = [
        pltpu.make_async_copy(src, ext.at[:, rows, cols], in_sems.at[n])
        for n, (src, rows, cols) in enumerate(places)
    ]
    loads.append(pltpu.make_async_copy(probe_in, probe, in_sems.at[len(places)]))
    for load in loads:
        load.start()
    grad[...] = jnp.zeros_like(grad)
    probe_sum[...] = jnp.zeros_like(probe_sum)
    for load in loads:
        load.wait()
    lane = lax.broadcasted_iota(jnp.int32, (rows_step, LANES), 1)
    lane3 = lax.broadcasted_iota(jnp.int32, (groups + 1, 8, LANES), 2)
    sublane = lax.broadcasted_iota(jnp.int32, (groups, 8, LANES), 1)
    sublane_tall = lax.broadcasted_iota(jnp.int32, (groups + 1, 8, LANES), 1)

    def rows_of(k, c, rows):
        start = (k * 2 + c) * extent
        return slice(start + rows.start, start + rows.stop)

    def visit(number, row_at, col_at):
        amp_load = pltpu.make_async_copy(amps.at[number], amp, amp_sem)
        amp_load.start()
        shift = lax.rem(col_at, LANES)
        col_base = pl.multiple_of(col_at - shift, LANES)
        back = lax.rem(LANES - shift, LANES)
        wide_cols = extent // LANES + 1
        row_shift = lax.rem(row_at, 8)
        row_base = pl.multiple_of(row_at - row_shift, 8)
        row_back = lax.rem(8 - row_shift, 8)

        for plane in range(2):
            for row in range(0, extent, rows_step):
                turned = []
                for c in range(wide_cols):
                    tall = ext[plane, pl.ds(row_base + row, rows_step + 8), pl.ds(col_base + LANES * c, LANES)]
                    tall = pltpu.roll(tall.reshape(groups + 1, 8, LANES), row_back, 1)
                    flat = jnp.where(sublane < 8 - row_shift, tall[:-1], tall[1:]).reshape(rows_step, LANES)
                    turned.append(pltpu.roll(flat, back, 1))
                for c in range(wide_cols - 1):
                    window[plane, row : row + rows_step, c * LANES : (c + 1) * LANES] = jnp.where(
                        lane < LANES - shift, turned[c], turned[c + 1]
                    )


        def psi(k, step=rows_step):
            for row in range(0, half, step):
                waves_at = []
                for base in (row, half + row):
                    rows = slice(base, base + step)
                    pr, pi = probe[k, 0, rows, :], probe[k, 1, rows, :]
                    o_re, o_im = window[0, rows, :], window[1, rows, :]
                    waves_at.append((pr * o_re - pi * o_im, pr * o_im + pi * o_re))
                for c in range(2):
                    rows = slice(c * half + row, c * half + row + step)
                    waves[k, 0, rows, :] = (waves_at[0][c] + waves_at[1][c]).astype(BF16)
                    waves[k, 1, rows, :] = (waves_at[0][c] - waves_at[1][c]).astype(BF16)

        def left(k):
            for a in range(2):
                z = dot(mats[0, a], waves[k, a])
                left, right_half = z[:, :half], z[:, half:]
                for b, value in enumerate((left + right_half, left - right_half)):
                    value = value.astype(BF16)
                    inner[k, b, a * half : (a + 1) * half, :half] = value[:half]
                    inner[k, b, a * half : (a + 1) * half, half:] = value[half:]

        def right(k):
            for b in range(2):
                f = dot(inner[k, b], mats[1, b])
                far[k, b] = f
                own_power = f[:, :half] * f[:, :half] + f[:, half:] * f[:, half:]
                power[b] = own_power if k == 0 else power[b] + own_power

        def factors():
            amp_load.wait()
            high = amp[...].astype(BF16)
            low = (amp[...] - high.astype(F32)).astype(BF16)
            turned = dot(high, order[...]) + dot(low, order[...])
            for b in range(2):
                sorted_amp[b] = turned[:, b * half : (b + 1) * half]
            for b in range(2):
                for a in range(2):
                    rows = slice(a * half, (a + 1) * half)
                    for_rows = sorted_amp[b, pl.ds(a, half, 2), :]
                    power[b, rows] = 2.0 - 2.0 * for_rows * lax.rsqrt(power[b, rows] + 0.5)

        def back_right(k):
            ys = []
            for b in range(2):
                factor = power[b]
                g = jnp.concatenate([far[k, b, :, :half] * factor, far[k, b, :, half:] * factor], 1)
                ys.append(dot(g.astype(BF16), mats[0, b]))
            for side, y in enumerate((ys[0] + ys[1], ys[0] - ys[1])):
                y = y.astype(BF16)
                cols = slice(side * half, (side + 1) * half)
                for a in range(2):
                    rows = slice(a * half, (a + 1) * half)
                    across[k, a, :half, cols] = y[rows, :half]
                    across[k, a, half:, cols] = y[rows, half:]

        def back_left(k):
            v0 = dot(mats[1, 0], across[k, 0])
            v1 = dot(mats[1, 1], across[k, 1])
            for side, v in enumerate((v0 + v1, v0 - v1)):
                rows = slice(side * half, (side + 1) * half)
                g_re, g_im = v[:half], v[half:]
                pr, pi = probe[k, 0, rows, :], probe[k, 1, rows, :]
                o_re, o_im = window[0, rows, :], window[1, rows, :]
                add_re = pr * g_re + pi * g_im
                add_im = pr * g_im - pi * g_re
                part[0, rows, :] = add_re if k == 0 else part[0, rows, :] + add_re
                part[1, rows, :] = add_im if k == 0 else part[1, rows, :] + add_im
                probe_sum[rows_of(k, 0, rows), :] += o_re * g_re + o_im * g_im
                probe_sum[rows_of(k, 1, rows), :] += o_re * g_im - o_im * g_re

        for stage in (psi, left, right):
            for k in range(modes):
                stage(k)
        factors()
        for stage in (back_right, back_left):
            for k in range(modes):
                stage(k)

        zero = jnp.zeros((groups + 1, 8, LANES), F32)
        edge = jnp.zeros((1, 8, LANES), F32)
        for plane in range(2):
            for row in range(0, extent, rows_step):
                turned = []
                for c in range(wide_cols - 1):
                    flat = part[plane, row : row + rows_step, c * LANES : (c + 1) * LANES]
                    flat = pltpu.roll(flat, shift, 1).reshape(groups, 8, LANES)
                    flat = pltpu.roll(flat, row_shift, 1)
                    low = jnp.concatenate([flat, edge], 0)
                    high = jnp.concatenate([edge, flat], 0)
                    turned.append(jnp.where(sublane_tall >= row_shift, low, high))
                turned = [zero] + turned + [zero]
                for c in range(wide_cols):
                    at = (plane, pl.ds(row_base + row, rows_step + 8), pl.ds(col_base + LANES * c, LANES))
                    value = jnp.where(lane3 >= shift, turned[c + 1], turned[c])
                    grad[at] += value.reshape(rows_step + 8, LANES)

    @pl.loop(0, count)
    def _(number):
        row_at = lax.rem(offsets[number, 0], tile_rows)
        col_at = lax.rem(offsets[number, 1], tile_cols)

        visit(number, row_at, col_at)

    own_half = (lax.axis_index("narrow") & 1) * (probe_sum.shape[0] // 2)
    other_half = probe_sum.shape[0] // 2 - own_half
    pairs = [
        (probe_sum.at[pl.ds(pl.multiple_of(start, 8), probe_sum.shape[0] // 2), :], dst)
        for start, dst in ((other_half, probe_send), (own_half, probe_keep))
    ] + [
        (grad.at[:, low_rows, rim], grad_corner),
        (grad.at[:, low_rows, whole], grad_below),
        (grad.at[:, 0:extent, rim], grad_right),
        (grad.at[:, extent:tile_rows, rim], grad_right_low),
        (grad.at[:, 0:tile_rows, whole], grad_own),
    ]
    stores = [pltpu.make_async_copy(src, dst, out_sems.at[n]) for n, (src, dst) in enumerate(pairs)]
    for store in stores:
        store.start()
    for store in stores:
        store.wait()


def run_slots(offsets, live, own, below, right, right_low, corner, probe, amps):
    extent = probe.shape[2]
    modes = probe.shape[0]
    tile_rows, tile_cols = own.shape[1:]
    mats = jnp.asarray(half_dft(extent))
    order = jnp.asarray(parity_order(extent)).astype(BF16)
    smem = pl.BlockSpec(memory_space=pltpu.SMEM)
    vmem = pl.BlockSpec(memory_space=pltpu.VMEM)
    hbm = pl.BlockSpec(memory_space=pl.ANY)
    grad_shape = (2, tile_rows + extent, tile_cols + extent)
    sum_shape = (modes * 2 * extent, extent)
    half_sum = (sum_shape[0] // 2, extent)
    outs = [(2, tile_rows, tile_cols), (2, extent, tile_cols), (2, extent, extent), (2, tile_rows - extent, extent)]
    outs += [(2, extent, extent), half_sum, half_sum]
    return pl.pallas_call(
        functools.partial(slots_kernel, tile_rows, tile_cols),
        out_shape=[jax.ShapeDtypeStruct(shape, F32) for shape in outs],
        in_specs=[smem, smem] + [hbm] * 7 + [vmem, vmem],
        out_specs=[hbm] * len(outs),
        scratch_shapes=[
            pltpu.VMEM(grad_shape, F32),
            pltpu.VMEM(grad_shape, F32),
            pltpu.VMEM(probe.shape, F32),
            pltpu.VMEM(sum_shape, F32),
            pltpu.VMEM((2, extent, extent), F32),
            pltpu.VMEM((2, extent, extent), F32),
            pltpu.VMEM((extent, extent), F32),
            pltpu.VMEM((2, extent, extent // 2), F32),
            pltpu.VMEM((modes, 2, extent, extent), BF16),
            pltpu.VMEM((modes, 2, extent, extent), BF16),
            pltpu.VMEM((modes, 2, extent, extent), F32),
            pltpu.VMEM((2, extent, extent // 2), F32),
            pltpu.VMEM((modes, 2, extent, extent), BF16),
            pltpu.SemaphoreType.DMA((6,)),
            pltpu.SemaphoreType.DMA(()),
            pltpu.SemaphoreType.DMA((7,)),
        ],
        compiler_params=pltpu.CompilerParams(vmem_limit_bytes=60 * 1024 * 1024),
        name="slots",
    )(offsets, live, own, below, right, right_low, corner, probe, amps, mats, order)


def shifted(value, axis, steps):
    count = lax.axis_size(axis)
    first, last = (max(0, -steps), min(count, count - steps))
    return lax.ppermute(value, axis, [(source, source + steps) for source in range(first, last)])


def place_in(bits):
    linear = lax.axis_index("wide") * lax.axis_size("narrow") + lax.axis_index("narrow")
    place = 0
    for n, bit in enumerate(bits):
        place = place + ((linear // bit) % 2) * (1 << n)
    return place


def partners(bits):
    return [sum(bit for n, bit in enumerate(bits) if step >> n & 1) for step in range(1 << len(bits))]


def swapped(value, mask):
    count = lax.axis_size("wide") * lax.axis_size("narrow")
    return lax.ppermute(value, ("wide", "narrow"), [(source, source ^ mask) for source in range(count)])


def add_kernel(bits, count, *refs):
    ins, outs = refs[:count], refs[count:]
    rows = outs[0].shape[0]
    place = place_in(bits)
    for step, out in enumerate(outs):
        at = pl.ds(pl.multiple_of((place ^ step) * rows, 8), rows)
        out[...] = sum(ref[at, :] for ref in ins)


def add_parts(parts, bits):
    count = 1 << len(bits)
    rows, cols = parts[0].shape
    vmem = pl.BlockSpec(memory_space=pltpu.VMEM)
    return pl.pallas_call(
        functools.partial(add_kernel, bits, len(parts)),
        out_shape=[jax.ShapeDtypeStruct((rows // count, cols), F32)] * count,
        in_specs=[vmem] * len(parts),
        out_specs=[vmem] * count,
        compiler_params=pltpu.CompilerParams(vmem_limit_bytes=8 * 1024 * 1024),
        name="add_parts",
    )(*parts)


def join_kernel(bits, scale, *refs):
    ins, out = refs[:-1], refs[-1]
    rows = ins[0].shape[0]
    place = place_in(bits)
    for step, ref in enumerate(ins):
        at = pl.ds(pl.multiple_of((place ^ step) * rows, 8), rows)
        out[at, :] = ref[...] if scale is None else ref[...] * scale


def join_parts(parts, bits, scale=None):
    rows, cols = parts[0].shape
    vmem = pl.BlockSpec(memory_space=pltpu.VMEM)
    return pl.pallas_call(
        functools.partial(join_kernel, bits, scale),
        out_shape=jax.ShapeDtypeStruct((rows * len(parts), cols), F32),
        in_specs=[vmem] * len(parts),
        out_specs=vmem,
        compiler_params=pltpu.CompilerParams(vmem_limit_bytes=8 * 1024 * 1024),
        name="join_parts",
    )(*parts)


def sum_everywhere(keep, send, scale, beside):
    narrow, wide = lax.axis_size("narrow"), lax.axis_size("wide")
    bits = [1 << n for n in range((narrow * wide).bit_length() - 1)]
    groups = [tuple(bits[n : n + 2]) for n in range(1, len(bits), 2)]
    parts = [keep, swapped(send, bits[0])]
    for group in groups:
        pieces = add_parts(parts, group)
        parts = [pieces[0]] + [swapped(piece, mask) for piece, mask in zip(pieces[1:], partners(group)[1:])]
        if group == groups[0]:
            parts, beside = lax.optimization_barrier((parts, beside))
    value = add_parts(parts, ())[0]
    for group in reversed(groups):
        parts = [value] + [swapped(value, mask) for mask in partners(group)[1:]]
        if group != groups[0]:
            value = join_parts(parts, group)
    parts = parts + [swapped(part, bits[0]) for part in parts]
    return join_parts(parts, groups[0] + (bits[0],), scale), beside


def on_device(object_field, probe, amplitudes, offsets, live):
    extent = probe.shape[2]
    top = object_field[:, :extent]
    right = shifted(top, "wide", -1)
    below = shifted(top, "narrow", -1)
    right_low = shifted(object_field[:, extent:], "wide", -1)
    corner = shifted(right, "narrow", -1)
    grad_own, grad_below, grad_right, grad_right_low, grad_corner, keep, send = run_slots(
        offsets, live, object_field, below, right, right_low, corner, probe, amplitudes
    )
    grad_right, keep, send = lax.optimization_barrier((grad_right + shifted(grad_corner, "narrow", 1), keep, send))
    beside = [shifted(grad_below, "narrow", 1), shifted(grad_right, "wide", 1), shifted(grad_right_low, "wide", 1)]
    total_slots = lax.axis_size("wide") * lax.axis_size("narrow") * offsets.shape[0]
    probe_grad, beside = sum_everywhere(keep, send, 1.0 / math.sqrt(total_slots), beside)
    came_below, came_right, came_right_low = beside
    rims = jnp.concatenate([came_right, came_right_low], 1)
    object_grad = grad_own.at[:, :extent, :].add(came_below).at[:, :, :extent].add(rims)
    return (object_grad, probe_grad.reshape(probe.shape))


def solution(mesh):
    return jax.shard_map(
        on_device,
        mesh=mesh,
        in_specs=(
            P(None, "narrow", "wide"),
            P(),
            P(("wide", "narrow"), None, None),
            P(("wide", "narrow"), None),
            P(("wide", "narrow")),
        ),
        out_specs=(P(None, "narrow", "wide"), P()),
        check_vma=False,
    )
```

```python
import functools
import math

import jax
import jax.numpy as jnp
import ml_dtypes
import numpy as np
from jax import lax
from jax.experimental import pallas as pl
from jax.experimental.pallas import tpu as pltpu
from jax.sharding import PartitionSpec as P

F32 = jnp.float32
BF16 = jnp.bfloat16
LANES = 128


def half_dft(extent):
    half = extent // 2
    blocks = []
    for parity in range(2):
        freq = 2 * np.arange(half)[:, None] + parity
        angles = (freq * np.arange(half)[None, :] % extent) * (2.0 * math.pi / extent)
        cosine = np.cos(angles) / math.sqrt(extent)
        sine = np.sin(angles) / math.sqrt(extent)
        blocks.append(np.block([[cosine, sine], [-sine, cosine]]))
    both = np.stack(blocks)
    return np.stack([both, np.swapaxes(both, 1, 2)]).astype(ml_dtypes.bfloat16)


def parity_order(extent):
    order = np.concatenate([np.arange(0, extent, 2), np.arange(1, extent, 2)])
    matrix = np.zeros((extent, extent), np.float32)
    matrix[order, np.arange(extent)] = 1.0
    return matrix


def dot(a, b):
    return jnp.dot(a, b, preferred_element_type=F32)


def slots_kernel(
    tile_rows, tile_cols, offsets, live, own, below, right, right_low, corner, probe_in, amps, mats, order,
    grad_own, grad_below, grad_right, grad_right_low, grad_corner, probe_keep, probe_send,
    ext, grad, probe, probe_sum, window, part, amp, sorted_amp, waves, inner, far, power, across,
    in_sems, amp_sem, out_sems,
):
    modes = probe.shape[0]
    extent = probe.shape[2]
    half = extent // 2
    rows_step = 32
    groups = rows_step // 8
    count = live[0]

    low_rows = slice(tile_rows, tile_rows + extent)
    whole = slice(0, tile_cols)
    rim = slice(tile_cols, tile_cols + extent)
    places = [
        (own, slice(0, tile_rows), whole),
        (below, low_rows, whole),
        (right, slice(0, extent), rim),
        (right_low, slice(extent, tile_rows), rim),
        (corner, low_rows, rim),
    ]
    loads = [
        pltpu.make_async_copy(src, ext.at[:, rows, cols], in_sems.at[n])
        for n, (src, rows, cols) in enumerate(places)
    ]
    loads.append(pltpu.make_async_copy(probe_in, probe, in_sems.at[len(places)]))
    for load in loads:
        load.start()
    grad[...] = jnp.zeros_like(grad)
    probe_sum[...] = jnp.zeros_like(probe_sum)
    for load in loads:
        load.wait()
    lane = lax.broadcasted_iota(jnp.int32, (rows_step, LANES), 1)
    lane3 = lax.broadcasted_iota(jnp.int32, (groups + 1, 8, LANES), 2)
    sublane = lax.broadcasted_iota(jnp.int32, (groups, 8, LANES), 1)
    sublane_tall = lax.broadcasted_iota(jnp.int32, (groups + 1, 8, LANES), 1)

    def rows_of(k, c, rows):
        start = (k * 2 + c) * extent
        return slice(start + rows.start, start + rows.stop)

    def visit(number, row_at, col_at):
        amp_load = pltpu.make_async_copy(amps.at[number], amp, amp_sem)
        amp_load.start()
        shift = lax.rem(col_at, LANES)
        col_base = pl.multiple_of(col_at - shift, LANES)
        back = lax.rem(LANES - shift, LANES)
        wide_cols = extent // LANES + 1
        row_shift = lax.rem(row_at, 8)
        row_base = pl.multiple_of(row_at - row_shift, 8)
        row_back = lax.rem(8 - row_shift, 8)

        for plane in range(2):
            for row in range(0, extent, rows_step):
                turned = []
                for c in range(wide_cols):
                    tall = ext[plane, pl.ds(row_base + row, rows_step + 8), pl.ds(col_base + LANES * c, LANES)]
                    tall = pltpu.roll(tall.reshape(groups + 1, 8, LANES), row_back, 1)
                    flat = jnp.where(sublane < 8 - row_shift, tall[:-1], tall[1:]).reshape(rows_step, LANES)
                    turned.append(pltpu.roll(flat, back, 1))
                for c in range(wide_cols - 1):
                    window[plane, row : row + rows_step, c * LANES : (c + 1) * LANES] = jnp.where(
                        lane < LANES - shift, turned[c], turned[c + 1]
                    )


        def psi(k, step=rows_step):
            for row in range(0, half, step):
                waves_at = []
                for base in (row, half + row):
                    rows = slice(base, base + step)
                    pr, pi = probe[k, 0, rows, :], probe[k, 1, rows, :]
                    o_re, o_im = window[0, rows, :], window[1, rows, :]
                    waves_at.append((pr * o_re - pi * o_im, pr * o_im + pi * o_re))
                for c in range(2):
                    rows = slice(c * half + row, c * half + row + step)
                    waves[k, 0, rows, :] = (waves_at[0][c] + waves_at[1][c]).astype(BF16)
                    waves[k, 1, rows, :] = (waves_at[0][c] - waves_at[1][c]).astype(BF16)

        def left(k):
            for a in range(2):
                z = dot(mats[0, a], waves[k, a])
                left, right_half = z[:, :half], z[:, half:]
                for b, value in enumerate((left + right_half, left - right_half)):
                    value = value.astype(BF16)
                    inner[k, b, a * half : (a + 1) * half, :half] = value[:half]
                    inner[k, b, a * half : (a + 1) * half, half:] = value[half:]

        def right(k):
            for b in range(2):
                f = dot(inner[k, b], mats[1, b])
                far[k, b] = f
                own_power = f[:, :half] * f[:, :half] + f[:, half:] * f[:, half:]
                power[b] = own_power if k == 0 else power[b] + own_power

        def factors():
            amp_load.wait()
            high = amp[...].astype(BF16)
            low = (amp[...] - high.astype(F32)).astype(BF16)
            turned = dot(high, order[...]) + dot(low, order[...])
            for b in range(2):
                sorted_amp[b] = turned[:, b * half : (b + 1) * half]
            for b in range(2):
                for a in range(2):
                    rows = slice(a * half, (a + 1) * half)
                    for_rows = sorted_amp[b, pl.ds(a, half, 2), :]
                    power[b, rows] = 2.0 - 2.0 * for_rows * lax.rsqrt(power[b, rows] + 0.5)

        def back_right(k):
            ys = []
            for b in range(2):
                factor = power[b]
                g = jnp.concatenate([far[k, b, :, :half] * factor, far[k, b, :, half:] * factor], 1)
                ys.append(dot(g.astype(BF16), mats[0, b]))
            for side, y in enumerate((ys[0] + ys[1], ys[0] - ys[1])):
                y = y.astype(BF16)
                cols = slice(side * half, (side + 1) * half)
                for a in range(2):
                    rows = slice(a * half, (a + 1) * half)
                    across[k, a, :half, cols] = y[rows, :half]
                    across[k, a, half:, cols] = y[rows, half:]

        def back_left(k):
            v0 = dot(mats[1, 0], across[k, 0])
            v1 = dot(mats[1, 1], across[k, 1])
            for side, v in enumerate((v0 + v1, v0 - v1)):
                rows = slice(side * half, (side + 1) * half)
                g_re, g_im = v[:half], v[half:]
                pr, pi = probe[k, 0, rows, :], probe[k, 1, rows, :]
                o_re, o_im = window[0, rows, :], window[1, rows, :]
                add_re = pr * g_re + pi * g_im
                add_im = pr * g_im - pi * g_re
                part[0, rows, :] = add_re if k == 0 else part[0, rows, :] + add_re
                part[1, rows, :] = add_im if k == 0 else part[1, rows, :] + add_im
                probe_sum[rows_of(k, 0, rows), :] += o_re * g_re + o_im * g_im
                probe_sum[rows_of(k, 1, rows), :] += o_re * g_im - o_im * g_re

        for stage in (psi, left, right):
            for k in range(modes):
                stage(k)
        factors()
        for stage in (back_right, back_left):
            for k in range(modes):
                stage(k)

        zero = jnp.zeros((groups + 1, 8, LANES), F32)
        edge = jnp.zeros((1, 8, LANES), F32)
        for plane in range(2):
            for row in range(0, extent, rows_step):
                turned = []
                for c in range(wide_cols - 1):
                    flat = part[plane, row : row + rows_step, c * LANES : (c + 1) * LANES]
                    flat = pltpu.roll(flat, shift, 1).reshape(groups, 8, LANES)
                    flat = pltpu.roll(flat, row_shift, 1)
                    low = jnp.concatenate([flat, edge], 0)
                    high = jnp.concatenate([edge, flat], 0)
                    turned.append(jnp.where(sublane_tall >= row_shift, low, high))
                turned = [zero] + turned + [zero]
                for c in range(wide_cols):
                    at = (plane, pl.ds(row_base + row, rows_step + 8), pl.ds(col_base + LANES * c, LANES))
                    value = jnp.where(lane3 >= shift, turned[c + 1], turned[c])
                    grad[at] += value.reshape(rows_step + 8, LANES)

    @pl.loop(0, count)
    def _(number):
        row_at = lax.rem(offsets[number, 0], tile_rows)
        col_at = lax.rem(offsets[number, 1], tile_cols)

        visit(number, row_at, col_at)

    own_half = (lax.axis_index("narrow") & 1) * (probe_sum.shape[0] // 2)
    other_half = probe_sum.shape[0] // 2 - own_half
    pairs = [
        (probe_sum.at[pl.ds(pl.multiple_of(start, 8), probe_sum.shape[0] // 2), :], dst)
        for start, dst in ((other_half, probe_send), (own_half, probe_keep))
    ] + [
        (grad.at[:, low_rows, rim], grad_corner),
        (grad.at[:, low_rows, whole], grad_below),
        (grad.at[:, 0:extent, rim], grad_right),
        (grad.at[:, extent:tile_rows, rim], grad_right_low),
        (grad.at[:, 0:tile_rows, whole], grad_own),
    ]
    stores = [pltpu.make_async_copy(src, dst, out_sems.at[n]) for n, (src, dst) in enumerate(pairs)]
    for store in stores:
        store.start()
    for store in stores:
        store.wait()


def run_slots(offsets, live, own, below, right, right_low, corner, probe, amps):
    extent = probe.shape[2]
    modes = probe.shape[0]
    tile_rows, tile_cols = own.shape[1:]
    mats = jnp.asarray(half_dft(extent))
    order = jnp.asarray(parity_order(extent)).astype(BF16)
    smem = pl.BlockSpec(memory_space=pltpu.SMEM)
    vmem = pl.BlockSpec(memory_space=pltpu.VMEM)
    hbm = pl.BlockSpec(memory_space=pl.ANY)
    grad_shape = (2, tile_rows + extent, tile_cols + extent)
    sum_shape = (modes * 2 * extent, extent)
    half_sum = (sum_shape[0] // 2, extent)
    outs = [(2, tile_rows, tile_cols), (2, extent, tile_cols), (2, extent, extent), (2, tile_rows - extent, extent)]
    outs += [(2, extent, extent), half_sum, half_sum]
    return pl.pallas_call(
        functools.partial(slots_kernel, tile_rows, tile_cols),
        out_shape=[jax.ShapeDtypeStruct(shape, F32) for shape in outs],
        in_specs=[smem, smem] + [hbm] * 7 + [vmem, vmem],
        out_specs=[hbm] * len(outs),
        scratch_shapes=[
            pltpu.VMEM(grad_shape, F32),
            pltpu.VMEM(grad_shape, F32),
            pltpu.VMEM(probe.shape, F32),
            pltpu.VMEM(sum_shape, F32),
            pltpu.VMEM((2, extent, extent), F32),
            pltpu.VMEM((2, extent, extent), F32),
            pltpu.VMEM((extent, extent), F32),
            pltpu.VMEM((2, extent, extent // 2), F32),
            pltpu.VMEM((modes, 2, extent, extent), BF16),
            pltpu.VMEM((modes, 2, extent, extent), BF16),
            pltpu.VMEM((modes, 2, extent, extent), F32),
            pltpu.VMEM((2, extent, extent // 2), F32),
            pltpu.VMEM((modes, 2, extent, extent), BF16),
            pltpu.SemaphoreType.DMA((6,)),
            pltpu.SemaphoreType.DMA(()),
            pltpu.SemaphoreType.DMA((7,)),
        ],
        compiler_params=pltpu.CompilerParams(vmem_limit_bytes=60 * 1024 * 1024),
        name="slots",
    )(offsets, live, own, below, right, right_low, corner, probe, amps, mats, order)


def shifted(value, axis, steps):
    count = lax.axis_size(axis)
    first, last = (max(0, -steps), min(count, count - steps))
    return lax.ppermute(value, axis, [(source, source + steps) for source in range(first, last)])


def place_in(bits):
    linear = lax.axis_index("wide") * lax.axis_size("narrow") + lax.axis_index("narrow")
    place = 0
    for n, bit in enumerate(bits):
        place = place + ((linear // bit) % 2) * (1 << n)
    return place


def partners(bits):
    return [sum(bit for n, bit in enumerate(bits) if step >> n & 1) for step in range(1 << len(bits))]


def swapped(value, mask):
    count = lax.axis_size("wide") * lax.axis_size("narrow")
    return lax.ppermute(value, ("wide", "narrow"), [(source, source ^ mask) for source in range(count)])


def add_kernel(bits, count, *refs):
    ins, outs = refs[:count], refs[count:]
    rows = outs[0].shape[0]
    place = place_in(bits)
    for step, out in enumerate(outs):
        at = pl.ds(pl.multiple_of((place ^ step) * rows, 8), rows)
        out[...] = sum(ref[at, :] for ref in ins)


def add_parts(parts, bits):
    count = 1 << len(bits)
    rows, cols = parts[0].shape
    vmem = pl.BlockSpec(memory_space=pltpu.VMEM)
    return pl.pallas_call(
        functools.partial(add_kernel, bits, len(parts)),
        out_shape=[jax.ShapeDtypeStruct((rows // count, cols), F32)] * count,
        in_specs=[vmem] * len(parts),
        out_specs=[vmem] * count,
        compiler_params=pltpu.CompilerParams(vmem_limit_bytes=8 * 1024 * 1024),
        name="add_parts",
    )(*parts)


def join_kernel(bits, scale, *refs):
    ins, out = refs[:-1], refs[-1]
    rows = ins[0].shape[0]
    place = place_in(bits)
    for step, ref in enumerate(ins):
        at = pl.ds(pl.multiple_of((place ^ step) * rows, 8), rows)
        out[at, :] = ref[...] if scale is None else ref[...] * scale


def join_parts(parts, bits, scale=None):
    rows, cols = parts[0].shape
    vmem = pl.BlockSpec(memory_space=pltpu.VMEM)
    return pl.pallas_call(
        functools.partial(join_kernel, bits, scale),
        out_shape=jax.ShapeDtypeStruct((rows * len(parts), cols), F32),
        in_specs=[vmem] * len(parts),
        out_specs=vmem,
        compiler_params=pltpu.CompilerParams(vmem_limit_bytes=8 * 1024 * 1024),
        name="join_parts",
    )(*parts)


def together(*values):
    return lax.optimization_barrier(values)


def sum_and_shift(keep, send, scale, grad_below, grad_right, grad_right_low, grad_corner):
    narrow, wide = lax.axis_size("narrow"), lax.axis_size("wide")
    bits = [1 << n for n in range((narrow * wide).bit_length() - 1)]
    groups = [(bits[1],)] + [tuple(bits[n : n + 2]) for n in range(2, len(bits), 2)]
    parts = [keep, swapped(send, bits[0])]
    came_right_low = shifted(grad_right_low, "wide", 1)
    for n, group in enumerate(groups):
        pieces = add_parts(parts, group)
        if n == 1:
            pieces, grad_corner = together(pieces, grad_corner)
            came_corner = shifted(grad_corner, "narrow", 1)
        if n == 2:
            pieces, grad_below = together(pieces, grad_below)
            came_below = shifted(grad_below, "narrow", 1)
        parts = [pieces[0]] + [swapped(piece, mask) for piece, mask in zip(pieces[1:], partners(group)[1:])]
        if n == 0:
            parts, came_right_low = together(parts, came_right_low)
    value = add_parts(parts, ())[0]
    for group in reversed(groups):
        if group == groups[0]:
            value, grad_right = together(value, grad_right + came_corner)
            came_right = shifted(grad_right, "wide", 1)
        parts = [value] + [swapped(value, mask) for mask in partners(group)[1:]]
        if group == groups[-1]:
            parts, came_below = together(parts, came_below)
        if group != groups[0]:
            value = join_parts(parts, group)
    parts = parts + [swapped(part, bits[0]) for part in parts]
    return join_parts(parts, groups[0] + (bits[0],), scale), came_below, came_right, came_right_low


def on_device(object_field, probe, amplitudes, offsets, live):
    extent = probe.shape[2]
    top = object_field[:, :extent]
    right = shifted(top, "wide", -1)
    below = shifted(top, "narrow", -1)
    right_low = shifted(object_field[:, extent:], "wide", -1)
    corner = shifted(right, "narrow", -1)
    grad_own, grad_below, grad_right, grad_right_low, grad_corner, keep, send = run_slots(
        offsets, live, object_field, below, right, right_low, corner, probe, amplitudes
    )
    total_slots = lax.axis_size("wide") * lax.axis_size("narrow") * offsets.shape[0]
    probe_grad, came_below, came_right, came_right_low = sum_and_shift(
        keep, send, 1.0 / math.sqrt(total_slots), grad_below, grad_right, grad_right_low, grad_corner
    )
    rims = jnp.concatenate([came_right, came_right_low], 1)
    object_grad = grad_own.at[:, :extent, :].add(came_below).at[:, :, :extent].add(rims)
    return (object_grad, probe_grad.reshape(probe.shape))


def solution(mesh):
    return jax.shard_map(
        on_device,
        mesh=mesh,
        in_specs=(
            P(None, "narrow", "wide"),
            P(),
            P(("wide", "narrow"), None, None),
            P(("wide", "narrow"), None),
            P(("wide", "narrow")),
        ),
        out_specs=(P(None, "narrow", "wide"), P()),
        check_vma=False,
    )
```

```python
import functools
import math

import jax
import jax.numpy as jnp
import ml_dtypes
import numpy as np
from jax import lax
from jax.experimental import pallas as pl
from jax.experimental.pallas import tpu as pltpu
from jax.sharding import PartitionSpec as P

F32 = jnp.float32
BF16 = jnp.bfloat16
LANES = 128


def half_dft(extent):
    half = extent // 2
    blocks = []
    for parity in range(2):
        freq = 2 * np.arange(half)[:, None] + parity
        angles = (freq * np.arange(half)[None, :] % extent) * (2.0 * math.pi / extent)
        cosine = np.cos(angles) / math.sqrt(extent)
        sine = np.sin(angles) / math.sqrt(extent)
        blocks.append(np.block([[cosine, sine], [-sine, cosine]]))
    both = np.stack(blocks)
    return np.stack([both, np.swapaxes(both, 1, 2)]).astype(ml_dtypes.bfloat16)


def parity_order(extent):
    order = np.concatenate([np.arange(0, extent, 2), np.arange(1, extent, 2)])
    matrix = np.zeros((extent, extent), np.float32)
    matrix[order, np.arange(extent)] = 1.0
    return matrix


def dot(a, b):
    return jnp.dot(a, b, preferred_element_type=F32)


def slots_kernel(
    tile_rows, tile_cols, offsets, live, own, below, right, right_low, corner, probe_in, amps, mats, order,
    grad_own, grad_below, grad_right, grad_right_low, grad_corner, probe_keep, probe_send,
    ext, grad, probe, probe_sum, window, part, amp, sorted_amp, waves, inner, far, power, across,
    in_sems, amp_sem, out_sems,
):
    modes = probe.shape[0]
    extent = probe.shape[2]
    half = extent // 2
    rows_step = 32
    groups = rows_step // 8
    count = live[0]

    low_rows = slice(tile_rows, tile_rows + extent)
    whole = slice(0, tile_cols)
    rim = slice(tile_cols, tile_cols + extent)
    places = [
        (own, slice(0, tile_rows), whole),
        (below, low_rows, whole),
        (right, slice(0, extent), rim),
        (right_low, slice(extent, tile_rows), rim),
        (corner, low_rows, rim),
    ]
    loads = [
        pltpu.make_async_copy(src, ext.at[:, rows, cols], in_sems.at[n])
        for n, (src, rows, cols) in enumerate(places)
    ]
    loads.append(pltpu.make_async_copy(probe_in, probe, in_sems.at[len(places)]))
    for load in loads:
        load.start()
    grad[...] = jnp.zeros_like(grad)
    probe_sum[...] = jnp.zeros_like(probe_sum)
    for load in loads:
        load.wait()
    lane = lax.broadcasted_iota(jnp.int32, (rows_step, LANES), 1)
    lane3 = lax.broadcasted_iota(jnp.int32, (groups + 1, 8, LANES), 2)
    sublane = lax.broadcasted_iota(jnp.int32, (groups, 8, LANES), 1)
    sublane_tall = lax.broadcasted_iota(jnp.int32, (groups + 1, 8, LANES), 1)

    def rows_of(k, c, rows):
        start = (k * 2 + c) * extent
        return slice(start + rows.start, start + rows.stop)

    def visit(number, row_at, col_at):
        amp_load = pltpu.make_async_copy(amps.at[number], amp, amp_sem)
        amp_load.start()
        shift = lax.rem(col_at, LANES)
        col_base = pl.multiple_of(col_at - shift, LANES)
        back = lax.rem(LANES - shift, LANES)
        wide_cols = extent // LANES + 1
        row_shift = lax.rem(row_at, 8)
        row_base = pl.multiple_of(row_at - row_shift, 8)
        row_back = lax.rem(8 - row_shift, 8)

        for plane in range(2):
            for row in range(0, extent, rows_step):
                turned = []
                for c in range(wide_cols):
                    tall = ext[plane, pl.ds(row_base + row, rows_step + 8), pl.ds(col_base + LANES * c, LANES)]
                    tall = pltpu.roll(tall.reshape(groups + 1, 8, LANES), row_back, 1)
                    flat = jnp.where(sublane < 8 - row_shift, tall[:-1], tall[1:]).reshape(rows_step, LANES)
                    turned.append(pltpu.roll(flat, back, 1))
                for c in range(wide_cols - 1):
                    window[plane, row : row + rows_step, c * LANES : (c + 1) * LANES] = jnp.where(
                        lane < LANES - shift, turned[c], turned[c + 1]
                    )


        def psi(k, step=rows_step):
            for row in range(0, half, step):
                waves_at = []
                for base in (row, half + row):
                    rows = slice(base, base + step)
                    pr, pi = probe[k, 0, rows, :], probe[k, 1, rows, :]
                    o_re, o_im = window[0, rows, :], window[1, rows, :]
                    waves_at.append((pr * o_re - pi * o_im, pr * o_im + pi * o_re))
                for c in range(2):
                    rows = slice(c * half + row, c * half + row + step)
                    waves[k, 0, rows, :] = (waves_at[0][c] + waves_at[1][c]).astype(BF16)
                    waves[k, 1, rows, :] = (waves_at[0][c] - waves_at[1][c]).astype(BF16)

        def left(k):
            for a in range(2):
                z = dot(mats[0, a], waves[k, a])
                left, right_half = z[:, :half], z[:, half:]
                for b, value in enumerate((left + right_half, left - right_half)):
                    value = value.astype(BF16)
                    inner[k, b, a * half : (a + 1) * half, :half] = value[:half]
                    inner[k, b, a * half : (a + 1) * half, half:] = value[half:]

        def right(k):
            for b in range(2):
                f = dot(inner[k, b], mats[1, b])
                far[k, b] = f
                own_power = f[:, :half] * f[:, :half] + f[:, half:] * f[:, half:]
                power[b] = own_power if k == 0 else power[b] + own_power

        def factors():
            amp_load.wait()
            high = amp[...].astype(BF16)
            low = (amp[...] - high.astype(F32)).astype(BF16)
            turned = dot(high, order[...]) + dot(low, order[...])
            for b in range(2):
                sorted_amp[b] = turned[:, b * half : (b + 1) * half]
            for b in range(2):
                for a in range(2):
                    rows = slice(a * half, (a + 1) * half)
                    for_rows = sorted_amp[b, pl.ds(a, half, 2), :]
                    power[b, rows] = 2.0 - 2.0 * for_rows * lax.rsqrt(power[b, rows] + 0.5)

        def back_right(k):
            ys = []
            for b in range(2):
                factor = power[b]
                g = jnp.concatenate([far[k, b, :, :half] * factor, far[k, b, :, half:] * factor], 1)
                ys.append(dot(g.astype(BF16), mats[0, b]))
            for side, y in enumerate((ys[0] + ys[1], ys[0] - ys[1])):
                y = y.astype(BF16)
                cols = slice(side * half, (side + 1) * half)
                for a in range(2):
                    rows = slice(a * half, (a + 1) * half)
                    across[k, a, :half, cols] = y[rows, :half]
                    across[k, a, half:, cols] = y[rows, half:]

        def back_left(k):
            v0 = dot(mats[1, 0], across[k, 0])
            v1 = dot(mats[1, 1], across[k, 1])
            for side, v in enumerate((v0 + v1, v0 - v1)):
                rows = slice(side * half, (side + 1) * half)
                g_re, g_im = v[:half], v[half:]
                pr, pi = probe[k, 0, rows, :], probe[k, 1, rows, :]
                o_re, o_im = window[0, rows, :], window[1, rows, :]
                add_re = pr * g_re + pi * g_im
                add_im = pr * g_im - pi * g_re
                part[0, rows, :] = add_re if k == 0 else part[0, rows, :] + add_re
                part[1, rows, :] = add_im if k == 0 else part[1, rows, :] + add_im
                probe_sum[rows_of(k, 0, rows), :] += o_re * g_re + o_im * g_im
                probe_sum[rows_of(k, 1, rows), :] += o_re * g_im - o_im * g_re

        for stage in (psi, left, right):
            for k in range(modes):
                stage(k)
        factors()
        for stage in (back_right, back_left):
            for k in range(modes):
                stage(k)

        zero = jnp.zeros((groups + 1, 8, LANES), F32)
        edge = jnp.zeros((1, 8, LANES), F32)
        for plane in range(2):
            for row in range(0, extent, rows_step):
                turned = []
                for c in range(wide_cols - 1):
                    flat = part[plane, row : row + rows_step, c * LANES : (c + 1) * LANES]
                    flat = pltpu.roll(flat, shift, 1).reshape(groups, 8, LANES)
                    flat = pltpu.roll(flat, row_shift, 1)
                    low = jnp.concatenate([flat, edge], 0)
                    high = jnp.concatenate([edge, flat], 0)
                    turned.append(jnp.where(sublane_tall >= row_shift, low, high))
                turned = [zero] + turned + [zero]
                for c in range(wide_cols):
                    at = (plane, pl.ds(row_base + row, rows_step + 8), pl.ds(col_base + LANES * c, LANES))
                    value = jnp.where(lane3 >= shift, turned[c + 1], turned[c])
                    grad[at] += value.reshape(rows_step + 8, LANES)

    @pl.loop(0, count)
    def _(number):
        row_at = lax.rem(offsets[number, 0], tile_rows)
        col_at = lax.rem(offsets[number, 1], tile_cols)

        visit(number, row_at, col_at)

    own_half = (lax.axis_index("narrow") & 1) * (probe_sum.shape[0] // 2)
    other_half = probe_sum.shape[0] // 2 - own_half
    pairs = [
        (probe_sum.at[pl.ds(pl.multiple_of(start, 8), probe_sum.shape[0] // 2), :], dst)
        for start, dst in ((other_half, probe_send), (own_half, probe_keep))
    ] + [
        (grad.at[:, low_rows, rim], grad_corner),
        (grad.at[:, low_rows, whole], grad_below),
        (grad.at[:, 0:extent, rim], grad_right),
        (grad.at[:, extent:tile_rows, rim], grad_right_low),
        (grad.at[:, 0:tile_rows, whole], grad_own),
    ]
    stores = [pltpu.make_async_copy(src, dst, out_sems.at[n]) for n, (src, dst) in enumerate(pairs)]
    for store in stores:
        store.start()
    for store in stores:
        store.wait()


def run_slots(offsets, live, own, below, right, right_low, corner, probe, amps):
    extent = probe.shape[2]
    modes = probe.shape[0]
    tile_rows, tile_cols = own.shape[1:]
    mats = jnp.asarray(half_dft(extent))
    order = jnp.asarray(parity_order(extent)).astype(BF16)
    smem = pl.BlockSpec(memory_space=pltpu.SMEM)
    vmem = pl.BlockSpec(memory_space=pltpu.VMEM)
    hbm = pl.BlockSpec(memory_space=pltpu.HBM)
    anywhere = pl.BlockSpec(memory_space=pl.ANY)
    grad_shape = (2, tile_rows + extent, tile_cols + extent)
    sum_shape = (modes * 2 * extent, extent)
    half_sum = (sum_shape[0] // 2, extent)
    outs = [(2, tile_rows, tile_cols), (2, extent, tile_cols), (2, extent, extent), (2, tile_rows - extent, extent)]
    outs += [(2, extent, extent), half_sum, half_sum]
    return pl.pallas_call(
        functools.partial(slots_kernel, tile_rows, tile_cols),
        out_shape=[jax.ShapeDtypeStruct(shape, F32) for shape in outs],
        in_specs=[smem, smem, hbm] + [anywhere] * 4 + [hbm, hbm, vmem, vmem],
        out_specs=[anywhere] * len(outs),
        scratch_shapes=[
            pltpu.VMEM(grad_shape, F32),
            pltpu.VMEM(grad_shape, F32),
            pltpu.VMEM(probe.shape, F32),
            pltpu.VMEM(sum_shape, F32),
            pltpu.VMEM((2, extent, extent), F32),
            pltpu.VMEM((2, extent, extent), F32),
            pltpu.VMEM((extent, extent), F32),
            pltpu.VMEM((2, extent, extent // 2), F32),
            pltpu.VMEM((modes, 2, extent, extent), BF16),
            pltpu.VMEM((modes, 2, extent, extent), BF16),
            pltpu.VMEM((modes, 2, extent, extent), F32),
            pltpu.VMEM((2, extent, extent // 2), F32),
            pltpu.VMEM((modes, 2, extent, extent), BF16),
            pltpu.SemaphoreType.DMA((6,)),
            pltpu.SemaphoreType.DMA(()),
            pltpu.SemaphoreType.DMA((7,)),
        ],
        compiler_params=pltpu.CompilerParams(vmem_limit_bytes=44 * 1024 * 1024),
        name="slots",
    )(offsets, live, own, below, right, right_low, corner, probe, amps, mats, order)


def shifted(value, axis, steps):
    count = lax.axis_size(axis)
    first, last = (max(0, -steps), min(count, count - steps))
    return lax.ppermute(value, axis, [(source, source + steps) for source in range(first, last)])


def place_in(bits):
    linear = lax.axis_index("wide") * lax.axis_size("narrow") + lax.axis_index("narrow")
    place = 0
    for n, bit in enumerate(bits):
        place = place + ((linear // bit) % 2) * (1 << n)
    return place


def partners(bits):
    return [sum(bit for n, bit in enumerate(bits) if step >> n & 1) for step in range(1 << len(bits))]


def swapped(value, mask):
    count = lax.axis_size("wide") * lax.axis_size("narrow")
    return lax.ppermute(value, ("wide", "narrow"), [(source, source ^ mask) for source in range(count)])


def add_kernel(bits, count, *refs):
    ins, outs = refs[:count], refs[count:]
    rows = outs[0].shape[0]
    place = place_in(bits)
    for step, out in enumerate(outs):
        at = pl.ds(pl.multiple_of((place ^ step) * rows, 8), rows)
        out[...] = sum(ref[at, :] for ref in ins)


def add_parts(parts, bits):
    count = 1 << len(bits)
    rows, cols = parts[0].shape
    vmem = pl.BlockSpec(memory_space=pltpu.VMEM)
    return pl.pallas_call(
        functools.partial(add_kernel, bits, len(parts)),
        out_shape=[jax.ShapeDtypeStruct((rows // count, cols), F32)] * count,
        in_specs=[vmem] * len(parts),
        out_specs=[vmem] * count,
        compiler_params=pltpu.CompilerParams(vmem_limit_bytes=8 * 1024 * 1024),
        name="add_parts",
    )(*parts)


def join_kernel(bits, scale, *refs):
    ins, out = refs[:-1], refs[-1]
    rows = ins[0].shape[0]
    place = place_in(bits)
    for step, ref in enumerate(ins):
        at = pl.ds(pl.multiple_of((place ^ step) * rows, 8), rows)
        out[at, :] = ref[...] if scale is None else ref[...] * scale


def join_parts(parts, bits, scale=None):
    rows, cols = parts[0].shape
    vmem = pl.BlockSpec(memory_space=pltpu.VMEM)
    return pl.pallas_call(
        functools.partial(join_kernel, bits, scale),
        out_shape=jax.ShapeDtypeStruct((rows * len(parts), cols), F32),
        in_specs=[vmem] * len(parts),
        out_specs=vmem,
        compiler_params=pltpu.CompilerParams(vmem_limit_bytes=8 * 1024 * 1024),
        name="join_parts",
    )(*parts)


def together(*values):
    return lax.optimization_barrier(values)


def sum_and_shift(keep, send, scale, grad_below, grad_right, grad_right_low, grad_corner):
    narrow, wide = lax.axis_size("narrow"), lax.axis_size("wide")
    bits = [1 << n for n in range((narrow * wide).bit_length() - 1)]
    groups = [(bits[1],)] + [tuple(bits[n : n + 2]) for n in range(2, len(bits), 2)]
    parts = [keep, swapped(send, bits[0])]
    came_right_low = shifted(grad_right_low, "wide", 1)
    for n, group in enumerate(groups):
        pieces = add_parts(parts, group)
        if n == 1:
            pieces, grad_corner = together(pieces, grad_corner)
            came_corner = shifted(grad_corner, "narrow", 1)
        if n == 2:
            pieces, grad_below = together(pieces, grad_below)
            came_below = shifted(grad_below, "narrow", 1)
        parts = [pieces[0]] + [swapped(piece, mask) for piece, mask in zip(pieces[1:], partners(group)[1:])]
        if n == 0:
            parts, came_right_low = together(parts, came_right_low)
    value = add_parts(parts, ())[0]
    for group in reversed(groups):
        if group == groups[0]:
            value, grad_right = together(value, grad_right + came_corner)
            came_right = shifted(grad_right, "wide", 1)
        parts = [value] + [swapped(value, mask) for mask in partners(group)[1:]]
        if group == groups[-1]:
            parts, came_below = together(parts, came_below)
        if group != groups[0]:
            value = join_parts(parts, group)
    parts = parts + [swapped(part, bits[0]) for part in parts]
    return join_parts(parts, groups[0] + (bits[0],), scale), came_below, came_right, came_right_low


def on_device(object_field, probe, amplitudes, offsets, live):
    extent = probe.shape[2]
    top = object_field[:, :extent]
    right = shifted(top, "wide", -1)
    below = shifted(top, "narrow", -1)
    right_low = shifted(object_field[:, extent:], "wide", -1)
    corner = shifted(right, "narrow", -1)
    grad_own, grad_below, grad_right, grad_right_low, grad_corner, keep, send = run_slots(
        offsets, live, object_field, below, right, right_low, corner, probe, amplitudes
    )
    total_slots = lax.axis_size("wide") * lax.axis_size("narrow") * offsets.shape[0]
    probe_grad, came_below, came_right, came_right_low = sum_and_shift(
        keep, send, 1.0 / math.sqrt(total_slots), grad_below, grad_right, grad_right_low, grad_corner
    )
    rims = jnp.concatenate([came_right, came_right_low], 1)
    object_grad = grad_own.at[:, :extent, :].add(came_below).at[:, :, :extent].add(rims)
    return (object_grad, probe_grad.reshape(probe.shape))


def solution(mesh):
    return jax.shard_map(
        on_device,
        mesh=mesh,
        in_specs=(
            P(None, "narrow", "wide"),
            P(),
            P(("wide", "narrow"), None, None),
            P(("wide", "narrow"), None),
            P(("wide", "narrow")),
        ),
        out_specs=(P(None, "narrow", "wide"), P()),
        check_vma=False,
    )
```

```python
import functools
import math

import jax
import jax.numpy as jnp
import ml_dtypes
import numpy as np
from jax import lax
from jax.experimental import pallas as pl
from jax.experimental.pallas import tpu as pltpu
from jax.sharding import PartitionSpec as P

F32 = jnp.float32
BF16 = jnp.bfloat16
LANES = 128


def half_dft(extent):
    half = extent // 2
    blocks = []
    for parity in range(2):
        freq = 2 * np.arange(half)[:, None] + parity
        angles = (freq * np.arange(half)[None, :] % extent) * (2.0 * math.pi / extent)
        cosine = np.cos(angles) / math.sqrt(extent)
        sine = np.sin(angles) / math.sqrt(extent)
        blocks.append(np.block([[cosine, sine], [-sine, cosine]]))
    both = np.stack(blocks)
    return np.stack([both, np.swapaxes(both, 1, 2)]).astype(ml_dtypes.bfloat16)


def parity_order(extent):
    order = np.concatenate([np.arange(0, extent, 2), np.arange(1, extent, 2)])
    matrix = np.zeros((extent, extent), np.float32)
    matrix[order, np.arange(extent)] = 1.0
    return matrix


def dot(a, b):
    return jnp.dot(a, b, preferred_element_type=F32)


def slots_kernel(
    tile_rows, tile_cols, offsets, live, own, below, right, right_low, corner, probe_in, amps, mats, order,
    grad_own, grad_below, grad_right, grad_corner, probe_keep, probe_send,
    ext, grad, probe, probe_sum, window, part, amp, sorted_amp, waves, inner, far, power, across,
    in_sems, amp_sem, out_sems,
):
    modes = probe.shape[0]
    extent = probe.shape[2]
    half = extent // 2
    rows_step = 32
    groups = rows_step // 8
    count = live[0]

    low_rows = slice(tile_rows, tile_rows + extent)
    whole = slice(0, tile_cols)
    rim = slice(tile_cols, tile_cols + extent)
    places = [
        (own, slice(0, tile_rows), whole),
        (below, low_rows, whole),
        (right, slice(0, extent), rim),
        (right_low, slice(extent, tile_rows), rim),
        (corner, low_rows, rim),
    ]
    loads = [
        pltpu.make_async_copy(src, ext.at[:, rows, cols], in_sems.at[n])
        for n, (src, rows, cols) in enumerate(places)
    ]
    loads.append(pltpu.make_async_copy(probe_in, probe, in_sems.at[len(places)]))
    for load in loads:
        load.start()
    grad[...] = jnp.zeros_like(grad)
    probe_sum[...] = jnp.zeros_like(probe_sum)
    for load in loads:
        load.wait()
    lane = lax.broadcasted_iota(jnp.int32, (rows_step, LANES), 1)
    lane3 = lax.broadcasted_iota(jnp.int32, (groups + 1, 8, LANES), 2)
    sublane = lax.broadcasted_iota(jnp.int32, (groups, 8, LANES), 1)
    sublane_tall = lax.broadcasted_iota(jnp.int32, (groups + 1, 8, LANES), 1)

    def rows_of(k, c, rows):
        start = (k * 2 + c) * extent
        return slice(start + rows.start, start + rows.stop)

    def visit(number, row_at, col_at):
        amp_load = pltpu.make_async_copy(amps.at[number], amp, amp_sem)
        amp_load.start()
        shift = lax.rem(col_at, LANES)
        col_base = pl.multiple_of(col_at - shift, LANES)
        back = lax.rem(LANES - shift, LANES)
        wide_cols = extent // LANES + 1
        row_shift = lax.rem(row_at, 8)
        row_base = pl.multiple_of(row_at - row_shift, 8)
        row_back = lax.rem(8 - row_shift, 8)

        for plane in range(2):
            for row in range(0, extent, rows_step):
                turned = []
                for c in range(wide_cols):
                    tall = ext[plane, pl.ds(row_base + row, rows_step + 8), pl.ds(col_base + LANES * c, LANES)]
                    tall = pltpu.roll(tall.reshape(groups + 1, 8, LANES), row_back, 1)
                    flat = jnp.where(sublane < 8 - row_shift, tall[:-1], tall[1:]).reshape(rows_step, LANES)
                    turned.append(pltpu.roll(flat, back, 1))
                for c in range(wide_cols - 1):
                    window[plane, row : row + rows_step, c * LANES : (c + 1) * LANES] = jnp.where(
                        lane < LANES - shift, turned[c], turned[c + 1]
                    )


        def psi(k, step=rows_step):
            for row in range(0, half, step):
                waves_at = []
                for base in (row, half + row):
                    rows = slice(base, base + step)
                    pr, pi = probe[k, 0, rows, :], probe[k, 1, rows, :]
                    o_re, o_im = window[0, rows, :], window[1, rows, :]
                    waves_at.append((pr * o_re - pi * o_im, pr * o_im + pi * o_re))
                for c in range(2):
                    rows = slice(c * half + row, c * half + row + step)
                    waves[k, 0, rows, :] = (waves_at[0][c] + waves_at[1][c]).astype(BF16)
                    waves[k, 1, rows, :] = (waves_at[0][c] - waves_at[1][c]).astype(BF16)

        def left(k):
            for a in range(2):
                z = dot(mats[0, a], waves[k, a])
                left, right_half = z[:, :half], z[:, half:]
                for b, value in enumerate((left + right_half, left - right_half)):
                    value = value.astype(BF16)
                    inner[k, b, a * half : (a + 1) * half, :half] = value[:half]
                    inner[k, b, a * half : (a + 1) * half, half:] = value[half:]

        def right(k):
            for b in range(2):
                f = dot(inner[k, b], mats[1, b])
                far[k, b] = f
                own_power = f[:, :half] * f[:, :half] + f[:, half:] * f[:, half:]
                power[b] = own_power if k == 0 else power[b] + own_power

        def factors():
            amp_load.wait()
            high = amp[...].astype(BF16)
            low = (amp[...] - high.astype(F32)).astype(BF16)
            turned = dot(high, order[...]) + dot(low, order[...])
            for b in range(2):
                sorted_amp[b] = turned[:, b * half : (b + 1) * half]
            for b in range(2):
                for a in range(2):
                    rows = slice(a * half, (a + 1) * half)
                    for_rows = sorted_amp[b, pl.ds(a, half, 2), :]
                    power[b, rows] = 2.0 - 2.0 * for_rows * lax.rsqrt(power[b, rows] + 0.5)

        def back_right(k):
            ys = []
            for b in range(2):
                factor = power[b]
                g = jnp.concatenate([far[k, b, :, :half] * factor, far[k, b, :, half:] * factor], 1)
                ys.append(dot(g.astype(BF16), mats[0, b]))
            for side, y in enumerate((ys[0] + ys[1], ys[0] - ys[1])):
                y = y.astype(BF16)
                cols = slice(side * half, (side + 1) * half)
                for a in range(2):
                    rows = slice(a * half, (a + 1) * half)
                    across[k, a, :half, cols] = y[rows, :half]
                    across[k, a, half:, cols] = y[rows, half:]

        def back_left(k):
            v0 = dot(mats[1, 0], across[k, 0])
            v1 = dot(mats[1, 1], across[k, 1])
            for side, v in enumerate((v0 + v1, v0 - v1)):
                rows = slice(side * half, (side + 1) * half)
                g_re, g_im = v[:half], v[half:]
                pr, pi = probe[k, 0, rows, :], probe[k, 1, rows, :]
                o_re, o_im = window[0, rows, :], window[1, rows, :]
                add_re = pr * g_re + pi * g_im
                add_im = pr * g_im - pi * g_re
                part[0, rows, :] = add_re if k == 0 else part[0, rows, :] + add_re
                part[1, rows, :] = add_im if k == 0 else part[1, rows, :] + add_im
                probe_sum[rows_of(k, 0, rows), :] += o_re * g_re + o_im * g_im
                probe_sum[rows_of(k, 1, rows), :] += o_re * g_im - o_im * g_re

        for stage in (psi, left, right):
            for k in range(modes):
                stage(k)
        factors()
        for stage in (back_right, back_left):
            for k in range(modes):
                stage(k)

        zero = jnp.zeros((groups + 1, 8, LANES), F32)
        edge = jnp.zeros((1, 8, LANES), F32)
        for plane in range(2):
            for row in range(0, extent, rows_step):
                turned = []
                for c in range(wide_cols - 1):
                    flat = part[plane, row : row + rows_step, c * LANES : (c + 1) * LANES]
                    flat = pltpu.roll(flat, shift, 1).reshape(groups, 8, LANES)
                    flat = pltpu.roll(flat, row_shift, 1)
                    low = jnp.concatenate([flat, edge], 0)
                    high = jnp.concatenate([edge, flat], 0)
                    turned.append(jnp.where(sublane_tall >= row_shift, low, high))
                turned = [zero] + turned + [zero]
                for c in range(wide_cols):
                    at = (plane, pl.ds(row_base + row, rows_step + 8), pl.ds(col_base + LANES * c, LANES))
                    value = jnp.where(lane3 >= shift, turned[c + 1], turned[c])
                    grad[at] += value.reshape(rows_step + 8, LANES)

    @pl.loop(0, count)
    def _(number):
        row_at = lax.rem(offsets[number, 0], tile_rows)
        col_at = lax.rem(offsets[number, 1], tile_cols)

        visit(number, row_at, col_at)

    own_half = (lax.axis_index("narrow") & 1) * (probe_sum.shape[0] // 2)
    other_half = probe_sum.shape[0] // 2 - own_half
    pairs = [
        (probe_sum.at[pl.ds(pl.multiple_of(start, 8), probe_sum.shape[0] // 2), :], dst)
        for start, dst in ((other_half, probe_send), (own_half, probe_keep))
    ] + [
        (grad.at[:, low_rows, rim], grad_corner),
        (grad.at[:, low_rows, whole], grad_below),
        (grad.at[:, 0:tile_rows, rim], grad_right),
        (grad.at[:, 0:tile_rows, whole], grad_own),
    ]
    stores = [pltpu.make_async_copy(src, dst, out_sems.at[n]) for n, (src, dst) in enumerate(pairs)]
    for store in stores:
        store.start()
    for store in stores:
        store.wait()


def run_slots(offsets, live, own, below, right, right_low, corner, probe, amps):
    extent = probe.shape[2]
    modes = probe.shape[0]
    tile_rows, tile_cols = own.shape[1:]
    mats = jnp.asarray(half_dft(extent))
    order = jnp.asarray(parity_order(extent)).astype(BF16)
    smem = pl.BlockSpec(memory_space=pltpu.SMEM)
    vmem = pl.BlockSpec(memory_space=pltpu.VMEM)
    hbm = pl.BlockSpec(memory_space=pltpu.HBM)
    anywhere = pl.BlockSpec(memory_space=pl.ANY)
    grad_shape = (2, tile_rows + extent, tile_cols + extent)
    sum_shape = (modes * 2 * extent, extent)
    half_sum = (sum_shape[0] // 2, extent)
    outs = [(2, tile_rows, tile_cols), (2, extent, tile_cols), (2, tile_rows, extent), (2, extent, extent)]
    outs += [half_sum, half_sum]
    return pl.pallas_call(
        functools.partial(slots_kernel, tile_rows, tile_cols),
        out_shape=[jax.ShapeDtypeStruct(shape, F32) for shape in outs],
        in_specs=[smem, smem, hbm] + [anywhere] * 4 + [hbm, hbm, vmem, vmem],
        out_specs=[anywhere] * len(outs),
        scratch_shapes=[
            pltpu.VMEM(grad_shape, F32),
            pltpu.VMEM(grad_shape, F32),
            pltpu.VMEM(probe.shape, F32),
            pltpu.VMEM(sum_shape, F32),
            pltpu.VMEM((2, extent, extent), F32),
            pltpu.VMEM((2, extent, extent), F32),
            pltpu.VMEM((extent, extent), F32),
            pltpu.VMEM((2, extent, extent // 2), F32),
            pltpu.VMEM((modes, 2, extent, extent), BF16),
            pltpu.VMEM((modes, 2, extent, extent), BF16),
            pltpu.VMEM((modes, 2, extent, extent), F32),
            pltpu.VMEM((2, extent, extent // 2), F32),
            pltpu.VMEM((modes, 2, extent, extent), BF16),
            pltpu.SemaphoreType.DMA((6,)),
            pltpu.SemaphoreType.DMA(()),
            pltpu.SemaphoreType.DMA((6,)),
        ],
        compiler_params=pltpu.CompilerParams(vmem_limit_bytes=44 * 1024 * 1024),
        name="slots",
    )(offsets, live, own, below, right, right_low, corner, probe, amps, mats, order)


def shifted(value, axis, steps):
    count = lax.axis_size(axis)
    first, last = (max(0, -steps), min(count, count - steps))
    return lax.ppermute(value, axis, [(source, source + steps) for source in range(first, last)])


def place_in(bits):
    linear = lax.axis_index("wide") * lax.axis_size("narrow") + lax.axis_index("narrow")
    place = 0
    for n, bit in enumerate(bits):
        place = place + ((linear // bit) % 2) * (1 << n)
    return place


def partners(bits):
    return [sum(bit for n, bit in enumerate(bits) if step >> n & 1) for step in range(1 << len(bits))]


def swapped(value, mask):
    count = lax.axis_size("wide") * lax.axis_size("narrow")
    return lax.ppermute(value, ("wide", "narrow"), [(source, source ^ mask) for source in range(count)])


def add_kernel(bits, count, *refs):
    ins, outs = refs[:count], refs[count:]
    rows = outs[0].shape[0]
    place = place_in(bits)
    for step, out in enumerate(outs):
        at = pl.ds(pl.multiple_of((place ^ step) * rows, 8), rows)
        out[...] = sum(ref[at, :] for ref in ins)


def add_parts(parts, bits):
    count = 1 << len(bits)
    rows, cols = parts[0].shape
    vmem = pl.BlockSpec(memory_space=pltpu.VMEM)
    return pl.pallas_call(
        functools.partial(add_kernel, bits, len(parts)),
        out_shape=[jax.ShapeDtypeStruct((rows // count, cols), F32)] * count,
        in_specs=[vmem] * len(parts),
        out_specs=[vmem] * count,
        compiler_params=pltpu.CompilerParams(vmem_limit_bytes=8 * 1024 * 1024),
        name="add_parts",
    )(*parts)


def join_kernel(bits, scale, *refs):
    ins, out = refs[:-1], refs[-1]
    rows = ins[0].shape[0]
    place = place_in(bits)
    for step, ref in enumerate(ins):
        at = pl.ds(pl.multiple_of((place ^ step) * rows, 8), rows)
        out[at, :] = ref[...] if scale is None else ref[...] * scale


def join_parts(parts, bits, scale=None):
    rows, cols = parts[0].shape
    vmem = pl.BlockSpec(memory_space=pltpu.VMEM)
    return pl.pallas_call(
        functools.partial(join_kernel, bits, scale),
        out_shape=jax.ShapeDtypeStruct((rows * len(parts), cols), F32),
        in_specs=[vmem] * len(parts),
        out_specs=vmem,
        compiler_params=pltpu.CompilerParams(vmem_limit_bytes=8 * 1024 * 1024),
        name="join_parts",
    )(*parts)


def together(*values):
    return lax.optimization_barrier(values)


def sum_everywhere(keep, send, scale, beside):
    narrow, wide = lax.axis_size("narrow"), lax.axis_size("wide")
    bits = [1 << n for n in range((narrow * wide).bit_length() - 1)]
    groups = [(bits[1],)] + [tuple(bits[n : n + 2]) for n in range(2, len(bits), 2)]
    parts = [keep, swapped(send, bits[0])]
    for n, group in enumerate(groups):
        pieces = add_parts(parts, group)
        parts = [pieces[0]] + [swapped(piece, mask) for piece, mask in zip(pieces[1:], partners(group)[1:])]
        if n == 1:
            parts, beside = together(parts, beside)
    value = add_parts(parts, ())[0]
    for group in reversed(groups):
        parts = [value] + [swapped(value, mask) for mask in partners(group)[1:]]
        if group != groups[0]:
            value = join_parts(parts, group)
    parts = parts + [swapped(part, bits[0]) for part in parts]
    return join_parts(parts, groups[0] + (bits[0],), scale), beside


def on_device(object_field, probe, amplitudes, offsets, live):
    extent = probe.shape[2]
    top = object_field[:, :extent]
    right = shifted(top, "wide", -1)
    below = shifted(top, "narrow", -1)
    right_low = shifted(object_field[:, extent:], "wide", -1)
    corner = shifted(right, "narrow", -1)
    grad_own, grad_below, grad_right, grad_corner, keep, send = run_slots(
        offsets, live, object_field, below, right, right_low, corner, probe, amplitudes
    )
    came_corner = shifted(grad_corner, "narrow", 1)
    grad_right, send = together(grad_right.at[:, :extent].add(came_corner), send)
    beside = [shifted(grad_below, "narrow", 1), shifted(grad_right, "wide", 1)]
    total_slots = lax.axis_size("wide") * lax.axis_size("narrow") * offsets.shape[0]
    probe_grad, beside = sum_everywhere(keep, send, 1.0 / math.sqrt(total_slots), beside)
    came_below, came_right = beside
    object_grad = grad_own.at[:, :extent, :].add(came_below).at[:, :, :extent].add(came_right)
    return (object_grad, probe_grad.reshape(probe.shape))


def solution(mesh):
    return jax.shard_map(
        on_device,
        mesh=mesh,
        in_specs=(
            P(None, "narrow", "wide"),
            P(),
            P(("wide", "narrow"), None, None),
            P(("wide", "narrow"), None),
            P(("wide", "narrow")),
        ),
        out_specs=(P(None, "narrow", "wide"), P()),
        check_vma=False,
    )
```

```python
import functools
import math

import jax
import jax.numpy as jnp
import ml_dtypes
import numpy as np
from jax import lax
from jax.experimental import pallas as pl
from jax.experimental.pallas import tpu as pltpu
from jax.sharding import PartitionSpec as P

F32 = jnp.float32
BF16 = jnp.bfloat16
LANES = 128


def half_dft(extent):
    half = extent // 2
    blocks = []
    for parity in range(2):
        freq = 2 * np.arange(half)[:, None] + parity
        angles = (freq * np.arange(half)[None, :] % extent) * (2.0 * math.pi / extent)
        cosine = np.cos(angles) / math.sqrt(extent)
        sine = np.sin(angles) / math.sqrt(extent)
        blocks.append(np.block([[cosine, sine], [-sine, cosine]]))
    both = np.stack(blocks)
    return np.stack([both, np.swapaxes(both, 1, 2)]).astype(ml_dtypes.bfloat16)


def parity_order(extent):
    order = np.concatenate([np.arange(0, extent, 2), np.arange(1, extent, 2)])
    matrix = np.zeros((extent, extent), np.float32)
    matrix[order, np.arange(extent)] = 1.0
    return matrix


def dot(a, b):
    return jnp.dot(a, b, preferred_element_type=F32)


def slots_kernel(
    tile_rows, tile_cols, offsets, live, own, below, right, right_low, corner, probe_in, amps, mats, order,
    grad_own, grad_below, grad_right, grad_right_low, grad_corner, probe_keep, probe_send,
    ext, grad, probe, probe_sum, window, part, amp, sorted_amp, waves, inner, far, power, across,
    in_sems, amp_sem, out_sems,
):
    modes = probe.shape[0]
    extent = probe.shape[2]
    half = extent // 2
    rows_step = 32
    groups = rows_step // 8
    count = live[0]

    low_rows = slice(tile_rows, tile_rows + extent)
    whole = slice(0, tile_cols)
    rim = slice(tile_cols, tile_cols + extent)
    places = [
        (own, slice(0, tile_rows), whole),
        (below, low_rows, whole),
        (right, slice(0, extent), rim),
        (right_low, slice(extent, tile_rows), rim),
        (corner, low_rows, rim),
    ]
    loads = [
        pltpu.make_async_copy(src, ext.at[:, rows, cols], in_sems.at[n])
        for n, (src, rows, cols) in enumerate(places)
    ]
    loads.append(pltpu.make_async_copy(probe_in, probe, in_sems.at[len(places)]))
    for load in loads:
        load.start()
    grad[...] = jnp.zeros_like(grad)
    probe_sum[...] = jnp.zeros_like(probe_sum)
    for load in loads:
        load.wait()
    lane = lax.broadcasted_iota(jnp.int32, (rows_step, LANES), 1)
    lane3 = lax.broadcasted_iota(jnp.int32, (groups + 1, 8, LANES), 2)
    sublane = lax.broadcasted_iota(jnp.int32, (groups, 8, LANES), 1)
    sublane_tall = lax.broadcasted_iota(jnp.int32, (groups + 1, 8, LANES), 1)

    def rows_of(k, c, rows):
        start = (k * 2 + c) * extent
        return slice(start + rows.start, start + rows.stop)

    def visit(number, row_at, col_at):
        amp_load = pltpu.make_async_copy(amps.at[number], amp, amp_sem)
        amp_load.start()
        shift = lax.rem(col_at, LANES)
        col_base = pl.multiple_of(col_at - shift, LANES)
        back = lax.rem(LANES - shift, LANES)
        wide_cols = extent // LANES + 1
        row_shift = lax.rem(row_at, 8)
        row_base = pl.multiple_of(row_at - row_shift, 8)
        row_back = lax.rem(8 - row_shift, 8)

        for plane in range(2):
            for row in range(0, extent, rows_step):
                turned = []
                for c in range(wide_cols):
                    tall = ext[plane, pl.ds(row_base + row, rows_step + 8), pl.ds(col_base + LANES * c, LANES)]
                    tall = pltpu.roll(tall.reshape(groups + 1, 8, LANES), row_back, 1)
                    flat = jnp.where(sublane < 8 - row_shift, tall[:-1], tall[1:]).reshape(rows_step, LANES)
                    turned.append(pltpu.roll(flat, back, 1))
                for c in range(wide_cols - 1):
                    window[plane, row : row + rows_step, c * LANES : (c + 1) * LANES] = jnp.where(
                        lane < LANES - shift, turned[c], turned[c + 1]
                    )


        def psi(k, step=rows_step):
            for row in range(0, half, step):
                waves_at = []
                for base in (row, half + row):
                    rows = slice(base, base + step)
                    pr, pi = probe[k, 0, rows, :], probe[k, 1, rows, :]
                    o_re, o_im = window[0, rows, :], window[1, rows, :]
                    waves_at.append((pr * o_re - pi * o_im, pr * o_im + pi * o_re))
                for c in range(2):
                    rows = slice(c * half + row, c * half + row + step)
                    waves[k, 0, rows, :] = (waves_at[0][c] + waves_at[1][c]).astype(BF16)
                    waves[k, 1, rows, :] = (waves_at[0][c] - waves_at[1][c]).astype(BF16)

        def left(k):
            for a in range(2):
                z = dot(mats[0, a], waves[k, a])
                left, right_half = z[:, :half], z[:, half:]
                for b, value in enumerate((left + right_half, left - right_half)):
                    value = value.astype(BF16)
                    inner[k, b, a * half : (a + 1) * half, :half] = value[:half]
                    inner[k, b, a * half : (a + 1) * half, half:] = value[half:]

        def right(k):
            for b in range(2):
                f = dot(inner[k, b], mats[1, b])
                far[k, b] = f
                own_power = f[:, :half] * f[:, :half] + f[:, half:] * f[:, half:]
                power[b] = own_power if k == 0 else power[b] + own_power

        def factors():
            amp_load.wait()
            high = amp[...].astype(BF16)
            low = (amp[...] - high.astype(F32)).astype(BF16)
            turned = dot(high, order[...]) + dot(low, order[...])
            for b in range(2):
                sorted_amp[b] = turned[:, b * half : (b + 1) * half]
            for b in range(2):
                for a in range(2):
                    rows = slice(a * half, (a + 1) * half)
                    for_rows = sorted_amp[b, pl.ds(a, half, 2), :]
                    power[b, rows] = 2.0 - 2.0 * for_rows * lax.rsqrt(power[b, rows] + 0.5)

        def back_right(k):
            ys = []
            for b in range(2):
                factor = power[b]
                g = jnp.concatenate([far[k, b, :, :half] * factor, far[k, b, :, half:] * factor], 1)
                ys.append(dot(g.astype(BF16), mats[0, b]))
            for side, y in enumerate((ys[0] + ys[1], ys[0] - ys[1])):
                y = y.astype(BF16)
                cols = slice(side * half, (side + 1) * half)
                for a in range(2):
                    rows = slice(a * half, (a + 1) * half)
                    across[k, a, :half, cols] = y[rows, :half]
                    across[k, a, half:, cols] = y[rows, half:]

        def back_left(k):
            v0 = dot(mats[1, 0], across[k, 0])
            v1 = dot(mats[1, 1], across[k, 1])
            for side, v in enumerate((v0 + v1, v0 - v1)):
                rows = slice(side * half, (side + 1) * half)
                g_re, g_im = v[:half], v[half:]
                pr, pi = probe[k, 0, rows, :], probe[k, 1, rows, :]
                o_re, o_im = window[0, rows, :], window[1, rows, :]
                add_re = pr * g_re + pi * g_im
                add_im = pr * g_im - pi * g_re
                part[0, rows, :] = add_re if k == 0 else part[0, rows, :] + add_re
                part[1, rows, :] = add_im if k == 0 else part[1, rows, :] + add_im
                probe_sum[rows_of(k, 0, rows), :] += o_re * g_re + o_im * g_im
                probe_sum[rows_of(k, 1, rows), :] += o_re * g_im - o_im * g_re

        for stage in (psi, left, right):
            for k in range(modes):
                stage(k)
        factors()
        for stage in (back_right, back_left):
            for k in range(modes):
                stage(k)

        zero = jnp.zeros((groups + 1, 8, LANES), F32)
        edge = jnp.zeros((1, 8, LANES), F32)
        for plane in range(2):
            for row in range(0, extent, rows_step):
                turned = []
                for c in range(wide_cols - 1):
                    flat = part[plane, row : row + rows_step, c * LANES : (c + 1) * LANES]
                    flat = pltpu.roll(flat, shift, 1).reshape(groups, 8, LANES)
                    flat = pltpu.roll(flat, row_shift, 1)
                    low = jnp.concatenate([flat, edge], 0)
                    high = jnp.concatenate([edge, flat], 0)
                    turned.append(jnp.where(sublane_tall >= row_shift, low, high))
                turned = [zero] + turned + [zero]
                for c in range(wide_cols):
                    at = (plane, pl.ds(row_base + row, rows_step + 8), pl.ds(col_base + LANES * c, LANES))
                    value = jnp.where(lane3 >= shift, turned[c + 1], turned[c])
                    grad[at] += value.reshape(rows_step + 8, LANES)

    @pl.loop(0, count)
    def _(number):
        row_at = lax.rem(offsets[number, 0], tile_rows)
        col_at = lax.rem(offsets[number, 1], tile_cols)

        visit(number, row_at, col_at)

    own_half = (lax.axis_index("narrow") & 1) * (probe_sum.shape[0] // 2)
    other_half = probe_sum.shape[0] // 2 - own_half
    pairs = [
        (probe_sum.at[pl.ds(pl.multiple_of(start, 8), probe_sum.shape[0] // 2), :], dst)
        for start, dst in ((other_half, probe_send), (own_half, probe_keep))
    ] + [
        (grad.at[:, low_rows, rim], grad_corner),
        (grad.at[:, low_rows, whole], grad_below),
        (grad.at[:, 0:extent, rim], grad_right),
        (grad.at[:, extent:tile_rows, rim], grad_right_low),
        (grad.at[:, 0:tile_rows, whole], grad_own),
    ]
    stores = [pltpu.make_async_copy(src, dst, out_sems.at[n]) for n, (src, dst) in enumerate(pairs)]
    for store in stores:
        store.start()
    for store in stores:
        store.wait()


def run_slots(offsets, live, own, below, right, right_low, corner, probe, amps):
    extent = probe.shape[2]
    modes = probe.shape[0]
    tile_rows, tile_cols = own.shape[1:]
    mats = jnp.asarray(half_dft(extent))
    order = jnp.asarray(parity_order(extent)).astype(BF16)
    smem = pl.BlockSpec(memory_space=pltpu.SMEM)
    vmem = pl.BlockSpec(memory_space=pltpu.VMEM)
    hbm = pl.BlockSpec(memory_space=pltpu.HBM)
    anywhere = pl.BlockSpec(memory_space=pl.ANY)
    grad_shape = (2, tile_rows + extent, tile_cols + extent)
    sum_shape = (modes * 2 * extent, extent)
    half_sum = (sum_shape[0] // 2, extent)
    outs = [(2, tile_rows, tile_cols), (2, extent, tile_cols), (2, extent, extent), (2, tile_rows - extent, extent)]
    outs += [(2, extent, extent), half_sum, half_sum]
    return pl.pallas_call(
        functools.partial(slots_kernel, tile_rows, tile_cols),
        out_shape=[jax.ShapeDtypeStruct(shape, F32) for shape in outs],
        in_specs=[smem, smem, hbm] + [anywhere] * 4 + [hbm, hbm, vmem, vmem],
        out_specs=[anywhere] * len(outs),
        scratch_shapes=[
            pltpu.VMEM(grad_shape, F32),
            pltpu.VMEM(grad_shape, F32),
            pltpu.VMEM(probe.shape, F32),
            pltpu.VMEM(sum_shape, F32),
            pltpu.VMEM((2, extent, extent), F32),
            pltpu.VMEM((2, extent, extent), F32),
            pltpu.VMEM((extent, extent), F32),
            pltpu.VMEM((2, extent, extent // 2), F32),
            pltpu.VMEM((modes, 2, extent, extent), BF16),
            pltpu.VMEM((modes, 2, extent, extent), BF16),
            pltpu.VMEM((modes, 2, extent, extent), F32),
            pltpu.VMEM((2, extent, extent // 2), F32),
            pltpu.VMEM((modes, 2, extent, extent), BF16),
            pltpu.SemaphoreType.DMA((6,)),
            pltpu.SemaphoreType.DMA(()),
            pltpu.SemaphoreType.DMA((7,)),
        ],
        compiler_params=pltpu.CompilerParams(vmem_limit_bytes=44 * 1024 * 1024),
        name="slots",
    )(offsets, live, own, below, right, right_low, corner, probe, amps, mats, order)


def shifted(value, axis, steps):
    count = lax.axis_size(axis)
    first, last = (max(0, -steps), min(count, count - steps))
    return lax.ppermute(value, axis, [(source, source + steps) for source in range(first, last)])


def place_in(bits):
    linear = lax.axis_index("wide") * lax.axis_size("narrow") + lax.axis_index("narrow")
    place = 0
    for n, bit in enumerate(bits):
        place = place + ((linear // bit) % 2) * (1 << n)
    return place


def partners(bits):
    return [sum(bit for n, bit in enumerate(bits) if step >> n & 1) for step in range(1 << len(bits))]


def swapped(value, mask):
    count = lax.axis_size("wide") * lax.axis_size("narrow")
    return lax.ppermute(value, ("wide", "narrow"), [(source, source ^ mask) for source in range(count)])


def add_kernel(bits, count, *refs):
    ins, outs = refs[:count], refs[count:]
    rows = outs[0].shape[0]
    place = place_in(bits)
    for step, out in enumerate(outs):
        at = pl.ds(pl.multiple_of((place ^ step) * rows, 8), rows)
        out[...] = sum(ref[at, :] for ref in ins)


def add_parts(parts, bits):
    count = 1 << len(bits)
    rows, cols = parts[0].shape
    vmem = pl.BlockSpec(memory_space=pltpu.VMEM)
    return pl.pallas_call(
        functools.partial(add_kernel, bits, len(parts)),
        out_shape=[jax.ShapeDtypeStruct((rows // count, cols), F32)] * count,
        in_specs=[vmem] * len(parts),
        out_specs=[vmem] * count,
        compiler_params=pltpu.CompilerParams(vmem_limit_bytes=8 * 1024 * 1024),
        name="add_parts",
    )(*parts)


def join_kernel(bits, scale, *refs):
    ins, out = refs[:-1], refs[-1]
    rows = ins[0].shape[0]
    place = place_in(bits)
    for step, ref in enumerate(ins):
        at = pl.ds(pl.multiple_of((place ^ step) * rows, 8), rows)
        out[at, :] = ref[...] if scale is None else ref[...] * scale


def join_parts(parts, bits, scale=None):
    rows, cols = parts[0].shape
    vmem = pl.BlockSpec(memory_space=pltpu.VMEM)
    return pl.pallas_call(
        functools.partial(join_kernel, bits, scale),
        out_shape=jax.ShapeDtypeStruct((rows * len(parts), cols), F32),
        in_specs=[vmem] * len(parts),
        out_specs=vmem,
        compiler_params=pltpu.CompilerParams(vmem_limit_bytes=8 * 1024 * 1024),
        name="join_parts",
    )(*parts)


def together(*values):
    return lax.optimization_barrier(values)


def sum_everywhere(keep, send, scale, first, second):
    narrow, wide = lax.axis_size("narrow"), lax.axis_size("wide")
    bits = [1 << n for n in range((narrow * wide).bit_length() - 1)]
    groups = [(bits[1],)] + [tuple(bits[n : n + 2]) for n in range(2, len(bits), 2)]
    parts = [keep, swapped(send, bits[0])]
    for n, group in enumerate(groups):
        pieces = add_parts(parts, group)
        parts = [pieces[0]] + [swapped(piece, mask) for piece, mask in zip(pieces[1:], partners(group)[1:])]
        if n == 0:
            parts, first = together(parts, first)
    value = add_parts(parts, ())[0]
    for group in reversed(groups):
        if group == groups[0]:
            value, second = together(value, second)
        parts = [value] + [swapped(value, mask) for mask in partners(group)[1:]]
        if group != groups[0]:
            value = join_parts(parts, group)
    parts = parts + [swapped(part, bits[0]) for part in parts]
    return join_parts(parts, groups[0] + (bits[0],), scale), first, second


def on_device(object_field, probe, amplitudes, offsets, live):
    extent = probe.shape[2]
    top = object_field[:, :extent]
    right = shifted(top, "wide", -1)
    below = shifted(top, "narrow", -1)
    right_low = shifted(object_field[:, extent:], "wide", -1)
    corner = shifted(right, "narrow", -1)
    grad_own, grad_below, grad_right, grad_right_low, grad_corner, keep, send = run_slots(
        offsets, live, object_field, below, right, right_low, corner, probe, amplitudes
    )
    came_right_low = shifted(grad_right_low, "wide", 1)
    grad_right, send = together(grad_right + shifted(grad_corner, "narrow", 1), send)
    came_below = shifted(grad_below, "narrow", 1)
    came_right = shifted(grad_right, "wide", 1)
    total_slots = lax.axis_size("wide") * lax.axis_size("narrow") * offsets.shape[0]
    probe_grad, came_right_low, (came_right, came_below) = sum_everywhere(
        keep, send, 1.0 / math.sqrt(total_slots), came_right_low, (came_right, came_below)
    )
    rims = jnp.concatenate([came_right, came_right_low], 1)
    object_grad = grad_own.at[:, :extent, :].add(came_below).at[:, :, :extent].add(rims)
    return (object_grad, probe_grad.reshape(probe.shape))


def solution(mesh):
    return jax.shard_map(
        on_device,
        mesh=mesh,
        in_specs=(
            P(None, "narrow", "wide"),
            P(),
            P(("wide", "narrow"), None, None),
            P(("wide", "narrow"), None),
            P(("wide", "narrow")),
        ),
        out_specs=(P(None, "narrow", "wide"), P()),
        check_vma=False,
    )
```

```python
import functools
import math

import jax
import jax.numpy as jnp
import ml_dtypes
import numpy as np
from jax import lax
from jax.experimental import pallas as pl
from jax.experimental.pallas import tpu as pltpu
from jax.sharding import PartitionSpec as P

F32 = jnp.float32
BF16 = jnp.bfloat16
LANES = 128


def half_dft(extent):
    half = extent // 2
    blocks = []
    for parity in range(2):
        freq = 2 * np.arange(half)[:, None] + parity
        angles = (freq * np.arange(half)[None, :] % extent) * (2.0 * math.pi / extent)
        cosine = np.cos(angles) / math.sqrt(extent)
        sine = np.sin(angles) / math.sqrt(extent)
        blocks.append(np.block([[cosine, sine], [-sine, cosine]]))
    both = np.stack(blocks)
    return np.stack([both, np.swapaxes(both, 1, 2)]).astype(ml_dtypes.bfloat16)


def parity_order(extent):
    order = np.concatenate([np.arange(0, extent, 2), np.arange(1, extent, 2)])
    matrix = np.zeros((extent, extent), np.float32)
    matrix[order, np.arange(extent)] = 1.0
    return matrix


def dot(a, b):
    return jnp.dot(a, b, preferred_element_type=F32)


def slots_kernel(
    tile_rows, tile_cols, offsets, live, own, below, right, right_low, corner, probe_in, amps, mats, order,
    grad_own, grad_below, grad_right, grad_right_low, grad_corner, probe_keep, probe_send,
    ext, grad, probe, probe_sum, window, part, amp, sorted_amp, waves, inner, far, power, across,
    in_sems, amp_sem, out_sems,
):
    modes = probe.shape[0]
    extent = probe.shape[2]
    half = extent // 2
    rows_step = 32
    groups = rows_step // 8
    count = live[0]

    low_rows = slice(tile_rows, tile_rows + extent)
    whole = slice(0, tile_cols)
    rim = slice(tile_cols, tile_cols + extent)
    places = [
        (own, slice(0, tile_rows), whole),
        (below, low_rows, whole),
        (right, slice(0, extent), rim),
        (right_low, slice(extent, tile_rows), rim),
        (corner, low_rows, rim),
    ]
    loads = [
        pltpu.make_async_copy(src, ext.at[:, rows, cols], in_sems.at[n])
        for n, (src, rows, cols) in enumerate(places)
    ]
    loads.append(pltpu.make_async_copy(probe_in, probe, in_sems.at[len(places)]))
    for load in loads:
        load.start()
    grad[...] = jnp.zeros_like(grad)
    probe_sum[...] = jnp.zeros_like(probe_sum)
    for load in loads:
        load.wait()
    lane = lax.broadcasted_iota(jnp.int32, (rows_step, LANES), 1)
    lane3 = lax.broadcasted_iota(jnp.int32, (groups + 1, 8, LANES), 2)
    sublane = lax.broadcasted_iota(jnp.int32, (groups, 8, LANES), 1)
    sublane_tall = lax.broadcasted_iota(jnp.int32, (groups + 1, 8, LANES), 1)

    def rows_of(k, c, rows):
        start = (k * 2 + c) * extent
        return slice(start + rows.start, start + rows.stop)

    def visit(number, row_at, col_at):
        amp_load = pltpu.make_async_copy(amps.at[number], amp, amp_sem)
        amp_load.start()
        shift = lax.rem(col_at, LANES)
        col_base = pl.multiple_of(col_at - shift, LANES)
        back = lax.rem(LANES - shift, LANES)
        wide_cols = extent // LANES + 1
        row_shift = lax.rem(row_at, 8)
        row_base = pl.multiple_of(row_at - row_shift, 8)
        row_back = lax.rem(8 - row_shift, 8)

        for plane in range(2):
            for row in range(0, extent, rows_step):
                turned = []
                for c in range(wide_cols):
                    tall = ext[plane, pl.ds(row_base + row, rows_step + 8), pl.ds(col_base + LANES * c, LANES)]
                    tall = pltpu.roll(tall.reshape(groups + 1, 8, LANES), row_back, 1)
                    flat = jnp.where(sublane < 8 - row_shift, tall[:-1], tall[1:]).reshape(rows_step, LANES)
                    turned.append(pltpu.roll(flat, back, 1))
                for c in range(wide_cols - 1):
                    window[plane, row : row + rows_step, c * LANES : (c + 1) * LANES] = jnp.where(
                        lane < LANES - shift, turned[c], turned[c + 1]
                    )


        def psi(k, step=rows_step):
            for row in range(0, half, step):
                waves_at = []
                for base in (row, half + row):
                    rows = slice(base, base + step)
                    pr, pi = probe[k, 0, rows, :], probe[k, 1, rows, :]
                    o_re, o_im = window[0, rows, :], window[1, rows, :]
                    waves_at.append((pr * o_re - pi * o_im, pr * o_im + pi * o_re))
                for c in range(2):
                    rows = slice(c * half + row, c * half + row + step)
                    waves[k, 0, rows, :] = (waves_at[0][c] + waves_at[1][c]).astype(BF16)
                    waves[k, 1, rows, :] = (waves_at[0][c] - waves_at[1][c]).astype(BF16)

        def left(k):
            for a in range(2):
                z = dot(mats[0, a], waves[k, a])
                left, right_half = z[:, :half], z[:, half:]
                for b, value in enumerate((left + right_half, left - right_half)):
                    value = value.astype(BF16)
                    inner[k, b, a * half : (a + 1) * half, :half] = value[:half]
                    inner[k, b, a * half : (a + 1) * half, half:] = value[half:]

        def right(k):
            for b in range(2):
                f = dot(inner[k, b], mats[1, b])
                far[k, b] = f
                own_power = f[:, :half] * f[:, :half] + f[:, half:] * f[:, half:]
                power[b] = own_power if k == 0 else power[b] + own_power

        def factors():
            amp_load.wait()
            high = amp[...].astype(BF16)
            low = (amp[...] - high.astype(F32)).astype(BF16)
            turned = dot(high, order[...]) + dot(low, order[...])
            for b in range(2):
                sorted_amp[b] = turned[:, b * half : (b + 1) * half]
            for b in range(2):
                for a in range(2):
                    rows = slice(a * half, (a + 1) * half)
                    for_rows = sorted_amp[b, pl.ds(a, half, 2), :]
                    power[b, rows] = 2.0 - 2.0 * for_rows * lax.rsqrt(power[b, rows] + 0.5)

        def back_right(k):
            ys = []
            for b in range(2):
                factor = power[b]
                g = jnp.concatenate([far[k, b, :, :half] * factor, far[k, b, :, half:] * factor], 1)
                ys.append(dot(g.astype(BF16), mats[0, b]))
            for side, y in enumerate((ys[0] + ys[1], ys[0] - ys[1])):
                y = y.astype(BF16)
                cols = slice(side * half, (side + 1) * half)
                for a in range(2):
                    rows = slice(a * half, (a + 1) * half)
                    across[k, a, :half, cols] = y[rows, :half]
                    across[k, a, half:, cols] = y[rows, half:]

        def back_left(k):
            v0 = dot(mats[1, 0], across[k, 0])
            v1 = dot(mats[1, 1], across[k, 1])
            for side, v in enumerate((v0 + v1, v0 - v1)):
                rows = slice(side * half, (side + 1) * half)
                g_re, g_im = v[:half], v[half:]
                pr, pi = probe[k, 0, rows, :], probe[k, 1, rows, :]
                o_re, o_im = window[0, rows, :], window[1, rows, :]
                add_re = pr * g_re + pi * g_im
                add_im = pr * g_im - pi * g_re
                part[0, rows, :] = add_re if k == 0 else part[0, rows, :] + add_re
                part[1, rows, :] = add_im if k == 0 else part[1, rows, :] + add_im
                probe_sum[rows_of(k, 0, rows), :] += o_re * g_re + o_im * g_im
                probe_sum[rows_of(k, 1, rows), :] += o_re * g_im - o_im * g_re

        for stage in (psi, left, right):
            for k in range(modes):
                stage(k)
        factors()
        for stage in (back_right, back_left):
            for k in range(modes):
                stage(k)

        zero = jnp.zeros((groups + 1, 8, LANES), F32)
        edge = jnp.zeros((1, 8, LANES), F32)
        for plane in range(2):
            for row in range(0, extent, rows_step):
                turned = []
                for c in range(wide_cols - 1):
                    flat = part[plane, row : row + rows_step, c * LANES : (c + 1) * LANES]
                    flat = pltpu.roll(flat, shift, 1).reshape(groups, 8, LANES)
                    flat = pltpu.roll(flat, row_shift, 1)
                    low = jnp.concatenate([flat, edge], 0)
                    high = jnp.concatenate([edge, flat], 0)
                    turned.append(jnp.where(sublane_tall >= row_shift, low, high))
                turned = [zero] + turned + [zero]
                for c in range(wide_cols):
                    at = (plane, pl.ds(row_base + row, rows_step + 8), pl.ds(col_base + LANES * c, LANES))
                    value = jnp.where(lane3 >= shift, turned[c + 1], turned[c])
                    grad[at] += value.reshape(rows_step + 8, LANES)

    @pl.loop(0, count)
    def _(number):
        row_at = lax.rem(offsets[number, 0], tile_rows)
        col_at = lax.rem(offsets[number, 1], tile_cols)

        visit(number, row_at, col_at)

    own_half = (lax.axis_index("narrow") & 1) * (probe_sum.shape[0] // 2)
    other_half = probe_sum.shape[0] // 2 - own_half
    pairs = [
        (probe_sum.at[pl.ds(pl.multiple_of(start, 8), probe_sum.shape[0] // 2), :], dst)
        for start, dst in ((other_half, probe_send), (own_half, probe_keep))
    ] + [
        (grad.at[:, low_rows, rim], grad_corner),
        (grad.at[:, low_rows, whole], grad_below),
        (grad.at[:, 0:extent, rim], grad_right),
        (grad.at[:, extent:tile_rows, rim], grad_right_low),
        (grad.at[:, 0:tile_rows, whole], grad_own),
    ]
    stores = [pltpu.make_async_copy(src, dst, out_sems.at[n]) for n, (src, dst) in enumerate(pairs)]
    for store in stores:
        store.start()
    for store in stores:
        store.wait()


def run_slots(offsets, live, own, below, right, right_low, corner, probe, amps):
    extent = probe.shape[2]
    modes = probe.shape[0]
    tile_rows, tile_cols = own.shape[1:]
    mats = jnp.asarray(half_dft(extent))
    order = jnp.asarray(parity_order(extent)).astype(BF16)
    smem = pl.BlockSpec(memory_space=pltpu.SMEM)
    vmem = pl.BlockSpec(memory_space=pltpu.VMEM)
    hbm = pl.BlockSpec(memory_space=pltpu.HBM)
    anywhere = pl.BlockSpec(memory_space=pl.ANY)
    grad_shape = (2, tile_rows + extent, tile_cols + extent)
    sum_shape = (modes * 2 * extent, extent)
    half_sum = (sum_shape[0] // 2, extent)
    outs = [(2, tile_rows, tile_cols), (2, extent, tile_cols), (2, extent, extent), (2, tile_rows - extent, extent)]
    outs += [(2, extent, extent), half_sum, half_sum]
    return pl.pallas_call(
        functools.partial(slots_kernel, tile_rows, tile_cols),
        out_shape=[jax.ShapeDtypeStruct(shape, F32) for shape in outs],
        in_specs=[smem, smem, hbm] + [anywhere] * 4 + [hbm, hbm, vmem, vmem],
        out_specs=[anywhere] * len(outs),
        scratch_shapes=[
            pltpu.VMEM(grad_shape, F32),
            pltpu.VMEM(grad_shape, F32),
            pltpu.VMEM(probe.shape, F32),
            pltpu.VMEM(sum_shape, F32),
            pltpu.VMEM((2, extent, extent), F32),
            pltpu.VMEM((2, extent, extent), F32),
            pltpu.VMEM((extent, extent), F32),
            pltpu.VMEM((2, extent, extent // 2), F32),
            pltpu.VMEM((modes, 2, extent, extent), BF16),
            pltpu.VMEM((modes, 2, extent, extent), BF16),
            pltpu.VMEM((modes, 2, extent, extent), F32),
            pltpu.VMEM((2, extent, extent // 2), F32),
            pltpu.VMEM((modes, 2, extent, extent), BF16),
            pltpu.SemaphoreType.DMA((6,)),
            pltpu.SemaphoreType.DMA(()),
            pltpu.SemaphoreType.DMA((7,)),
        ],
        compiler_params=pltpu.CompilerParams(vmem_limit_bytes=44 * 1024 * 1024),
        name="slots",
    )(offsets, live, own, below, right, right_low, corner, probe, amps, mats, order)


def shifted(value, axis, steps):
    count = lax.axis_size(axis)
    first, last = (max(0, -steps), min(count, count - steps))
    return lax.ppermute(value, axis, [(source, source + steps) for source in range(first, last)])


def place_in(bits):
    linear = lax.axis_index("wide") * lax.axis_size("narrow") + lax.axis_index("narrow")
    place = 0
    for n, bit in enumerate(bits):
        place = place + ((linear // bit) % 2) * (1 << n)
    return place


def partners(bits):
    return [sum(bit for n, bit in enumerate(bits) if step >> n & 1) for step in range(1 << len(bits))]


def swapped(value, mask):
    count = lax.axis_size("wide") * lax.axis_size("narrow")
    return lax.ppermute(value, ("wide", "narrow"), [(source, source ^ mask) for source in range(count)])


def add_kernel(bits, count, *refs):
    ins, outs = refs[:count], refs[count:]
    rows = outs[0].shape[0]
    place = place_in(bits)
    for step, out in enumerate(outs):
        at = pl.ds(pl.multiple_of((place ^ step) * rows, 8), rows)
        out[...] = sum(ref[at, :] for ref in ins)


def add_parts(parts, bits):
    count = 1 << len(bits)
    rows, cols = parts[0].shape
    vmem = pl.BlockSpec(memory_space=pltpu.VMEM)
    return pl.pallas_call(
        functools.partial(add_kernel, bits, len(parts)),
        out_shape=[jax.ShapeDtypeStruct((rows // count, cols), F32)] * count,
        in_specs=[vmem] * len(parts),
        out_specs=[vmem] * count,
        compiler_params=pltpu.CompilerParams(vmem_limit_bytes=8 * 1024 * 1024),
        name="add_parts",
    )(*parts)


def join_kernel(bits, scale, *refs):
    ins, out = refs[:-1], refs[-1]
    rows = ins[0].shape[0]
    place = place_in(bits)
    for step, ref in enumerate(ins):
        at = pl.ds(pl.multiple_of((place ^ step) * rows, 8), rows)
        out[at, :] = ref[...] if scale is None else ref[...] * scale


def join_parts(parts, bits, scale=None):
    rows, cols = parts[0].shape
    vmem = pl.BlockSpec(memory_space=pltpu.VMEM)
    return pl.pallas_call(
        functools.partial(join_kernel, bits, scale),
        out_shape=jax.ShapeDtypeStruct((rows * len(parts), cols), F32),
        in_specs=[vmem] * len(parts),
        out_specs=vmem,
        compiler_params=pltpu.CompilerParams(vmem_limit_bytes=8 * 1024 * 1024),
        name="join_parts",
    )(*parts)


def together(*values):
    return lax.optimization_barrier(values)


def sum_everywhere(keep, send, scale, came_right, came_right_low, grad_below):
    narrow, wide = lax.axis_size("narrow"), lax.axis_size("wide")
    bits = [1 << n for n in range((narrow * wide).bit_length() - 1)]
    rest = bits[1:]
    groups = [tuple(rest[n :: (len(rest) + 1) // 2]) for n in range((len(rest) + 1) // 2)]
    parts = [keep, swapped(send, bits[0])]
    for n, group in enumerate(groups):
        pieces = add_parts(parts, group)
        if n == 1:
            pieces, grad_below = together(pieces, grad_below)
            came_below = shifted(grad_below, "narrow", 1)
        parts = [pieces[0]] + [swapped(piece, mask) for piece, mask in zip(pieces[1:], partners(group)[1:])]
        if n == 0:
            parts, came_right_low = together(parts, came_right_low)
    value = add_parts(parts, ())[0]
    for group in reversed(groups):
        if group == groups[0]:
            value, came_right, came_below = together(value, came_right, came_below)
        parts = [value] + [swapped(value, mask) for mask in partners(group)[1:]]
        if group != groups[0]:
            value = join_parts(parts, group)
    parts = parts + [swapped(part, bits[0]) for part in parts]
    return join_parts(parts, groups[0] + (bits[0],), scale), came_right, came_right_low, came_below


def on_device(object_field, probe, amplitudes, offsets, live):
    extent = probe.shape[2]
    top = object_field[:, :extent]
    right = shifted(top, "wide", -1)
    below = shifted(top, "narrow", -1)
    right_low = shifted(object_field[:, extent:], "wide", -1)
    corner = shifted(right, "narrow", -1)
    grad_own, grad_below, grad_right, grad_right_low, grad_corner, keep, send = run_slots(
        offsets, live, object_field, below, right, right_low, corner, probe, amplitudes
    )
    came_right_low = shifted(grad_right_low, "wide", 1)
    grad_right, send = together(grad_right + shifted(grad_corner, "narrow", 1), send)
    came_right = shifted(grad_right, "wide", 1)
    total_slots = lax.axis_size("wide") * lax.axis_size("narrow") * offsets.shape[0]
    probe_grad, came_right, came_right_low, came_below = sum_everywhere(
        keep, send, 1.0 / math.sqrt(total_slots), came_right, came_right_low, grad_below
    )
    rims = jnp.concatenate([came_right, came_right_low], 1)
    object_grad = grad_own.at[:, :extent, :].add(came_below).at[:, :, :extent].add(rims)
    return (object_grad, probe_grad.reshape(probe.shape))


def solution(mesh):
    return jax.shard_map(
        on_device,
        mesh=mesh,
        in_specs=(
            P(None, "narrow", "wide"),
            P(),
            P(("wide", "narrow"), None, None),
            P(("wide", "narrow"), None),
            P(("wide", "narrow")),
        ),
        out_specs=(P(None, "narrow", "wide"), P()),
        check_vma=False,
    )
```

```python
import functools
import math

import jax
import jax.numpy as jnp
import ml_dtypes
import numpy as np
from jax import lax
from jax.experimental import pallas as pl
from jax.experimental.pallas import tpu as pltpu
from jax.sharding import PartitionSpec as P

F32 = jnp.float32
BF16 = jnp.bfloat16
LANES = 128


def half_dft(extent):
    half = extent // 2
    blocks = []
    for parity in range(2):
        freq = 2 * np.arange(half)[:, None] + parity
        angles = (freq * np.arange(half)[None, :] % extent) * (2.0 * math.pi / extent)
        cosine = np.cos(angles) / math.sqrt(extent)
        sine = np.sin(angles) / math.sqrt(extent)
        blocks.append(np.block([[cosine, sine], [-sine, cosine]]))
    both = np.stack(blocks)
    return np.stack([both, np.swapaxes(both, 1, 2)]).astype(ml_dtypes.bfloat16)


def parity_order(extent):
    order = np.concatenate([np.arange(0, extent, 2), np.arange(1, extent, 2)])
    matrix = np.zeros((extent, extent), np.float32)
    matrix[order, np.arange(extent)] = 1.0
    return matrix


def dot(a, b):
    return jnp.dot(a, b, preferred_element_type=F32)


def slots_kernel(
    tile_rows, tile_cols, offsets, live, own, below, right, right_low, corner, probe_in, amps, mats, order,
    grad_own, grad_below, grad_right, grad_right_low, grad_corner, probe_keep, probe_send,
    ext, grad, probe, probe_sum, window, part, amp, sorted_amp, waves, inner, far, power, across,
    in_sems, amp_sem, out_sems,
):
    modes = probe.shape[0]
    extent = probe.shape[2]
    half = extent // 2
    rows_step = 32
    wide_cols = extent // LANES + 1
    count = live[0]

    low_rows = slice(tile_rows, tile_rows + extent)
    whole = slice(0, tile_cols)
    rim = slice(tile_cols, tile_cols + extent)
    places = [
        (own, slice(0, tile_rows), whole),
        (below, low_rows, whole),
        (right, slice(0, extent), rim),
        (right_low, slice(extent, tile_rows), rim),
        (corner, low_rows, rim),
    ]

    def strips(array, rows, cols):
        for start in range(0, cols.stop - cols.start, LANES):
            yield array.at[:, :, start : start + LANES], ((slice(None), (cols.start + start) // LANES, rows, slice(None)))

    strip_loads = [(src, at) for array, rows, cols in places for src, at in strips(array, rows, cols)]
    loads = [pltpu.make_async_copy(src, ext.at[at], in_sems.at[n]) for n, (src, at) in enumerate(strip_loads)]
    loads.append(pltpu.make_async_copy(probe_in, probe, in_sems.at[len(loads)]))
    for load in loads:
        load.start()
    grad[...] = jnp.zeros_like(grad)
    probe_sum[...] = jnp.zeros_like(probe_sum)
    for load in loads:
        load.wait()
    lane = lax.broadcasted_iota(jnp.int32, (rows_step, LANES), 1)

    def rows_of(k, c, rows):
        start = (k * 2 + c) * extent
        return slice(start + rows.start, start + rows.stop)

    def visit(number, row_at, col_at):
        amp_load = pltpu.make_async_copy(amps.at[number], amp, amp_sem)
        amp_load.start()
        shift = lax.rem(col_at, LANES)
        first_tile = col_at // LANES
        back = lax.rem(LANES - shift, LANES)

        for plane in range(2):
            for row in range(0, extent, rows_step):
                rows = pl.ds(row_at + row, rows_step)
                turned = [pltpu.roll(ext[plane, first_tile + c, rows, :], back, 1) for c in range(wide_cols)]
                for c in range(wide_cols - 1):
                    window[plane, row : row + rows_step, c * LANES : (c + 1) * LANES] = jnp.where(
                        lane < LANES - shift, turned[c], turned[c + 1]
                    )

        def psi(k, step=rows_step):
            for row in range(0, half, step):
                waves_at = []
                for base in (row, half + row):
                    rows = slice(base, base + step)
                    pr, pi = probe[k, 0, rows, :], probe[k, 1, rows, :]
                    o_re, o_im = window[0, rows, :], window[1, rows, :]
                    waves_at.append((pr * o_re - pi * o_im, pr * o_im + pi * o_re))
                for c in range(2):
                    rows = slice(c * half + row, c * half + row + step)
                    waves[k, 0, rows, :] = (waves_at[0][c] + waves_at[1][c]).astype(BF16)
                    waves[k, 1, rows, :] = (waves_at[0][c] - waves_at[1][c]).astype(BF16)

        def left(k):
            for a in range(2):
                z = dot(mats[0, a], waves[k, a])
                left, right_half = z[:, :half], z[:, half:]
                for b, value in enumerate((left + right_half, left - right_half)):
                    value = value.astype(BF16)
                    inner[k, b, a * half : (a + 1) * half, :half] = value[:half]
                    inner[k, b, a * half : (a + 1) * half, half:] = value[half:]

        def right(k):
            for b in range(2):
                f = dot(inner[k, b], mats[1, b])
                far[k, b] = f
                own_power = f[:, :half] * f[:, :half] + f[:, half:] * f[:, half:]
                power[b] = own_power if k == 0 else power[b] + own_power

        def factors():
            amp_load.wait()
            high = amp[...].astype(BF16)
            low = (amp[...] - high.astype(F32)).astype(BF16)
            turned = dot(high, order[...]) + dot(low, order[...])
            for b in range(2):
                sorted_amp[b] = turned[:, b * half : (b + 1) * half]
            for b in range(2):
                for a in range(2):
                    rows = slice(a * half, (a + 1) * half)
                    for_rows = sorted_amp[b, pl.ds(a, half, 2), :]
                    power[b, rows] = 2.0 - 2.0 * for_rows * lax.rsqrt(power[b, rows] + 0.5)

        def back_right(k):
            ys = []
            for b in range(2):
                factor = power[b]
                g = jnp.concatenate([far[k, b, :, :half] * factor, far[k, b, :, half:] * factor], 1)
                ys.append(dot(g.astype(BF16), mats[0, b]))
            for side, y in enumerate((ys[0] + ys[1], ys[0] - ys[1])):
                y = y.astype(BF16)
                cols = slice(side * half, (side + 1) * half)
                for a in range(2):
                    rows = slice(a * half, (a + 1) * half)
                    across[k, a, :half, cols] = y[rows, :half]
                    across[k, a, half:, cols] = y[rows, half:]

        def back_left(k):
            v0 = dot(mats[1, 0], across[k, 0])
            v1 = dot(mats[1, 1], across[k, 1])
            for side, v in enumerate((v0 + v1, v0 - v1)):
                rows = slice(side * half, (side + 1) * half)
                g_re, g_im = v[:half], v[half:]
                pr, pi = probe[k, 0, rows, :], probe[k, 1, rows, :]
                o_re, o_im = window[0, rows, :], window[1, rows, :]
                add_re = pr * g_re + pi * g_im
                add_im = pr * g_im - pi * g_re
                part[0, rows, :] = add_re if k == 0 else part[0, rows, :] + add_re
                part[1, rows, :] = add_im if k == 0 else part[1, rows, :] + add_im
                probe_sum[rows_of(k, 0, rows), :] += o_re * g_re + o_im * g_im
                probe_sum[rows_of(k, 1, rows), :] += o_re * g_im - o_im * g_re

        for stage in (psi, left, right):
            for k in range(modes):
                stage(k)
        factors()
        for stage in (back_right, back_left):
            for k in range(modes):
                stage(k)

        zero = jnp.zeros((rows_step, LANES), F32)
        for plane in range(2):
            for row in range(0, extent, rows_step):
                rows = pl.ds(row_at + row, rows_step)
                turned = [zero]
                for c in range(wide_cols - 1):
                    turned.append(pltpu.roll(part[plane, row : row + rows_step, c * LANES : (c + 1) * LANES], shift, 1))
                turned.append(zero)
                for c in range(wide_cols):
                    grad[plane, first_tile + c, rows, :] += jnp.where(lane >= shift, turned[c + 1], turned[c])

    @pl.loop(0, count)
    def _(number):
        row_at = lax.rem(offsets[number, 0], tile_rows)
        col_at = lax.rem(offsets[number, 1], tile_cols)

        visit(number, row_at, col_at)

    own_half = (lax.axis_index("narrow") & 1) * (probe_sum.shape[0] // 2)
    other_half = probe_sum.shape[0] // 2 - own_half
    pairs = [
        (probe_sum.at[pl.ds(pl.multiple_of(start, 8), probe_sum.shape[0] // 2), :], dst)
        for start, dst in ((other_half, probe_send), (own_half, probe_keep))
    ]
    for array, rows, cols in (
        (grad_corner, low_rows, rim),
        (grad_below, low_rows, whole),
        (grad_right, slice(0, extent), rim),
        (grad_right_low, slice(extent, tile_rows), rim),
        (grad_own, slice(0, tile_rows), whole),
    ):
        pairs += [(grad.at[at], dst) for dst, at in strips(array, rows, cols)]
    stores = [pltpu.make_async_copy(src, dst, out_sems.at[n]) for n, (src, dst) in enumerate(pairs)]
    for store in stores:
        store.start()
    for store in stores:
        store.wait()


def run_slots(offsets, live, own, below, right, right_low, corner, probe, amps):
    extent = probe.shape[2]
    modes = probe.shape[0]
    tile_rows, tile_cols = own.shape[1:]
    mats = jnp.asarray(half_dft(extent))
    order = jnp.asarray(parity_order(extent)).astype(BF16)
    smem = pl.BlockSpec(memory_space=pltpu.SMEM)
    vmem = pl.BlockSpec(memory_space=pltpu.VMEM)
    hbm = pl.BlockSpec(memory_space=pltpu.HBM)
    anywhere = pl.BlockSpec(memory_space=pl.ANY)
    tiles_shape = (2, (tile_cols + extent) // LANES, tile_rows + extent, LANES)
    sum_shape = (modes * 2 * extent, extent)
    half_sum = (sum_shape[0] // 2, extent)
    outs = [(2, tile_rows, tile_cols), (2, extent, tile_cols), (2, extent, extent), (2, tile_rows - extent, extent)]
    outs += [(2, extent, extent), half_sum, half_sum]
    return pl.pallas_call(
        functools.partial(slots_kernel, tile_rows, tile_cols),
        out_shape=[jax.ShapeDtypeStruct(shape, F32) for shape in outs],
        in_specs=[smem, smem, hbm] + [anywhere] * 4 + [hbm, hbm, vmem, vmem],
        out_specs=[anywhere] * len(outs),
        scratch_shapes=[
            pltpu.VMEM(tiles_shape, F32),
            pltpu.VMEM(tiles_shape, F32),
            pltpu.VMEM(probe.shape, F32),
            pltpu.VMEM(sum_shape, F32),
            pltpu.VMEM((2, extent, extent), F32),
            pltpu.VMEM((2, extent, extent), F32),
            pltpu.VMEM((extent, extent), F32),
            pltpu.VMEM((2, extent, extent // 2), F32),
            pltpu.VMEM((modes, 2, extent, extent), BF16),
            pltpu.VMEM((modes, 2, extent, extent), BF16),
            pltpu.VMEM((modes, 2, extent, extent), F32),
            pltpu.VMEM((2, extent, extent // 2), F32),
            pltpu.VMEM((modes, 2, extent, extent), BF16),
            pltpu.SemaphoreType.DMA((4 * tiles_shape[1],)),
            pltpu.SemaphoreType.DMA(()),
            pltpu.SemaphoreType.DMA((4 * tiles_shape[1],)),
        ],
        compiler_params=pltpu.CompilerParams(vmem_limit_bytes=44 * 1024 * 1024),
        name="slots",
    )(offsets, live, own, below, right, right_low, corner, probe, amps, mats, order)


def shifted(value, axis, steps):
    count = lax.axis_size(axis)
    first, last = (max(0, -steps), min(count, count - steps))
    return lax.ppermute(value, axis, [(source, source + steps) for source in range(first, last)])


def place_in(bits):
    linear = lax.axis_index("wide") * lax.axis_size("narrow") + lax.axis_index("narrow")
    place = 0
    for n, bit in enumerate(bits):
        place = place + ((linear // bit) % 2) * (1 << n)
    return place


def partners(bits):
    return [sum(bit for n, bit in enumerate(bits) if step >> n & 1) for step in range(1 << len(bits))]


def swapped(value, mask):
    count = lax.axis_size("wide") * lax.axis_size("narrow")
    return lax.ppermute(value, ("wide", "narrow"), [(source, source ^ mask) for source in range(count)])


def add_kernel(bits, count, *refs):
    ins, outs = refs[:count], refs[count:]
    rows = outs[0].shape[0]
    place = place_in(bits)
    for step, out in enumerate(outs):
        at = pl.ds(pl.multiple_of((place ^ step) * rows, 8), rows)
        out[...] = sum(ref[at, :] for ref in ins)


def add_parts(parts, bits):
    count = 1 << len(bits)
    rows, cols = parts[0].shape
    vmem = pl.BlockSpec(memory_space=pltpu.VMEM)
    return pl.pallas_call(
        functools.partial(add_kernel, bits, len(parts)),
        out_shape=[jax.ShapeDtypeStruct((rows // count, cols), F32)] * count,
        in_specs=[vmem] * len(parts),
        out_specs=[vmem] * count,
        compiler_params=pltpu.CompilerParams(vmem_limit_bytes=8 * 1024 * 1024),
        name="add_parts",
    )(*parts)


def join_kernel(bits, scale, *refs):
    ins, out = refs[:-1], refs[-1]
    rows = ins[0].shape[0]
    place = place_in(bits)
    for step, ref in enumerate(ins):
        at = pl.ds(pl.multiple_of((place ^ step) * rows, 8), rows)
        out[at, :] = ref[...] if scale is None else ref[...] * scale


def join_parts(parts, bits, scale=None):
    rows, cols = parts[0].shape
    vmem = pl.BlockSpec(memory_space=pltpu.VMEM)
    return pl.pallas_call(
        functools.partial(join_kernel, bits, scale),
        out_shape=jax.ShapeDtypeStruct((rows * len(parts), cols), F32),
        in_specs=[vmem] * len(parts),
        out_specs=vmem,
        compiler_params=pltpu.CompilerParams(vmem_limit_bytes=8 * 1024 * 1024),
        name="join_parts",
    )(*parts)


def together(*values):
    return lax.optimization_barrier(values)


def sum_everywhere(keep, send, scale, grad_right, came_right_low, grad_below):
    narrow, wide = lax.axis_size("narrow"), lax.axis_size("wide")
    bits = [1 << n for n in range((narrow * wide).bit_length() - 1)]
    rest = bits[1:]
    groups = [tuple(rest[n :: (len(rest) + 1) // 2]) for n in range((len(rest) + 1) // 2)]
    parts = [keep, swapped(send, bits[0])]
    for n, group in enumerate(groups):
        pieces = add_parts(parts, group)
        if n == 0:
            pieces, grad_right = together(pieces, grad_right)
            came_right = shifted(grad_right, "wide", 1)
        if n == 1:
            pieces, grad_below = together(pieces, grad_below)
            came_below = shifted(grad_below, "narrow", 1)
        parts = [pieces[0]] + [swapped(piece, mask) for piece, mask in zip(pieces[1:], partners(group)[1:])]
        if n == 0:
            parts, came_right_low = together(parts, came_right_low)
    value = add_parts(parts, ())[0]
    for group in reversed(groups):
        if group == groups[0]:
            value, came_right, came_below = together(value, came_right, came_below)
        parts = [value] + [swapped(value, mask) for mask in partners(group)[1:]]
        if group != groups[0]:
            value = join_parts(parts, group)
    parts = parts + [swapped(part, bits[0]) for part in parts]
    return join_parts(parts, groups[0] + (bits[0],), scale), came_right, came_right_low, came_below


def on_device(object_field, probe, amplitudes, offsets, live):
    extent = probe.shape[2]
    top, whole = together(object_field[:, :extent], object_field)
    right = shifted(top, "wide", -1)
    below = shifted(top, "narrow", -1)
    right_low = shifted(whole[:, extent:], "wide", -1)
    corner = shifted(right, "narrow", -1)
    grad_own, grad_below, grad_right, grad_right_low, grad_corner, keep, send = run_slots(
        offsets, live, object_field, below, right, right_low, corner, probe, amplitudes
    )
    came_right_low = shifted(grad_right_low, "wide", 1)
    grad_right = grad_right + shifted(grad_corner, "narrow", 1)
    total_slots = lax.axis_size("wide") * lax.axis_size("narrow") * offsets.shape[0]
    probe_grad, came_right, came_right_low, came_below = sum_everywhere(
        keep, send, 1.0 / math.sqrt(total_slots), grad_right, came_right_low, grad_below
    )
    rims = jnp.concatenate([came_right, came_right_low], 1)
    object_grad = grad_own.at[:, :extent, :].add(came_below).at[:, :, :extent].add(rims)
    return (object_grad, probe_grad.reshape(probe.shape))


def solution(mesh):
    return jax.shard_map(
        on_device,
        mesh=mesh,
        in_specs=(
            P(None, "narrow", "wide"),
            P(),
            P(("wide", "narrow"), None, None),
            P(("wide", "narrow"), None),
            P(("wide", "narrow")),
        ),
        out_specs=(P(None, "narrow", "wide"), P()),
        check_vma=False,
    )
```

```python
import functools
import math

import jax
import jax.numpy as jnp
import ml_dtypes
import numpy as np
from jax import lax
from jax.experimental import pallas as pl
from jax.experimental.pallas import tpu as pltpu
from jax.sharding import PartitionSpec as P

F32 = jnp.float32
BF16 = jnp.bfloat16
LANES = 128


def half_dft(extent):
    half = extent // 2
    blocks = []
    for parity in range(2):
        freq = 2 * np.arange(half)[:, None] + parity
        angles = (freq * np.arange(half)[None, :] % extent) * (2.0 * math.pi / extent)
        cosine = np.cos(angles) / math.sqrt(extent)
        sine = np.sin(angles) / math.sqrt(extent)
        blocks.append(np.block([[cosine, sine], [-sine, cosine]]))
    both = np.stack(blocks)
    return np.stack([both, np.swapaxes(both, 1, 2)]).astype(ml_dtypes.bfloat16)


def parity_order(extent):
    order = np.concatenate([np.arange(0, extent, 2), np.arange(1, extent, 2)])
    matrix = np.zeros((extent, extent), np.float32)
    matrix[order, np.arange(extent)] = 1.0
    return matrix


def dot(a, b):
    return jnp.dot(a, b, preferred_element_type=F32)


def slots_kernel(
    tile_rows, tile_cols, offsets, live, own, below, right, right_low, corner, probe_in, amps, mats, order,
    grad_own, grad_low, grad_right, grad_right_low, probe_keep, probe_send,
    ext, grad, probe, probe_sum, window, part, amp, sorted_amp, waves, inner, far, power, across,
    in_sems, amp_sem, out_sems,
):
    modes = probe.shape[0]
    extent = probe.shape[2]
    half = extent // 2
    rows_step = 32
    wide_cols = extent // LANES + 1
    count = live[0]

    low_rows = slice(tile_rows, tile_rows + extent)
    whole = slice(0, tile_cols)
    rim = slice(tile_cols, tile_cols + extent)
    places = [
        (own, slice(0, tile_rows), whole),
        (below, low_rows, whole),
        (right, slice(0, extent), rim),
        (right_low, slice(extent, tile_rows), rim),
        (corner, low_rows, rim),
    ]

    def strips(array, rows, cols):
        for start in range(0, cols.stop - cols.start, LANES):
            yield array.at[:, :, start : start + LANES], ((slice(None), (cols.start + start) // LANES, rows, slice(None)))

    strip_loads = [(src, at) for array, rows, cols in places for src, at in strips(array, rows, cols)]
    loads = [pltpu.make_async_copy(src, ext.at[at], in_sems.at[n]) for n, (src, at) in enumerate(strip_loads)]
    loads.append(pltpu.make_async_copy(probe_in, probe, in_sems.at[len(loads)]))
    for load in loads:
        load.start()
    grad[...] = jnp.zeros_like(grad)
    probe_sum[...] = jnp.zeros_like(probe_sum)
    for load in loads:
        load.wait()
    lane = lax.broadcasted_iota(jnp.int32, (rows_step, LANES), 1)

    def rows_of(k, c, rows):
        start = (k * 2 + c) * extent
        return slice(start + rows.start, start + rows.stop)

    def visit(number, row_at, col_at):
        amp_load = pltpu.make_async_copy(amps.at[number], amp, amp_sem)
        amp_load.start()
        shift = lax.rem(col_at, LANES)
        first_tile = col_at // LANES
        back = lax.rem(LANES - shift, LANES)

        for plane in range(2):
            for row in range(0, extent, rows_step):
                rows = pl.ds(row_at + row, rows_step)
                turned = [pltpu.roll(ext[plane, first_tile + c, rows, :], back, 1) for c in range(wide_cols)]
                for c in range(wide_cols - 1):
                    window[plane, row : row + rows_step, c * LANES : (c + 1) * LANES] = jnp.where(
                        lane < LANES - shift, turned[c], turned[c + 1]
                    )

        def psi(k, step=rows_step):
            for row in range(0, half, step):
                waves_at = []
                for base in (row, half + row):
                    rows = slice(base, base + step)
                    pr, pi = probe[k, 0, rows, :], probe[k, 1, rows, :]
                    o_re, o_im = window[0, rows, :], window[1, rows, :]
                    waves_at.append((pr * o_re - pi * o_im, pr * o_im + pi * o_re))
                for c in range(2):
                    rows = slice(c * half + row, c * half + row + step)
                    waves[k, 0, rows, :] = (waves_at[0][c] + waves_at[1][c]).astype(BF16)
                    waves[k, 1, rows, :] = (waves_at[0][c] - waves_at[1][c]).astype(BF16)

        def left(k):
            for a in range(2):
                z = dot(mats[0, a], waves[k, a])
                left, right_half = z[:, :half], z[:, half:]
                for b, value in enumerate((left + right_half, left - right_half)):
                    value = value.astype(BF16)
                    inner[k, b, a * half : (a + 1) * half, :half] = value[:half]
                    inner[k, b, a * half : (a + 1) * half, half:] = value[half:]

        def right(k):
            for b in range(2):
                f = dot(inner[k, b], mats[1, b])
                far[k, b] = f
                own_power = f[:, :half] * f[:, :half] + f[:, half:] * f[:, half:]
                power[b] = own_power if k == 0 else power[b] + own_power

        def factors():
            amp_load.wait()
            high = amp[...].astype(BF16)
            low = (amp[...] - high.astype(F32)).astype(BF16)
            turned = dot(high, order[...]) + dot(low, order[...])
            for b in range(2):
                sorted_amp[b] = turned[:, b * half : (b + 1) * half]
            for b in range(2):
                for a in range(2):
                    rows = slice(a * half, (a + 1) * half)
                    for_rows = sorted_amp[b, pl.ds(a, half, 2), :]
                    power[b, rows] = 2.0 - 2.0 * for_rows * lax.rsqrt(power[b, rows] + 0.5)

        def back_right(k):
            ys = []
            for b in range(2):
                factor = power[b]
                g = jnp.concatenate([far[k, b, :, :half] * factor, far[k, b, :, half:] * factor], 1)
                ys.append(dot(g.astype(BF16), mats[0, b]))
            for side, y in enumerate((ys[0] + ys[1], ys[0] - ys[1])):
                y = y.astype(BF16)
                cols = slice(side * half, (side + 1) * half)
                for a in range(2):
                    rows = slice(a * half, (a + 1) * half)
                    across[k, a, :half, cols] = y[rows, :half]
                    across[k, a, half:, cols] = y[rows, half:]

        def back_left(k):
            v0 = dot(mats[1, 0], across[k, 0])
            v1 = dot(mats[1, 1], across[k, 1])
            for side, v in enumerate((v0 + v1, v0 - v1)):
                rows = slice(side * half, (side + 1) * half)
                g_re, g_im = v[:half], v[half:]
                pr, pi = probe[k, 0, rows, :], probe[k, 1, rows, :]
                o_re, o_im = window[0, rows, :], window[1, rows, :]
                add_re = pr * g_re + pi * g_im
                add_im = pr * g_im - pi * g_re
                part[0, rows, :] = add_re if k == 0 else part[0, rows, :] + add_re
                part[1, rows, :] = add_im if k == 0 else part[1, rows, :] + add_im
                probe_sum[rows_of(k, 0, rows), :] += o_re * g_re + o_im * g_im
                probe_sum[rows_of(k, 1, rows), :] += o_re * g_im - o_im * g_re

        for stage in (psi, left, right):
            for k in range(modes):
                stage(k)
        factors()
        for stage in (back_right, back_left):
            for k in range(modes):
                stage(k)

        zero = jnp.zeros((rows_step, LANES), F32)
        for plane in range(2):
            for row in range(0, extent, rows_step):
                rows = pl.ds(row_at + row, rows_step)
                turned = [zero]
                for c in range(wide_cols - 1):
                    turned.append(pltpu.roll(part[plane, row : row + rows_step, c * LANES : (c + 1) * LANES], shift, 1))
                turned.append(zero)
                for c in range(wide_cols):
                    grad[plane, first_tile + c, rows, :] += jnp.where(lane >= shift, turned[c + 1], turned[c])

    @pl.loop(0, count)
    def _(number):
        row_at = lax.rem(offsets[number, 0], tile_rows)
        col_at = lax.rem(offsets[number, 1], tile_cols)

        visit(number, row_at, col_at)

    own_half = (lax.axis_index("narrow") & 1) * (probe_sum.shape[0] // 2)
    other_half = probe_sum.shape[0] // 2 - own_half
    pairs = [
        (probe_sum.at[pl.ds(pl.multiple_of(start, 8), probe_sum.shape[0] // 2), :], dst)
        for start, dst in ((other_half, probe_send), (own_half, probe_keep))
    ]
    for array, rows, cols in (
        (grad_low, low_rows, slice(0, tile_cols + extent)),
        (grad_right, slice(0, extent), rim),
        (grad_right_low, slice(extent, tile_rows), rim),
        (grad_own, slice(0, tile_rows), whole),
    ):
        pairs += [(grad.at[at], dst) for dst, at in strips(array, rows, cols)]
    stores = [pltpu.make_async_copy(src, dst, out_sems.at[n]) for n, (src, dst) in enumerate(pairs)]
    for store in stores:
        store.start()
    for store in stores:
        store.wait()


def run_slots(offsets, live, own, below, right, right_low, corner, probe, amps):
    extent = probe.shape[2]
    modes = probe.shape[0]
    tile_rows, tile_cols = own.shape[1:]
    mats = jnp.asarray(half_dft(extent))
    order = jnp.asarray(parity_order(extent)).astype(BF16)
    smem = pl.BlockSpec(memory_space=pltpu.SMEM)
    vmem = pl.BlockSpec(memory_space=pltpu.VMEM)
    hbm = pl.BlockSpec(memory_space=pltpu.HBM)
    anywhere = pl.BlockSpec(memory_space=pl.ANY)
    tiles_shape = (2, (tile_cols + extent) // LANES, tile_rows + extent, LANES)
    sum_shape = (modes * 2 * extent, extent)
    half_sum = (sum_shape[0] // 2, extent)
    outs = [(2, tile_rows, tile_cols), (2, extent, tile_cols + extent), (2, extent, extent)]
    outs += [(2, tile_rows - extent, extent), half_sum, half_sum]
    return pl.pallas_call(
        functools.partial(slots_kernel, tile_rows, tile_cols),
        out_shape=[jax.ShapeDtypeStruct(shape, F32) for shape in outs],
        in_specs=[smem, smem, hbm] + [anywhere] * 4 + [hbm, hbm, vmem, vmem],
        out_specs=[anywhere] * len(outs),
        scratch_shapes=[
            pltpu.VMEM(tiles_shape, F32),
            pltpu.VMEM(tiles_shape, F32),
            pltpu.VMEM(probe.shape, F32),
            pltpu.VMEM(sum_shape, F32),
            pltpu.VMEM((2, extent, extent), F32),
            pltpu.VMEM((2, extent, extent), F32),
            pltpu.VMEM((extent, extent), F32),
            pltpu.VMEM((2, extent, extent // 2), F32),
            pltpu.VMEM((modes, 2, extent, extent), BF16),
            pltpu.VMEM((modes, 2, extent, extent), BF16),
            pltpu.VMEM((modes, 2, extent, extent), F32),
            pltpu.VMEM((2, extent, extent // 2), F32),
            pltpu.VMEM((modes, 2, extent, extent), BF16),
            pltpu.SemaphoreType.DMA((4 * tiles_shape[1],)),
            pltpu.SemaphoreType.DMA(()),
            pltpu.SemaphoreType.DMA((4 * tiles_shape[1],)),
        ],
        compiler_params=pltpu.CompilerParams(vmem_limit_bytes=44 * 1024 * 1024),
        name="slots",
    )(offsets, live, own, below, right, right_low, corner, probe, amps, mats, order)


def shifted(value, axis, steps):
    count = lax.axis_size(axis)
    first, last = (max(0, -steps), min(count, count - steps))
    return lax.ppermute(value, axis, [(source, source + steps) for source in range(first, last)])


def place_in(bits):
    linear = lax.axis_index("wide") * lax.axis_size("narrow") + lax.axis_index("narrow")
    place = 0
    for n, bit in enumerate(bits):
        place = place + ((linear // bit) % 2) * (1 << n)
    return place


def partners(bits):
    return [sum(bit for n, bit in enumerate(bits) if step >> n & 1) for step in range(1 << len(bits))]


def swapped(value, mask):
    count = lax.axis_size("wide") * lax.axis_size("narrow")
    return lax.ppermute(value, ("wide", "narrow"), [(source, source ^ mask) for source in range(count)])


def add_kernel(bits, count, *refs):
    ins, outs = refs[:count], refs[count:]
    rows = outs[0].shape[0]
    place = place_in(bits)
    for step, out in enumerate(outs):
        at = pl.ds(pl.multiple_of((place ^ step) * rows, 8), rows)
        out[...] = sum(ref[at, :] for ref in ins)


def add_parts(parts, bits):
    count = 1 << len(bits)
    rows, cols = parts[0].shape
    vmem = pl.BlockSpec(memory_space=pltpu.VMEM)
    return pl.pallas_call(
        functools.partial(add_kernel, bits, len(parts)),
        out_shape=[jax.ShapeDtypeStruct((rows // count, cols), F32)] * count,
        in_specs=[vmem] * len(parts),
        out_specs=[vmem] * count,
        compiler_params=pltpu.CompilerParams(vmem_limit_bytes=8 * 1024 * 1024),
        name="add_parts",
    )(*parts)


def join_kernel(bits, scale, *refs):
    ins, out = refs[:-1], refs[-1]
    rows = ins[0].shape[0]
    place = place_in(bits)
    for step, ref in enumerate(ins):
        at = pl.ds(pl.multiple_of((place ^ step) * rows, 8), rows)
        out[at, :] = ref[...] if scale is None else ref[...] * scale


def join_parts(parts, bits, scale=None):
    rows, cols = parts[0].shape
    vmem = pl.BlockSpec(memory_space=pltpu.VMEM)
    return pl.pallas_call(
        functools.partial(join_kernel, bits, scale),
        out_shape=jax.ShapeDtypeStruct((rows * len(parts), cols), F32),
        in_specs=[vmem] * len(parts),
        out_specs=vmem,
        compiler_params=pltpu.CompilerParams(vmem_limit_bytes=8 * 1024 * 1024),
        name="join_parts",
    )(*parts)


def together(*values):
    return lax.optimization_barrier(values)


def sum_everywhere(keep, send, scale, grad_low, grad_right, came_right_low):
    narrow, wide = lax.axis_size("narrow"), lax.axis_size("wide")
    bits = [1 << n for n in range((narrow * wide).bit_length() - 1)]
    rest = bits[1:]
    groups = [tuple(rest[n :: (len(rest) + 1) // 2]) for n in range((len(rest) + 1) // 2)]
    cols = grad_low.shape[2] - grad_right.shape[2]
    parts = [keep, swapped(send, bits[0])]
    for n, group in enumerate(groups):
        pieces = add_parts(parts, group)
        if n == 1:
            pieces, grad_low = together(pieces, grad_low)
            came_low = shifted(grad_low, "narrow", 1)
        parts = [pieces[0]] + [swapped(piece, mask) for piece, mask in zip(pieces[1:], partners(group)[1:])]
        if n == 0:
            parts, came_right_low = together(parts, came_right_low)
    value = add_parts(parts, ())[0]
    for group in reversed(groups):
        if group == groups[0]:
            value, grad_right = together(value, grad_right + came_low[:, :, cols:])
            came_right = shifted(grad_right, "wide", 1)
        parts = [value] + [swapped(value, mask) for mask in partners(group)[1:]]
        if group != groups[0]:
            value = join_parts(parts, group)
    parts = parts + [swapped(part, bits[0]) for part in parts]
    return join_parts(parts, groups[0] + (bits[0],), scale), came_low[:, :, :cols], came_right, came_right_low


def on_device(object_field, probe, amplitudes, offsets, live):
    extent = probe.shape[2]
    top, whole = together(object_field[:, :extent], object_field)
    right = shifted(top, "wide", -1)
    below = shifted(top, "narrow", -1)
    right_low = shifted(whole[:, extent:], "wide", -1)
    corner = shifted(right, "narrow", -1)
    grad_own, grad_low, grad_right, grad_right_low, keep, send = run_slots(
        offsets, live, object_field, below, right, right_low, corner, probe, amplitudes
    )
    came_right_low = shifted(grad_right_low, "wide", 1)
    total_slots = lax.axis_size("wide") * lax.axis_size("narrow") * offsets.shape[0]
    probe_grad, came_below, came_right, came_right_low = sum_everywhere(
        keep, send, 1.0 / math.sqrt(total_slots), grad_low, grad_right, came_right_low
    )
    rims = jnp.concatenate([came_right, came_right_low], 1)
    object_grad = grad_own.at[:, :extent, :].add(came_below).at[:, :, :extent].add(rims)
    return (object_grad, probe_grad.reshape(probe.shape))


def solution(mesh):
    return jax.shard_map(
        on_device,
        mesh=mesh,
        in_specs=(
            P(None, "narrow", "wide"),
            P(),
            P(("wide", "narrow"), None, None),
            P(("wide", "narrow"), None),
            P(("wide", "narrow")),
        ),
        out_specs=(P(None, "narrow", "wide"), P()),
        check_vma=False,
    )
```

```python
import functools
import math

import jax
import jax.numpy as jnp
import ml_dtypes
import numpy as np
from jax import lax
from jax.experimental import pallas as pl
from jax.experimental.pallas import tpu as pltpu
from jax.sharding import PartitionSpec as P

F32 = jnp.float32
BF16 = jnp.bfloat16
LANES = 128
PAIR = 2


def half_dft(extent):
    half = extent // 2
    blocks = []
    for parity in range(2):
        freq = 2 * np.arange(half)[:, None] + parity
        angles = (freq * np.arange(half)[None, :] % extent) * (2.0 * math.pi / extent)
        cosine = np.cos(angles) / math.sqrt(extent)
        sine = np.sin(angles) / math.sqrt(extent)
        blocks.append(np.block([[cosine, sine], [-sine, cosine]]))
    both = np.stack(blocks)
    return np.stack([both, np.swapaxes(both, 1, 2)]).astype(ml_dtypes.bfloat16)


def parity_order(extent):
    order = np.concatenate([np.arange(0, extent, 2), np.arange(1, extent, 2)])
    matrix = np.zeros((extent, extent), np.float32)
    matrix[order, np.arange(extent)] = 1.0
    return matrix


def dot(a, b):
    return jnp.dot(a, b, preferred_element_type=F32)


def slots_kernel(
    tile_rows, tile_cols, offsets, live, own, below, right, right_low, corner, probe_in, amps, mats, order,
    grad_own, grad_below, grad_right, grad_right_low, grad_corner, probe_keep, probe_send,
    ext, grad, probe, probe_sum, window, part, amp, sorted_amp, waves, inner, far, power, across,
    in_sems, amp_sems, out_sems,
):
    modes = probe.shape[0]
    extent = probe.shape[2]
    half = extent // 2
    rows_step = 32
    wide_cols = extent // LANES + 1
    count = live[0]

    low_rows = slice(tile_rows, tile_rows + extent)
    whole = slice(0, tile_cols)
    rim = slice(tile_cols, tile_cols + extent)
    places = [
        (own, slice(0, tile_rows), whole),
        (below, low_rows, whole),
        (right, slice(0, extent), rim),
        (right_low, slice(extent, tile_rows), rim),
        (corner, low_rows, rim),
    ]

    def strips(array, rows, cols):
        for start in range(0, cols.stop - cols.start, LANES):
            yield array.at[:, :, start : start + LANES], ((slice(None), (cols.start + start) // LANES, rows, slice(None)))

    strip_loads = [(src, at) for array, rows, cols in places for src, at in strips(array, rows, cols)]
    loads = [pltpu.make_async_copy(src, ext.at[at], in_sems.at[n]) for n, (src, at) in enumerate(strip_loads)]
    loads.append(pltpu.make_async_copy(probe_in, probe, in_sems.at[len(loads)]))
    for load in loads:
        load.start()
    grad[...] = jnp.zeros_like(grad)
    probe_sum[...] = jnp.zeros_like(probe_sum)
    for load in loads:
        load.wait()
    lane = lax.broadcasted_iota(jnp.int32, (rows_step, LANES), 1)

    def rows_of(k, c, rows):
        start = (k * 2 + c) * extent
        return slice(start + rows.start, start + rows.stop)

    def take(q, row_at, first_tile, shift):
        back = lax.rem(LANES - shift, LANES)
        for plane in range(2):
            for row in range(0, extent, rows_step):
                rows = pl.ds(row_at + row, rows_step)
                turned = [pltpu.roll(ext[plane, first_tile + c, rows, :], back, 1) for c in range(wide_cols)]
                for c in range(wide_cols - 1):
                    window[q, plane, row : row + rows_step, c * LANES : (c + 1) * LANES] = jnp.where(
                        lane < LANES - shift, turned[c], turned[c + 1]
                    )

    def give(q, row_at, first_tile, shift):
        zero = jnp.zeros((rows_step, LANES), F32)
        for plane in range(2):
            for row in range(0, extent, rows_step):
                rows = pl.ds(row_at + row, rows_step)
                turned = [zero]
                for c in range(wide_cols - 1):
                    turned.append(pltpu.roll(part[q, plane, row : row + rows_step, c * LANES : (c + 1) * LANES], shift, 1))
                turned.append(zero)
                for c in range(wide_cols):
                    grad[plane, first_tile + c, rows, :] += jnp.where(lane >= shift, turned[c + 1], turned[c])

    def psi(k):
        for row in range(0, half, rows_step):
            spans = [slice(base, base + rows_step) for base in (row, half + row)]
            probes = [(probe[k, 0, rows, :], probe[k, 1, rows, :]) for rows in spans]
            for q in range(PAIR):
                waves_at = []
                for rows, (pr, pi) in zip(spans, probes):
                    o_re, o_im = window[q, 0, rows, :], window[q, 1, rows, :]
                    waves_at.append((pr * o_re - pi * o_im, pr * o_im + pi * o_re))
                for c in range(2):
                    rows = slice(c * half + row, c * half + row + rows_step)
                    waves[q, k, 0, rows, :] = (waves_at[0][c] + waves_at[1][c]).astype(BF16)
                    waves[q, k, 1, rows, :] = (waves_at[0][c] - waves_at[1][c]).astype(BF16)

    def left(q, k):
        for a in range(2):
            z = dot(mats[0, a], waves[q, k, a])
            left, right_half = z[:, :half], z[:, half:]
            for b, value in enumerate((left + right_half, left - right_half)):
                value = value.astype(BF16)
                inner[q, k, b, a * half : (a + 1) * half, :half] = value[:half]
                inner[q, k, b, a * half : (a + 1) * half, half:] = value[half:]

    def right(q, k):
        for b in range(2):
            f = dot(inner[q, k, b], mats[1, b])
            far[q, k, b] = f
            own_power = f[:, :half] * f[:, :half] + f[:, half:] * f[:, half:]
            power[q, b] = own_power if k == 0 else power[q, b] + own_power

    def factors(q, used):
        high = amp[q].astype(BF16)
        low = (amp[q] - high.astype(F32)).astype(BF16)
        turned = dot(high, order[...]) + dot(low, order[...])
        for b in range(2):
            sorted_amp[q, b] = turned[:, b * half : (b + 1) * half]
        for b in range(2):
            for a in range(2):
                rows = slice(a * half, (a + 1) * half)
                for_rows = sorted_amp[q, b, pl.ds(a, half, 2), :]
                factor = 2.0 - 2.0 * for_rows * lax.rsqrt(power[q, b, rows] + 0.5)
                power[q, b, rows] = factor if q == 0 else jnp.where(used, factor, 0.0)

    def back_right(q, k):
        ys = []
        for b in range(2):
            factor = power[q, b]
            g = jnp.concatenate([far[q, k, b, :, :half] * factor, far[q, k, b, :, half:] * factor], 1)
            ys.append(dot(g.astype(BF16), mats[0, b]))
        for side, y in enumerate((ys[0] + ys[1], ys[0] - ys[1])):
            y = y.astype(BF16)
            cols = slice(side * half, (side + 1) * half)
            for a in range(2):
                rows = slice(a * half, (a + 1) * half)
                across[q, k, a, :half, cols] = y[rows, :half]
                across[q, k, a, half:, cols] = y[rows, half:]

    def back_left(k):
        vs = [(dot(mats[1, 0], across[q, k, 0]), dot(mats[1, 1], across[q, k, 1])) for q in range(PAIR)]
        for side in range(2):
            rows = slice(side * half, (side + 1) * half)
            pr, pi = probe[k, 0, rows, :], probe[k, 1, rows, :]
            sum_re, sum_im = probe_sum[rows_of(k, 0, rows), :], probe_sum[rows_of(k, 1, rows), :]
            for q, (v0, v1) in enumerate(vs):
                v = v0 + v1 if side == 0 else v0 - v1
                g_re, g_im = v[:half], v[half:]
                o_re, o_im = window[q, 0, rows, :], window[q, 1, rows, :]
                add_re = pr * g_re + pi * g_im
                add_im = pr * g_im - pi * g_re
                part[q, 0, rows, :] = add_re if k == 0 else part[q, 0, rows, :] + add_re
                part[q, 1, rows, :] = add_im if k == 0 else part[q, 1, rows, :] + add_im
                sum_re = sum_re + o_re * g_re + o_im * g_im
                sum_im = sum_im + o_re * g_im - o_im * g_re
            probe_sum[rows_of(k, 0, rows), :] = sum_re
            probe_sum[rows_of(k, 1, rows), :] = sum_im

    @pl.loop(0, (count + PAIR - 1) // PAIR)
    def _(step):
        numbers = [jnp.minimum(step * PAIR + q, count - 1) for q in range(PAIR)]
        amp_loads = [pltpu.make_async_copy(amps.at[n], amp.at[q], amp_sems.at[q]) for q, n in enumerate(numbers)]
        for load in amp_loads:
            load.start()
        places = []
        for q, n in enumerate(numbers):
            col_at = lax.rem(offsets[n, 1], tile_cols)
            places.append((lax.rem(offsets[n, 0], tile_rows), col_at // LANES, lax.rem(col_at, LANES)))
            take(q, *places[q])
        every = [(q, k) for k in range(modes) for q in range(PAIR)]
        for k in range(modes):
            psi(k)
        for q, k in every:
            left(q, k)
        for q, k in every:
            right(q, k)
        for load in amp_loads:
            load.wait()
        for q in range(PAIR):
            factors(q, step * PAIR + q < count)
        for q, k in every:
            back_right(q, k)
        for k in range(modes):
            back_left(k)
        for q in range(PAIR):
            give(q, *places[q])

    own_half = (lax.axis_index("narrow") & 1) * (probe_sum.shape[0] // 2)
    other_half = probe_sum.shape[0] // 2 - own_half
    pairs = [
        (probe_sum.at[pl.ds(pl.multiple_of(start, 8), probe_sum.shape[0] // 2), :], dst)
        for start, dst in ((other_half, probe_send), (own_half, probe_keep))
    ]
    for array, rows, cols in (
        (grad_corner, low_rows, rim),
        (grad_below, low_rows, whole),
        (grad_right, slice(0, extent), rim),
        (grad_right_low, slice(extent, tile_rows), rim),
        (grad_own, slice(0, tile_rows), whole),
    ):
        pairs += [(grad.at[at], dst) for dst, at in strips(array, rows, cols)]
    stores = [pltpu.make_async_copy(src, dst, out_sems.at[n]) for n, (src, dst) in enumerate(pairs)]
    for store in stores:
        store.start()
    for store in stores:
        store.wait()


def run_slots(offsets, live, own, below, right, right_low, corner, probe, amps):
    extent = probe.shape[2]
    modes = probe.shape[0]
    tile_rows, tile_cols = own.shape[1:]
    mats = jnp.asarray(half_dft(extent))
    order = jnp.asarray(parity_order(extent)).astype(BF16)
    smem = pl.BlockSpec(memory_space=pltpu.SMEM)
    vmem = pl.BlockSpec(memory_space=pltpu.VMEM)
    hbm = pl.BlockSpec(memory_space=pltpu.HBM)
    anywhere = pl.BlockSpec(memory_space=pl.ANY)
    tiles_shape = (2, (tile_cols + extent) // LANES, tile_rows + extent, LANES)
    sum_shape = (modes * 2 * extent, extent)
    half_sum = (sum_shape[0] // 2, extent)
    outs = [(2, tile_rows, tile_cols), (2, extent, tile_cols), (2, extent, extent), (2, tile_rows - extent, extent)]
    outs += [(2, extent, extent), half_sum, half_sum]
    return pl.pallas_call(
        functools.partial(slots_kernel, tile_rows, tile_cols),
        out_shape=[jax.ShapeDtypeStruct(shape, F32) for shape in outs],
        in_specs=[smem, smem, hbm] + [anywhere] * 4 + [hbm, hbm, vmem, vmem],
        out_specs=[anywhere] * len(outs),
        scratch_shapes=[
            pltpu.VMEM(tiles_shape, F32),
            pltpu.VMEM(tiles_shape, F32),
            pltpu.VMEM(probe.shape, F32),
            pltpu.VMEM(sum_shape, F32),
            pltpu.VMEM((PAIR, 2, extent, extent), F32),
            pltpu.VMEM((PAIR, 2, extent, extent), F32),
            pltpu.VMEM((PAIR, extent, extent), F32),
            pltpu.VMEM((PAIR, 2, extent, extent // 2), F32),
            pltpu.VMEM((PAIR, modes, 2, extent, extent), BF16),
            pltpu.VMEM((PAIR, modes, 2, extent, extent), BF16),
            pltpu.VMEM((PAIR, modes, 2, extent, extent), F32),
            pltpu.VMEM((PAIR, 2, extent, extent // 2), F32),
            pltpu.VMEM((PAIR, modes, 2, extent, extent), BF16),
            pltpu.SemaphoreType.DMA((4 * tiles_shape[1],)),
            pltpu.SemaphoreType.DMA((PAIR,)),
            pltpu.SemaphoreType.DMA((4 * tiles_shape[1],)),
        ],
        compiler_params=pltpu.CompilerParams(vmem_limit_bytes=44 * 1024 * 1024),
        name="slots",
    )(offsets, live, own, below, right, right_low, corner, probe, amps, mats, order)


def shifted(value, axis, steps):
    count = lax.axis_size(axis)
    first, last = (max(0, -steps), min(count, count - steps))
    return lax.ppermute(value, axis, [(source, source + steps) for source in range(first, last)])


def place_in(bits):
    linear = lax.axis_index("wide") * lax.axis_size("narrow") + lax.axis_index("narrow")
    place = 0
    for n, bit in enumerate(bits):
        place = place + ((linear // bit) % 2) * (1 << n)
    return place


def partners(bits):
    return [sum(bit for n, bit in enumerate(bits) if step >> n & 1) for step in range(1 << len(bits))]


def swapped(value, mask):
    count = lax.axis_size("wide") * lax.axis_size("narrow")
    return lax.ppermute(value, ("wide", "narrow"), [(source, source ^ mask) for source in range(count)])


def add_kernel(bits, count, *refs):
    ins, outs = refs[:count], refs[count:]
    rows = outs[0].shape[0]
    place = place_in(bits)
    for step, out in enumerate(outs):
        at = pl.ds(pl.multiple_of((place ^ step) * rows, 8), rows)
        out[...] = sum(ref[at, :] for ref in ins)


def add_parts(parts, bits):
    count = 1 << len(bits)
    rows, cols = parts[0].shape
    vmem = pl.BlockSpec(memory_space=pltpu.VMEM)
    return pl.pallas_call(
        functools.partial(add_kernel, bits, len(parts)),
        out_shape=[jax.ShapeDtypeStruct((rows // count, cols), F32)] * count,
        in_specs=[vmem] * len(parts),
        out_specs=[vmem] * count,
        compiler_params=pltpu.CompilerParams(vmem_limit_bytes=8 * 1024 * 1024),
        name="add_parts",
    )(*parts)


def join_kernel(bits, scale, *refs):
    ins, out = refs[:-1], refs[-1]
    rows = ins[0].shape[0]
    place = place_in(bits)
    for step, ref in enumerate(ins):
        at = pl.ds(pl.multiple_of((place ^ step) * rows, 8), rows)
        out[at, :] = ref[...] if scale is None else ref[...] * scale


def join_parts(parts, bits, scale=None):
    rows, cols = parts[0].shape
    vmem = pl.BlockSpec(memory_space=pltpu.VMEM)
    return pl.pallas_call(
        functools.partial(join_kernel, bits, scale),
        out_shape=jax.ShapeDtypeStruct((rows * len(parts), cols), F32),
        in_specs=[vmem] * len(parts),
        out_specs=vmem,
        compiler_params=pltpu.CompilerParams(vmem_limit_bytes=8 * 1024 * 1024),
        name="join_parts",
    )(*parts)


def together(*values):
    return lax.optimization_barrier(values)


def sum_everywhere(keep, send, scale, grad_right, came_right_low, grad_below):
    narrow, wide = lax.axis_size("narrow"), lax.axis_size("wide")
    bits = [1 << n for n in range((narrow * wide).bit_length() - 1)]
    rest = bits[1:]
    groups = [tuple(rest[n :: (len(rest) + 1) // 2]) for n in range((len(rest) + 1) // 2)]
    parts = [keep, swapped(send, bits[0])]
    for n, group in enumerate(groups):
        pieces = add_parts(parts, group)
        if n == 0:
            pieces, grad_right = together(pieces, grad_right)
            came_right = shifted(grad_right, "wide", 1)
        if n == 1:
            pieces, grad_below = together(pieces, grad_below)
            came_below = shifted(grad_below, "narrow", 1)
        parts = [pieces[0]] + [swapped(piece, mask) for piece, mask in zip(pieces[1:], partners(group)[1:])]
        if n == 0:
            parts, came_right_low = together(parts, came_right_low)
    value = add_parts(parts, ())[0]
    for group in reversed(groups):
        if group == groups[0]:
            value, came_right, came_below = together(value, came_right, came_below)
        parts = [value] + [swapped(value, mask) for mask in partners(group)[1:]]
        if group != groups[0]:
            value = join_parts(parts, group)
    parts = parts + [swapped(part, bits[0]) for part in parts]
    return join_parts(parts, groups[0] + (bits[0],), scale), came_right, came_right_low, came_below


def on_device(object_field, probe, amplitudes, offsets, live):
    extent = probe.shape[2]
    top, whole = together(object_field[:, :extent], object_field)
    right = shifted(top, "wide", -1)
    below = shifted(top, "narrow", -1)
    right_low = shifted(whole[:, extent:], "wide", -1)
    corner = shifted(right, "narrow", -1)
    grad_own, grad_below, grad_right, grad_right_low, grad_corner, keep, send = run_slots(
        offsets, live, object_field, below, right, right_low, corner, probe, amplitudes
    )
    came_right_low = shifted(grad_right_low, "wide", 1)
    grad_right = grad_right + shifted(grad_corner, "narrow", 1)
    total_slots = lax.axis_size("wide") * lax.axis_size("narrow") * offsets.shape[0]
    probe_grad, came_right, came_right_low, came_below = sum_everywhere(
        keep, send, 1.0 / math.sqrt(total_slots), grad_right, came_right_low, grad_below
    )
    rims = jnp.concatenate([came_right, came_right_low], 1)
    object_grad = grad_own.at[:, :extent, :].add(came_below).at[:, :, :extent].add(rims)
    return (object_grad, probe_grad.reshape(probe.shape))


def solution(mesh):
    return jax.shard_map(
        on_device,
        mesh=mesh,
        in_specs=(
            P(None, "narrow", "wide"),
            P(),
            P(("wide", "narrow"), None, None),
            P(("wide", "narrow"), None),
            P(("wide", "narrow")),
        ),
        out_specs=(P(None, "narrow", "wide"), P()),
        check_vma=False,
    )
```

```python
import functools
import math

import jax
import jax.numpy as jnp
import ml_dtypes
import numpy as np
from jax import lax
from jax.experimental import pallas as pl
from jax.experimental.pallas import tpu as pltpu
from jax.sharding import PartitionSpec as P

F32 = jnp.float32
BF16 = jnp.bfloat16
LANES = 128
PAIR = 2


def half_dft(extent):
    half = extent // 2
    blocks = []
    for parity in range(2):
        freq = 2 * np.arange(half)[:, None] + parity
        angles = (freq * np.arange(half)[None, :] % extent) * (2.0 * math.pi / extent)
        cosine = np.cos(angles) / math.sqrt(extent)
        sine = np.sin(angles) / math.sqrt(extent)
        blocks.append(np.block([[cosine, sine], [-sine, cosine]]))
    both = np.stack(blocks)
    return np.stack([both, np.swapaxes(both, 1, 2)]).astype(ml_dtypes.bfloat16)


def parity_order(extent):
    order = np.concatenate([np.arange(0, extent, 2), np.arange(1, extent, 2)])
    matrix = np.zeros((extent, extent), np.float32)
    matrix[order, np.arange(extent)] = 1.0
    return matrix


def dot(a, b):
    return jnp.dot(a, b, preferred_element_type=F32)


def slots_kernel(
    tile_rows, tile_cols, offsets, live, own, below, right, right_low, corner, probe_in, amps, mats, order,
    grad_own, grad_below, grad_right, grad_right_low, grad_corner, probe_keep, probe_send,
    ext, grad, probe, probe_sum, window, part, amp, sorted_amp, waves, inner, far, power, across,
    in_sems, amp_sems, out_sems,
):
    modes = probe.shape[0]
    extent = probe.shape[2]
    half = extent // 2
    rows_step = 32
    wide_cols = extent // LANES + 1
    count = live[0]

    low_rows = slice(tile_rows, tile_rows + extent)
    whole = slice(0, tile_cols)
    rim = slice(tile_cols, tile_cols + extent)
    places = [
        (own, slice(0, tile_rows), whole),
        (below, low_rows, whole),
        (right, slice(0, extent), rim),
        (right_low, slice(extent, tile_rows), rim),
        (corner, low_rows, rim),
    ]

    def strips(array, rows, cols):
        for start in range(0, cols.stop - cols.start, LANES):
            yield array.at[:, :, start : start + LANES], ((slice(None), (cols.start + start) // LANES, rows, slice(None)))

    strip_loads = [(src, at) for array, rows, cols in places for src, at in strips(array, rows, cols)]
    loads = [pltpu.make_async_copy(src, ext.at[at], in_sems.at[n]) for n, (src, at) in enumerate(strip_loads)]
    loads.append(pltpu.make_async_copy(probe_in, probe, in_sems.at[len(loads)]))
    for load in loads:
        load.start()
    grad[...] = jnp.zeros_like(grad)
    probe_sum[...] = jnp.zeros_like(probe_sum)
    for load in loads:
        load.wait()
    lane = lax.broadcasted_iota(jnp.int32, (rows_step, LANES), 1)

    def rows_of(k, c, rows):
        start = (k * 2 + c) * extent
        return slice(start + rows.start, start + rows.stop)

    def take(q, row_at, first_tile, shift):
        back = lax.rem(LANES - shift, LANES)
        for plane in range(2):
            for row in range(0, extent, rows_step):
                rows = pl.ds(row_at + row, rows_step)
                turned = [pltpu.roll(ext[plane, first_tile + c, rows, :], back, 1) for c in range(wide_cols)]
                for c in range(wide_cols - 1):
                    window[q, plane, row : row + rows_step, c * LANES : (c + 1) * LANES] = jnp.where(
                        lane < LANES - shift, turned[c], turned[c + 1]
                    )

    def give(q, row_at, first_tile, shift):
        zero = jnp.zeros((rows_step, LANES), F32)
        for plane in range(2):
            for row in range(0, extent, rows_step):
                rows = pl.ds(row_at + row, rows_step)
                turned = [zero]
                for c in range(wide_cols - 1):
                    turned.append(pltpu.roll(part[q, plane, row : row + rows_step, c * LANES : (c + 1) * LANES], shift, 1))
                turned.append(zero)
                for c in range(wide_cols):
                    grad[plane, first_tile + c, rows, :] += jnp.where(lane >= shift, turned[c + 1], turned[c])

    def psi(k):
        for row in range(0, half, rows_step):
            spans = [slice(base, base + rows_step) for base in (row, half + row)]
            probes = [(probe[k, 0, rows, :], probe[k, 1, rows, :]) for rows in spans]
            for q in range(PAIR):
                waves_at = []
                for rows, (pr, pi) in zip(spans, probes):
                    o_re, o_im = window[q, 0, rows, :], window[q, 1, rows, :]
                    waves_at.append((pr * o_re - pi * o_im, pr * o_im + pi * o_re))
                for c in range(2):
                    rows = slice(c * half + row, c * half + row + rows_step)
                    waves[q, k, 0, rows, :] = (waves_at[0][c] + waves_at[1][c]).astype(BF16)
                    waves[q, k, 1, rows, :] = (waves_at[0][c] - waves_at[1][c]).astype(BF16)

    def left(q, k):
        for a in range(2):
            z = dot(mats[0, a], waves[q, k, a])
            left, right_half = z[:, :half], z[:, half:]
            for b, value in enumerate((left + right_half, left - right_half)):
                value = value.astype(BF16)
                inner[q, k, b, a * half : (a + 1) * half, :half] = value[:half]
                inner[q, k, b, a * half : (a + 1) * half, half:] = value[half:]

    def right(q, k):
        for b in range(2):
            f = dot(inner[q, k, b], mats[1, b])
            far[q, k, b] = f
            own_power = f[:, :half] * f[:, :half] + f[:, half:] * f[:, half:]
            power[q, b] = own_power if k == 0 else power[q, b] + own_power

    def factors(q, used):
        high = amp[q].astype(BF16)
        low = (amp[q] - high.astype(F32)).astype(BF16)
        turned = dot(high, order[...]) + dot(low, order[...])
        for b in range(2):
            sorted_amp[q, b] = turned[:, b * half : (b + 1) * half]
        for b in range(2):
            for a in range(2):
                rows = slice(a * half, (a + 1) * half)
                for_rows = sorted_amp[q, b, pl.ds(a, half, 2), :]
                factor = 2.0 - 2.0 * for_rows * lax.rsqrt(power[q, b, rows] + 0.5)
                power[q, b, rows] = factor if q == 0 else jnp.where(used, factor, 0.0)

    def back_right(q, k):
        ys = []
        for b in range(2):
            factor = power[q, b]
            g = jnp.concatenate([far[q, k, b, :, :half] * factor, far[q, k, b, :, half:] * factor], 1)
            ys.append(dot(g.astype(BF16), mats[0, b]))
        for side, y in enumerate((ys[0] + ys[1], ys[0] - ys[1])):
            y = y.astype(BF16)
            cols = slice(side * half, (side + 1) * half)
            for a in range(2):
                rows = slice(a * half, (a + 1) * half)
                across[q, k, a, :half, cols] = y[rows, :half]
                across[q, k, a, half:, cols] = y[rows, half:]

    def back_left(k):
        vs = [(dot(mats[1, 0], across[q, k, 0]), dot(mats[1, 1], across[q, k, 1])) for q in range(PAIR)]
        for side in range(2):
            rows = slice(side * half, (side + 1) * half)
            pr, pi = probe[k, 0, rows, :], probe[k, 1, rows, :]
            sum_re, sum_im = probe_sum[rows_of(k, 0, rows), :], probe_sum[rows_of(k, 1, rows), :]
            for q, (v0, v1) in enumerate(vs):
                v = v0 + v1 if side == 0 else v0 - v1
                g_re, g_im = v[:half], v[half:]
                o_re, o_im = window[q, 0, rows, :], window[q, 1, rows, :]
                add_re = pr * g_re + pi * g_im
                add_im = pr * g_im - pi * g_re
                part[q, 0, rows, :] = add_re if k == 0 else part[q, 0, rows, :] + add_re
                part[q, 1, rows, :] = add_im if k == 0 else part[q, 1, rows, :] + add_im
                sum_re = sum_re + o_re * g_re + o_im * g_im
                sum_im = sum_im + o_re * g_im - o_im * g_re
            probe_sum[rows_of(k, 0, rows), :] = sum_re
            probe_sum[rows_of(k, 1, rows), :] = sum_im

    @pl.loop(0, (count + PAIR - 1) // PAIR)
    def _(step):
        numbers = [jnp.minimum(step * PAIR + q, count - 1) for q in range(PAIR)]
        amp_loads = [pltpu.make_async_copy(amps.at[n], amp.at[q], amp_sems.at[q]) for q, n in enumerate(numbers)]
        for load in amp_loads:
            load.start()
        places = []
        for q, n in enumerate(numbers):
            col_at = lax.rem(offsets[n, 1], tile_cols)
            places.append((lax.rem(offsets[n, 0], tile_rows), col_at // LANES, lax.rem(col_at, LANES)))
            take(q, *places[q])
        every = [(q, k) for k in range(modes) for q in range(PAIR)]
        for k in range(modes):
            psi(k)
        for q, k in every:
            left(q, k)
        for q, k in every:
            right(q, k)
        for load in amp_loads:
            load.wait()
        for q in range(PAIR):
            factors(q, step * PAIR + q < count)
        for q, k in every:
            back_right(q, k)
        for k in range(modes):
            back_left(k)
        for q in range(PAIR):
            give(q, *places[q])

    own_half = (lax.axis_index("narrow") & 1) * (probe_sum.shape[0] // 2)
    other_half = probe_sum.shape[0] // 2 - own_half
    pairs = [
        (probe_sum.at[pl.ds(pl.multiple_of(start, 8), probe_sum.shape[0] // 2), :], dst)
        for start, dst in ((other_half, probe_send), (own_half, probe_keep))
    ]
    for array, rows, cols in (
        (grad_corner, low_rows, rim),
        (grad_below, low_rows, whole),
        (grad_right, slice(0, extent), rim),
        (grad_right_low, slice(extent, tile_rows), rim),
        (grad_own, slice(0, tile_rows), whole),
    ):
        pairs += [(grad.at[at], dst) for dst, at in strips(array, rows, cols)]
    stores = [pltpu.make_async_copy(src, dst, out_sems.at[n]) for n, (src, dst) in enumerate(pairs)]
    for store in stores:
        store.start()
    for store in stores:
        store.wait()


def run_slots(offsets, live, own, below, right, right_low, corner, probe, amps):
    extent = probe.shape[2]
    modes = probe.shape[0]
    tile_rows, tile_cols = own.shape[1:]
    mats = jnp.asarray(half_dft(extent))
    order = jnp.asarray(parity_order(extent)).astype(BF16)
    smem = pl.BlockSpec(memory_space=pltpu.SMEM)
    vmem = pl.BlockSpec(memory_space=pltpu.VMEM)
    hbm = pl.BlockSpec(memory_space=pltpu.HBM)
    anywhere = pl.BlockSpec(memory_space=pl.ANY)
    tiles_shape = (2, (tile_cols + extent) // LANES, tile_rows + extent, LANES)
    sum_shape = (modes * 2 * extent, extent)
    half_sum = (sum_shape[0] // 2, extent)
    outs = [(2, tile_rows, tile_cols), (2, extent, tile_cols), (2, extent, extent), (2, tile_rows - extent, extent)]
    outs += [(2, extent, extent), half_sum, half_sum]
    return pl.pallas_call(
        functools.partial(slots_kernel, tile_rows, tile_cols),
        out_shape=[jax.ShapeDtypeStruct(shape, F32) for shape in outs],
        in_specs=[smem, smem, hbm] + [anywhere] * 4 + [hbm, hbm, vmem, vmem],
        out_specs=[anywhere] * len(outs),
        scratch_shapes=[
            pltpu.VMEM(tiles_shape, F32),
            pltpu.VMEM(tiles_shape, F32),
            pltpu.VMEM(probe.shape, F32),
            pltpu.VMEM(sum_shape, F32),
            pltpu.VMEM((PAIR, 2, extent, extent), F32),
            pltpu.VMEM((PAIR, 2, extent, extent), F32),
            pltpu.VMEM((PAIR, extent, extent), F32),
            pltpu.VMEM((PAIR, 2, extent, extent // 2), F32),
            pltpu.VMEM((PAIR, modes, 2, extent, extent), BF16),
            pltpu.VMEM((PAIR, modes, 2, extent, extent), BF16),
            pltpu.VMEM((PAIR, modes, 2, extent, extent), F32),
            pltpu.VMEM((PAIR, 2, extent, extent // 2), F32),
            pltpu.VMEM((PAIR, modes, 2, extent, extent), BF16),
            pltpu.SemaphoreType.DMA((4 * tiles_shape[1],)),
            pltpu.SemaphoreType.DMA((PAIR,)),
            pltpu.SemaphoreType.DMA((4 * tiles_shape[1],)),
        ],
        compiler_params=pltpu.CompilerParams(vmem_limit_bytes=44 * 1024 * 1024),
        name="slots",
    )(offsets, live, own, below, right, right_low, corner, probe, amps, mats, order)


def shifted(value, axis, steps):
    count = lax.axis_size(axis)
    first, last = (max(0, -steps), min(count, count - steps))
    return lax.ppermute(value, axis, [(source, source + steps) for source in range(first, last)])


def aslant(value):
    narrow, wide = lax.axis_size("narrow"), lax.axis_size("wide")
    pairs = [(w * narrow + n, (w + 1) * narrow + n + 1) for w in range(wide - 1) for n in range(narrow - 1)]
    return lax.ppermute(value, ("wide", "narrow"), pairs)


def place_in(bits):
    linear = lax.axis_index("wide") * lax.axis_size("narrow") + lax.axis_index("narrow")
    place = 0
    for n, bit in enumerate(bits):
        place = place + ((linear // bit) % 2) * (1 << n)
    return place


def partners(bits):
    return [sum(bit for n, bit in enumerate(bits) if step >> n & 1) for step in range(1 << len(bits))]


def swapped(value, mask):
    count = lax.axis_size("wide") * lax.axis_size("narrow")
    return lax.ppermute(value, ("wide", "narrow"), [(source, source ^ mask) for source in range(count)])


def add_kernel(bits, count, *refs):
    ins, outs = refs[:count], refs[count:]
    rows = outs[0].shape[0]
    place = place_in(bits)
    for step, out in enumerate(outs):
        at = pl.ds(pl.multiple_of((place ^ step) * rows, 8), rows)
        out[...] = sum(ref[at, :] for ref in ins)


def add_parts(parts, bits):
    count = 1 << len(bits)
    rows, cols = parts[0].shape
    vmem = pl.BlockSpec(memory_space=pltpu.VMEM)
    return pl.pallas_call(
        functools.partial(add_kernel, bits, len(parts)),
        out_shape=[jax.ShapeDtypeStruct((rows // count, cols), F32)] * count,
        in_specs=[vmem] * len(parts),
        out_specs=[vmem] * count,
        compiler_params=pltpu.CompilerParams(vmem_limit_bytes=8 * 1024 * 1024),
        name="add_parts",
    )(*parts)


def join_kernel(bits, scale, *refs):
    ins, out = refs[:-1], refs[-1]
    rows = ins[0].shape[0]
    place = place_in(bits)
    for step, ref in enumerate(ins):
        at = pl.ds(pl.multiple_of((place ^ step) * rows, 8), rows)
        out[at, :] = ref[...] if scale is None else ref[...] * scale


def join_parts(parts, bits, scale=None):
    rows, cols = parts[0].shape
    vmem = pl.BlockSpec(memory_space=pltpu.VMEM)
    return pl.pallas_call(
        functools.partial(join_kernel, bits, scale),
        out_shape=jax.ShapeDtypeStruct((rows * len(parts), cols), F32),
        in_specs=[vmem] * len(parts),
        out_specs=vmem,
        compiler_params=pltpu.CompilerParams(vmem_limit_bytes=8 * 1024 * 1024),
        name="join_parts",
    )(*parts)


def together(*values):
    return lax.optimization_barrier(values)


def sum_everywhere(keep, send, scale, grad_right, came_right_low, grad_corner, grad_below):
    narrow, wide = lax.axis_size("narrow"), lax.axis_size("wide")
    bits = [1 << n for n in range((narrow * wide).bit_length() - 1)]
    rest = bits[1:]
    groups = [tuple(rest[n :: (len(rest) + 1) // 2]) for n in range((len(rest) + 1) // 2)]
    parts = [keep, swapped(send, bits[0])]
    for n, group in enumerate(groups):
        pieces = add_parts(parts, group)
        if n == 0:
            pieces, grad_right, grad_corner = together(pieces, grad_right, grad_corner)
            came_right = shifted(grad_right, "wide", 1)
            came_corner = aslant(grad_corner)
        if n == 1:
            pieces, grad_below = together(pieces, grad_below)
            came_below = shifted(grad_below, "narrow", 1)
        parts = [pieces[0]] + [swapped(piece, mask) for piece, mask in zip(pieces[1:], partners(group)[1:])]
        if n == 0:
            parts, came_right_low = together(parts, came_right_low)
    value = add_parts(parts, ())[0]
    for group in reversed(groups):
        if group == groups[0]:
            value, came_right, came_corner, came_below = together(value, came_right, came_corner, came_below)
        parts = [value] + [swapped(value, mask) for mask in partners(group)[1:]]
        if group != groups[0]:
            value = join_parts(parts, group)
    parts = parts + [swapped(part, bits[0]) for part in parts]
    return join_parts(parts, groups[0] + (bits[0],), scale), came_right, came_right_low, came_corner, came_below


def on_device(object_field, probe, amplitudes, offsets, live):
    extent = probe.shape[2]
    top, whole = together(object_field[:, :extent], object_field)
    right = shifted(top, "wide", -1)
    below = shifted(top, "narrow", -1)
    right_low = shifted(whole[:, extent:], "wide", -1)
    corner = shifted(right, "narrow", -1)
    grad_own, grad_below, grad_right, grad_right_low, grad_corner, keep, send = run_slots(
        offsets, live, object_field, below, right, right_low, corner, probe, amplitudes
    )
    came_right_low = shifted(grad_right_low, "wide", 1)
    total_slots = lax.axis_size("wide") * lax.axis_size("narrow") * offsets.shape[0]
    probe_grad, came_right, came_right_low, came_corner, came_below = sum_everywhere(
        keep, send, 1.0 / math.sqrt(total_slots), grad_right, came_right_low, grad_corner, grad_below
    )
    rims = jnp.concatenate([came_right + came_corner, came_right_low], 1)
    object_grad = grad_own.at[:, :extent, :].add(came_below).at[:, :, :extent].add(rims)
    return (object_grad, probe_grad.reshape(probe.shape))


def solution(mesh):
    return jax.shard_map(
        on_device,
        mesh=mesh,
        in_specs=(
            P(None, "narrow", "wide"),
            P(),
            P(("wide", "narrow"), None, None),
            P(("wide", "narrow"), None),
            P(("wide", "narrow")),
        ),
        out_specs=(P(None, "narrow", "wide"), P()),
        check_vma=False,
    )
```

```python
import functools
import math

import jax
import jax.numpy as jnp
import ml_dtypes
import numpy as np
from jax import lax
from jax.experimental import pallas as pl
from jax.experimental.pallas import tpu as pltpu
from jax.sharding import PartitionSpec as P

F32 = jnp.float32
BF16 = jnp.bfloat16
LANES = 128
PAIR = 2


def half_dft(extent):
    half = extent // 2
    blocks = []
    for parity in range(2):
        freq = 2 * np.arange(half)[:, None] + parity
        angles = (freq * np.arange(half)[None, :] % extent) * (2.0 * math.pi / extent)
        cosine = np.cos(angles) / math.sqrt(extent)
        sine = np.sin(angles) / math.sqrt(extent)
        blocks.append(np.block([[cosine, sine], [-sine, cosine]]))
    both = np.stack(blocks)
    return np.stack([both, np.swapaxes(both, 1, 2)]).astype(ml_dtypes.bfloat16)


def parity_order(extent):
    order = np.concatenate([np.arange(0, extent, 2), np.arange(1, extent, 2)])
    matrix = np.zeros((extent, extent), np.float32)
    matrix[order, np.arange(extent)] = 1.0
    return matrix


def dot(a, b):
    return jnp.dot(a, b, preferred_element_type=F32)


def slots_kernel(
    tile_rows, tile_cols, offsets, live, own, below, right, right_low, corner, probe_in, amps, mats, order,
    grad_own, grad_low, grad_right, grad_right_low, probe_keep, probe_send,
    ext, grad, probe, probe_sum, window, part, amp, sorted_amp, waves, inner, far, power, across,
    in_sems, amp_sems, out_sems,
):
    modes = probe.shape[0]
    extent = probe.shape[2]
    half = extent // 2
    rows_step = 32
    wide_cols = extent // LANES + 1
    count = live[0]

    low_rows = slice(tile_rows, tile_rows + extent)
    whole = slice(0, tile_cols)
    rim = slice(tile_cols, tile_cols + extent)
    places = [
        (own, slice(0, tile_rows), whole),
        (below, low_rows, whole),
        (right, slice(0, extent), rim),
        (right_low, slice(extent, tile_rows), rim),
        (corner, low_rows, rim),
    ]

    def strips(array, rows, cols):
        for start in range(0, cols.stop - cols.start, LANES):
            yield array.at[:, :, start : start + LANES], ((slice(None), (cols.start + start) // LANES, rows, slice(None)))

    strip_loads = [(src, at) for array, rows, cols in places for src, at in strips(array, rows, cols)]
    loads = [pltpu.make_async_copy(src, ext.at[at], in_sems.at[n]) for n, (src, at) in enumerate(strip_loads)]
    loads.append(pltpu.make_async_copy(probe_in, probe, in_sems.at[len(loads)]))
    for load in loads:
        load.start()
    grad[...] = jnp.zeros_like(grad)
    probe_sum[...] = jnp.zeros_like(probe_sum)
    for load in loads:
        load.wait()
    lane = lax.broadcasted_iota(jnp.int32, (rows_step, LANES), 1)

    def rows_of(k, c, rows):
        start = (k * 2 + c) * extent
        return slice(start + rows.start, start + rows.stop)

    def take(q, row_at, first_tile, shift):
        back = lax.rem(LANES - shift, LANES)
        for plane in range(2):
            for row in range(0, extent, rows_step):
                rows = pl.ds(row_at + row, rows_step)
                turned = [pltpu.roll(ext[plane, first_tile + c, rows, :], back, 1) for c in range(wide_cols)]
                for c in range(wide_cols - 1):
                    window[q, plane, row : row + rows_step, c * LANES : (c + 1) * LANES] = jnp.where(
                        lane < LANES - shift, turned[c], turned[c + 1]
                    )

    def give(q, row_at, first_tile, shift):
        zero = jnp.zeros((rows_step, LANES), F32)
        for plane in range(2):
            for row in range(0, extent, rows_step):
                rows = pl.ds(row_at + row, rows_step)
                turned = [zero]
                for c in range(wide_cols - 1):
                    turned.append(pltpu.roll(part[q, plane, row : row + rows_step, c * LANES : (c + 1) * LANES], shift, 1))
                turned.append(zero)
                for c in range(wide_cols):
                    grad[plane, first_tile + c, rows, :] += jnp.where(lane >= shift, turned[c + 1], turned[c])

    def psi(k):
        for row in range(0, half, rows_step):
            spans = [slice(base, base + rows_step) for base in (row, half + row)]
            probes = [(probe[k, 0, rows, :], probe[k, 1, rows, :]) for rows in spans]
            for q in range(PAIR):
                waves_at = []
                for rows, (pr, pi) in zip(spans, probes):
                    o_re, o_im = window[q, 0, rows, :], window[q, 1, rows, :]
                    waves_at.append((pr * o_re - pi * o_im, pr * o_im + pi * o_re))
                for c in range(2):
                    rows = slice(c * half + row, c * half + row + rows_step)
                    waves[q, k, 0, rows, :] = (waves_at[0][c] + waves_at[1][c]).astype(BF16)
                    waves[q, k, 1, rows, :] = (waves_at[0][c] - waves_at[1][c]).astype(BF16)

    def left(q, k):
        for a in range(2):
            z = dot(mats[0, a], waves[q, k, a])
            left, right_half = z[:, :half], z[:, half:]
            for b, value in enumerate((left + right_half, left - right_half)):
                value = value.astype(BF16)
                inner[q, k, b, a * half : (a + 1) * half, :half] = value[:half]
                inner[q, k, b, a * half : (a + 1) * half, half:] = value[half:]

    def right(q, k):
        for b in range(2):
            f = dot(inner[q, k, b], mats[1, b])
            far[q, k, b] = f
            own_power = f[:, :half] * f[:, :half] + f[:, half:] * f[:, half:]
            power[q, b] = own_power if k == 0 else power[q, b] + own_power

    def factors(q, used):
        high = amp[q].astype(BF16)
        low = (amp[q] - high.astype(F32)).astype(BF16)
        turned = dot(high, order[...]) + dot(low, order[...])
        for b in range(2):
            sorted_amp[q, b] = turned[:, b * half : (b + 1) * half]
        for b in range(2):
            for a in range(2):
                rows = slice(a * half, (a + 1) * half)
                for_rows = sorted_amp[q, b, pl.ds(a, half, 2), :]
                factor = 2.0 - 2.0 * for_rows * lax.rsqrt(power[q, b, rows] + 0.5)
                power[q, b, rows] = factor if q == 0 else jnp.where(used, factor, 0.0)

    def back_right(q, k):
        ys = []
        for b in range(2):
            factor = power[q, b]
            g = jnp.concatenate([far[q, k, b, :, :half] * factor, far[q, k, b, :, half:] * factor], 1)
            ys.append(dot(g.astype(BF16), mats[0, b]))
        for side, y in enumerate((ys[0] + ys[1], ys[0] - ys[1])):
            y = y.astype(BF16)
            cols = slice(side * half, (side + 1) * half)
            for a in range(2):
                rows = slice(a * half, (a + 1) * half)
                across[q, k, a, :half, cols] = y[rows, :half]
                across[q, k, a, half:, cols] = y[rows, half:]

    def back_left(k):
        vs = [(dot(mats[1, 0], across[q, k, 0]), dot(mats[1, 1], across[q, k, 1])) for q in range(PAIR)]
        for side in range(2):
            rows = slice(side * half, (side + 1) * half)
            pr, pi = probe[k, 0, rows, :], probe[k, 1, rows, :]
            sum_re, sum_im = probe_sum[rows_of(k, 0, rows), :], probe_sum[rows_of(k, 1, rows), :]
            for q, (v0, v1) in enumerate(vs):
                v = v0 + v1 if side == 0 else v0 - v1
                g_re, g_im = v[:half], v[half:]
                o_re, o_im = window[q, 0, rows, :], window[q, 1, rows, :]
                add_re = pr * g_re + pi * g_im
                add_im = pr * g_im - pi * g_re
                part[q, 0, rows, :] = add_re if k == 0 else part[q, 0, rows, :] + add_re
                part[q, 1, rows, :] = add_im if k == 0 else part[q, 1, rows, :] + add_im
                sum_re = sum_re + o_re * g_re + o_im * g_im
                sum_im = sum_im + o_re * g_im - o_im * g_re
            probe_sum[rows_of(k, 0, rows), :] = sum_re
            probe_sum[rows_of(k, 1, rows), :] = sum_im

    @pl.loop(0, (count + PAIR - 1) // PAIR)
    def _(step):
        numbers = [jnp.minimum(step * PAIR + q, count - 1) for q in range(PAIR)]
        amp_loads = [pltpu.make_async_copy(amps.at[n], amp.at[q], amp_sems.at[q]) for q, n in enumerate(numbers)]
        for load in amp_loads:
            load.start()
        places = []
        for q, n in enumerate(numbers):
            col_at = lax.rem(offsets[n, 1], tile_cols)
            places.append((lax.rem(offsets[n, 0], tile_rows), col_at // LANES, lax.rem(col_at, LANES)))
            take(q, *places[q])
        every = [(q, k) for k in range(modes) for q in range(PAIR)]
        for k in range(modes):
            psi(k)
        for q, k in every:
            left(q, k)
        for q, k in every:
            right(q, k)
        for load in amp_loads:
            load.wait()
        for q in range(PAIR):
            factors(q, step * PAIR + q < count)
        for q, k in every:
            back_right(q, k)
        for k in range(modes):
            back_left(k)
        for q in range(PAIR):
            give(q, *places[q])

    own_half = (lax.axis_index("narrow") & 1) * (probe_sum.shape[0] // 2)
    other_half = probe_sum.shape[0] // 2 - own_half
    pairs = [
        (probe_sum.at[pl.ds(pl.multiple_of(start, 8), probe_sum.shape[0] // 2), :], dst)
        for start, dst in ((other_half, probe_send), (own_half, probe_keep))
    ]
    for array, rows, cols in (
        (grad_low, low_rows, slice(0, tile_cols + extent)),
        (grad_right, slice(0, extent), rim),
        (grad_right_low, slice(extent, tile_rows), rim),
        (grad_own, slice(0, tile_rows), whole),
    ):
        pairs += [(grad.at[at], dst) for dst, at in strips(array, rows, cols)]
    stores = [pltpu.make_async_copy(src, dst, out_sems.at[n]) for n, (src, dst) in enumerate(pairs)]
    for store in stores:
        store.start()
    for store in stores:
        store.wait()


def run_slots(offsets, live, own, below, right, right_low, corner, probe, amps):
    extent = probe.shape[2]
    modes = probe.shape[0]
    tile_rows, tile_cols = own.shape[1:]
    mats = jnp.asarray(half_dft(extent))
    order = jnp.asarray(parity_order(extent)).astype(BF16)
    smem = pl.BlockSpec(memory_space=pltpu.SMEM)
    vmem = pl.BlockSpec(memory_space=pltpu.VMEM)
    hbm = pl.BlockSpec(memory_space=pltpu.HBM)
    anywhere = pl.BlockSpec(memory_space=pl.ANY)
    tiles_shape = (2, (tile_cols + extent) // LANES, tile_rows + extent, LANES)
    sum_shape = (modes * 2 * extent, extent)
    half_sum = (sum_shape[0] // 2, extent)
    outs = [(2, tile_rows, tile_cols), (2, extent, tile_cols + extent), (2, extent, extent)]
    outs += [(2, tile_rows - extent, extent), half_sum, half_sum]
    return pl.pallas_call(
        functools.partial(slots_kernel, tile_rows, tile_cols),
        out_shape=[jax.ShapeDtypeStruct(shape, F32) for shape in outs],
        in_specs=[smem, smem, hbm] + [anywhere] * 4 + [hbm, hbm, vmem, vmem],
        out_specs=[anywhere] * len(outs),
        scratch_shapes=[
            pltpu.VMEM(tiles_shape, F32),
            pltpu.VMEM(tiles_shape, F32),
            pltpu.VMEM(probe.shape, F32),
            pltpu.VMEM(sum_shape, F32),
            pltpu.VMEM((PAIR, 2, extent, extent), F32),
            pltpu.VMEM((PAIR, 2, extent, extent), F32),
            pltpu.VMEM((PAIR, extent, extent), F32),
            pltpu.VMEM((PAIR, 2, extent, extent // 2), F32),
            pltpu.VMEM((PAIR, modes, 2, extent, extent), BF16),
            pltpu.VMEM((PAIR, modes, 2, extent, extent), BF16),
            pltpu.VMEM((PAIR, modes, 2, extent, extent), F32),
            pltpu.VMEM((PAIR, 2, extent, extent // 2), F32),
            pltpu.VMEM((PAIR, modes, 2, extent, extent), BF16),
            pltpu.SemaphoreType.DMA((4 * tiles_shape[1],)),
            pltpu.SemaphoreType.DMA((PAIR,)),
            pltpu.SemaphoreType.DMA((4 * tiles_shape[1],)),
        ],
        compiler_params=pltpu.CompilerParams(vmem_limit_bytes=44 * 1024 * 1024),
        name="slots",
    )(offsets, live, own, below, right, right_low, corner, probe, amps, mats, order)


def shifted(value, axis, steps):
    count = lax.axis_size(axis)
    first, last = (max(0, -steps), min(count, count - steps))
    return lax.ppermute(value, axis, [(source, source + steps) for source in range(first, last)])


def place_in(bits):
    linear = lax.axis_index("wide") * lax.axis_size("narrow") + lax.axis_index("narrow")
    place = 0
    for n, bit in enumerate(bits):
        place = place + ((linear // bit) % 2) * (1 << n)
    return place


def partners(bits):
    return [sum(bit for n, bit in enumerate(bits) if step >> n & 1) for step in range(1 << len(bits))]


def swapped(value, mask):
    count = lax.axis_size("wide") * lax.axis_size("narrow")
    return lax.ppermute(value, ("wide", "narrow"), [(source, source ^ mask) for source in range(count)])


def add_kernel(bits, count, *refs):
    ins, outs = refs[:count], refs[count:]
    rows = outs[0].shape[0]
    place = place_in(bits)
    for step, out in enumerate(outs):
        at = pl.ds(pl.multiple_of((place ^ step) * rows, 8), rows)
        out[...] = sum(ref[at, :] for ref in ins)


def add_parts(parts, bits):
    count = 1 << len(bits)
    rows, cols = parts[0].shape
    vmem = pl.BlockSpec(memory_space=pltpu.VMEM)
    return pl.pallas_call(
        functools.partial(add_kernel, bits, len(parts)),
        out_shape=[jax.ShapeDtypeStruct((rows // count, cols), F32)] * count,
        in_specs=[vmem] * len(parts),
        out_specs=[vmem] * count,
        compiler_params=pltpu.CompilerParams(vmem_limit_bytes=8 * 1024 * 1024),
        name="add_parts",
    )(*parts)


def join_kernel(bits, scale, *refs):
    ins, out = refs[:-1], refs[-1]
    rows = ins[0].shape[0]
    place = place_in(bits)
    for step, ref in enumerate(ins):
        at = pl.ds(pl.multiple_of((place ^ step) * rows, 8), rows)
        out[at, :] = ref[...] if scale is None else ref[...] * scale


def join_parts(parts, bits, scale=None):
    rows, cols = parts[0].shape
    vmem = pl.BlockSpec(memory_space=pltpu.VMEM)
    return pl.pallas_call(
        functools.partial(join_kernel, bits, scale),
        out_shape=jax.ShapeDtypeStruct((rows * len(parts), cols), F32),
        in_specs=[vmem] * len(parts),
        out_specs=vmem,
        compiler_params=pltpu.CompilerParams(vmem_limit_bytes=8 * 1024 * 1024),
        name="join_parts",
    )(*parts)


def together(*values):
    return lax.optimization_barrier(values)


def sum_everywhere(keep, send, scale, grad_low, grad_right, came_right_low):
    narrow, wide = lax.axis_size("narrow"), lax.axis_size("wide")
    bits = [1 << n for n in range((narrow * wide).bit_length() - 1)]
    rest = bits[1:]
    groups = [tuple(rest[n :: (len(rest) + 1) // 2]) for n in range((len(rest) + 1) // 2)]
    cols = grad_low.shape[2] - grad_right.shape[2]
    parts = [keep, swapped(send, bits[0])]
    for n, group in enumerate(groups):
        pieces = add_parts(parts, group)
        if n == 1:
            pieces, grad_low = together(pieces, grad_low)
            came_low = shifted(grad_low, "narrow", 1)
        parts = [pieces[0]] + [swapped(piece, mask) for piece, mask in zip(pieces[1:], partners(group)[1:])]
        if n == 0:
            parts, came_right_low = together(parts, came_right_low)
    value = add_parts(parts, ())[0]
    for group in reversed(groups):
        if group == groups[0]:
            _, grad_right = together(value, grad_right + came_low[:, :, cols:])
            came_right = shifted(grad_right, "wide", 1)
        parts = [value] + [swapped(value, mask) for mask in partners(group)[1:]]
        if group != groups[0]:
            value = join_parts(parts, group)
    parts = parts + [swapped(part, bits[0]) for part in parts]
    return join_parts(parts, groups[0] + (bits[0],), scale), came_low[:, :, :cols], came_right, came_right_low


def on_device(object_field, probe, amplitudes, offsets, live):
    extent = probe.shape[2]
    top, whole = together(object_field[:, :extent], object_field)
    right = shifted(top, "wide", -1)
    below = shifted(top, "narrow", -1)
    right_low = shifted(whole[:, extent:], "wide", -1)
    corner = shifted(right, "narrow", -1)
    grad_own, grad_low, grad_right, grad_right_low, keep, send = run_slots(
        offsets, live, object_field, below, right, right_low, corner, probe, amplitudes
    )
    came_right_low = shifted(grad_right_low, "wide", 1)
    total_slots = lax.axis_size("wide") * lax.axis_size("narrow") * offsets.shape[0]
    probe_grad, came_below, came_right, came_right_low = sum_everywhere(
        keep, send, 1.0 / math.sqrt(total_slots), grad_low, grad_right, came_right_low
    )
    rims = jnp.concatenate([came_right, came_right_low], 1)
    object_grad = grad_own.at[:, :extent, :].add(came_below).at[:, :, :extent].add(rims)
    return (object_grad, probe_grad.reshape(probe.shape))


def solution(mesh):
    return jax.shard_map(
        on_device,
        mesh=mesh,
        in_specs=(
            P(None, "narrow", "wide"),
            P(),
            P(("wide", "narrow"), None, None),
            P(("wide", "narrow"), None),
            P(("wide", "narrow")),
        ),
        out_specs=(P(None, "narrow", "wide"), P()),
        check_vma=False,
    )
```

```python
import functools
import math

import jax
import jax.numpy as jnp
import ml_dtypes
import numpy as np
from jax import lax
from jax.experimental import pallas as pl
from jax.experimental.pallas import tpu as pltpu
from jax.sharding import PartitionSpec as P

F32 = jnp.float32
BF16 = jnp.bfloat16
LANES = 128
PAIR = 2


def half_dft(extent):
    half = extent // 2
    blocks = []
    for parity in range(2):
        freq = 2 * np.arange(half)[:, None] + parity
        angles = (freq * np.arange(half)[None, :] % extent) * (2.0 * math.pi / extent)
        cosine = np.cos(angles) / math.sqrt(extent)
        sine = np.sin(angles) / math.sqrt(extent)
        blocks.append(np.block([[cosine, sine], [-sine, cosine]]))
    both = np.stack(blocks)
    return np.stack([both, np.swapaxes(both, 1, 2)]).astype(ml_dtypes.bfloat16)


def parity_order(extent):
    order = np.concatenate([np.arange(0, extent, 2), np.arange(1, extent, 2)])
    matrix = np.zeros((extent, extent), np.float32)
    matrix[order, np.arange(extent)] = 1.0
    return matrix


def dot(a, b):
    return jnp.dot(a, b, preferred_element_type=F32)


def slots_kernel(
    tile_rows, tile_cols, offsets, live, own, below, right, right_low, corner, probe_in, amps, mats, order,
    grad_own, grad_low, grad_right, grad_right_low, probe_keep, probe_send,
    ext, grad, probe, probe_sum, window, part, amp, sorted_amp, waves, inner, far, power, across,
    in_sems, amp_sems, out_sems,
):
    modes = probe.shape[0]
    extent = probe.shape[2]
    half = extent // 2
    rows_step = 32
    wide_cols = extent // LANES + 1
    count = live[0]

    low_rows = slice(tile_rows, tile_rows + extent)
    whole = slice(0, tile_cols)
    rim = slice(tile_cols, tile_cols + extent)
    places = [
        (own, slice(0, tile_rows), whole),
        (below, low_rows, whole),
        (right, slice(0, extent), rim),
        (right_low, slice(extent, tile_rows), rim),
        (corner, low_rows, rim),
    ]

    def strips(array, rows, cols):
        for start in range(0, cols.stop - cols.start, LANES):
            yield array.at[:, :, start : start + LANES], ((slice(None), (cols.start + start) // LANES, rows, slice(None)))

    strip_loads = [(src, at) for array, rows, cols in places for src, at in strips(array, rows, cols)]
    loads = [pltpu.make_async_copy(src, ext.at[at], in_sems.at[n]) for n, (src, at) in enumerate(strip_loads)]
    loads.append(pltpu.make_async_copy(probe_in, probe, in_sems.at[len(loads)]))
    for load in loads:
        load.start()
    grad[...] = jnp.zeros_like(grad)
    probe_sum[...] = jnp.zeros_like(probe_sum)
    for load in loads:
        load.wait()
    lane = lax.broadcasted_iota(jnp.int32, (rows_step, LANES), 1)

    def rows_of(k, c, rows):
        start = (k * 2 + c) * extent
        return slice(start + rows.start, start + rows.stop)

    def take(q, row_at, first_tile, shift):
        back = lax.rem(LANES - shift, LANES)
        for plane in range(2):
            for row in range(0, extent, rows_step):
                rows = pl.ds(row_at + row, rows_step)
                turned = [pltpu.roll(ext[plane, first_tile + c, rows, :], back, 1) for c in range(wide_cols)]
                for c in range(wide_cols - 1):
                    window[q, plane, row : row + rows_step, c * LANES : (c + 1) * LANES] = jnp.where(
                        lane < LANES - shift, turned[c], turned[c + 1]
                    )

    def give(q, row_at, first_tile, shift):
        zero = jnp.zeros((rows_step, LANES), F32)
        for plane in range(2):
            for row in range(0, extent, rows_step):
                rows = pl.ds(row_at + row, rows_step)
                turned = [zero]
                for c in range(wide_cols - 1):
                    turned.append(pltpu.roll(part[q, plane, row : row + rows_step, c * LANES : (c + 1) * LANES], shift, 1))
                turned.append(zero)
                for c in range(wide_cols):
                    grad[plane, first_tile + c, rows, :] += jnp.where(lane >= shift, turned[c + 1], turned[c])

    def psi(k):
        for row in range(0, half, rows_step):
            spans = [slice(base, base + rows_step) for base in (row, half + row)]
            probes = [(probe[k, 0, rows, :], probe[k, 1, rows, :]) for rows in spans]
            for q in range(PAIR):
                waves_at = []
                for rows, (pr, pi) in zip(spans, probes):
                    o_re, o_im = window[q, 0, rows, :], window[q, 1, rows, :]
                    waves_at.append((pr * o_re - pi * o_im, pr * o_im + pi * o_re))
                for c in range(2):
                    rows = slice(c * half + row, c * half + row + rows_step)
                    waves[q, k, 0, rows, :] = (waves_at[0][c] + waves_at[1][c]).astype(BF16)
                    waves[q, k, 1, rows, :] = (waves_at[0][c] - waves_at[1][c]).astype(BF16)

    def left(q, k):
        for a in range(2):
            z = dot(mats[0, a], waves[q, k, a])
            left, right_half = z[:, :half], z[:, half:]
            for b, value in enumerate((left + right_half, left - right_half)):
                value = value.astype(BF16)
                inner[q, k, b, a * half : (a + 1) * half, :half] = value[:half]
                inner[q, k, b, a * half : (a + 1) * half, half:] = value[half:]

    def right(q, k):
        for b in range(2):
            f = dot(inner[q, k, b], mats[1, b])
            far[q, k, b] = f
            own_power = f[:, :half] * f[:, :half] + f[:, half:] * f[:, half:]
            power[q, b] = own_power if k == 0 else power[q, b] + own_power

    def factors(q, used):
        high = amp[q].astype(BF16)
        low = (amp[q] - high.astype(F32)).astype(BF16)
        turned = dot(high, order[...]) + dot(low, order[...])
        for b in range(2):
            sorted_amp[q, b] = turned[:, b * half : (b + 1) * half]
        for b in range(2):
            for a in range(2):
                rows = slice(a * half, (a + 1) * half)
                for_rows = sorted_amp[q, b, pl.ds(a, half, 2), :]
                factor = 2.0 - 2.0 * for_rows * lax.rsqrt(power[q, b, rows] + 0.5)
                power[q, b, rows] = factor if q == 0 else jnp.where(used, factor, 0.0)

    def back_right(q, k):
        ys = []
        for b in range(2):
            factor = power[q, b]
            g = jnp.concatenate([far[q, k, b, :, :half] * factor, far[q, k, b, :, half:] * factor], 1)
            ys.append(dot(g.astype(BF16), mats[0, b]))
        for side, y in enumerate((ys[0] + ys[1], ys[0] - ys[1])):
            y = y.astype(BF16)
            cols = slice(side * half, (side + 1) * half)
            for a in range(2):
                rows = slice(a * half, (a + 1) * half)
                across[q, k, a, :half, cols] = y[rows, :half]
                across[q, k, a, half:, cols] = y[rows, half:]

    def back_left(k):
        vs = [(dot(mats[1, 0], across[q, k, 0]), dot(mats[1, 1], across[q, k, 1])) for q in range(PAIR)]
        for side in range(2):
            rows = slice(side * half, (side + 1) * half)
            pr, pi = probe[k, 0, rows, :], probe[k, 1, rows, :]
            sum_re, sum_im = probe_sum[rows_of(k, 0, rows), :], probe_sum[rows_of(k, 1, rows), :]
            for q, (v0, v1) in enumerate(vs):
                v = v0 + v1 if side == 0 else v0 - v1
                g_re, g_im = v[:half], v[half:]
                o_re, o_im = window[q, 0, rows, :], window[q, 1, rows, :]
                add_re = pr * g_re + pi * g_im
                add_im = pr * g_im - pi * g_re
                part[q, 0, rows, :] = add_re if k == 0 else part[q, 0, rows, :] + add_re
                part[q, 1, rows, :] = add_im if k == 0 else part[q, 1, rows, :] + add_im
                sum_re = sum_re + o_re * g_re + o_im * g_im
                sum_im = sum_im + o_re * g_im - o_im * g_re
            probe_sum[rows_of(k, 0, rows), :] = sum_re
            probe_sum[rows_of(k, 1, rows), :] = sum_im

    @pl.loop(0, (count + PAIR - 1) // PAIR)
    def _(step):
        numbers = [jnp.minimum(step * PAIR + q, count - 1) for q in range(PAIR)]
        amp_loads = [pltpu.make_async_copy(amps.at[n], amp.at[q], amp_sems.at[q]) for q, n in enumerate(numbers)]
        for load in amp_loads:
            load.start()
        places = []
        for q, n in enumerate(numbers):
            col_at = lax.rem(offsets[n, 1], tile_cols)
            places.append((lax.rem(offsets[n, 0], tile_rows), col_at // LANES, lax.rem(col_at, LANES)))
            take(q, *places[q])
        every = [(q, k) for k in range(modes) for q in range(PAIR)]
        for k in range(modes):
            psi(k)
        for q, k in every:
            left(q, k)
        for q, k in every:
            right(q, k)
        for load in amp_loads:
            load.wait()
        for q in range(PAIR):
            factors(q, step * PAIR + q < count)
        for q, k in every:
            back_right(q, k)
        for k in range(modes):
            back_left(k)
        for q in range(PAIR):
            give(q, *places[q])

    own_half = (lax.axis_index("narrow") & 1) * (probe_sum.shape[0] // 2)
    other_half = probe_sum.shape[0] // 2 - own_half
    pairs = [
        (probe_sum.at[pl.ds(pl.multiple_of(start, 8), probe_sum.shape[0] // 2), :], dst)
        for start, dst in ((other_half, probe_send), (own_half, probe_keep))
    ]
    for array, rows, cols in (
        (grad_low, low_rows, slice(0, tile_cols + extent)),
        (grad_right, slice(0, extent), rim),
        (grad_right_low, slice(extent, tile_rows), rim),
        (grad_own, slice(0, tile_rows), whole),
    ):
        pairs += [(grad.at[at], dst) for dst, at in strips(array, rows, cols)]
    stores = [pltpu.make_async_copy(src, dst, out_sems.at[n]) for n, (src, dst) in enumerate(pairs)]
    for store in stores:
        store.start()
    for store in stores:
        store.wait()


def run_slots(offsets, live, own, below, right, right_low, corner, probe, amps):
    extent = probe.shape[2]
    modes = probe.shape[0]
    tile_rows, tile_cols = own.shape[1:]
    mats = jnp.asarray(half_dft(extent))
    order = jnp.asarray(parity_order(extent)).astype(BF16)
    smem = pl.BlockSpec(memory_space=pltpu.SMEM)
    vmem = pl.BlockSpec(memory_space=pltpu.VMEM)
    hbm = pl.BlockSpec(memory_space=pltpu.HBM)
    anywhere = pl.BlockSpec(memory_space=pl.ANY)
    tiles_shape = (2, (tile_cols + extent) // LANES, tile_rows + extent, LANES)
    sum_shape = (modes * 2 * extent, extent)
    half_sum = (sum_shape[0] // 2, extent)
    outs = [(2, tile_rows, tile_cols), (2, extent, tile_cols + extent), (2, extent, extent)]
    outs += [(2, tile_rows - extent, extent), half_sum, half_sum]
    return pl.pallas_call(
        functools.partial(slots_kernel, tile_rows, tile_cols),
        out_shape=[jax.ShapeDtypeStruct(shape, F32) for shape in outs],
        in_specs=[smem, smem, hbm] + [anywhere] * 4 + [hbm, hbm, vmem, vmem],
        out_specs=[anywhere] * len(outs),
        scratch_shapes=[
            pltpu.VMEM(tiles_shape, F32),
            pltpu.VMEM(tiles_shape, F32),
            pltpu.VMEM(probe.shape, F32),
            pltpu.VMEM(sum_shape, F32),
            pltpu.VMEM((PAIR, 2, extent, extent), F32),
            pltpu.VMEM((PAIR, 2, extent, extent), F32),
            pltpu.VMEM((PAIR, extent, extent), F32),
            pltpu.VMEM((PAIR, 2, extent, extent // 2), F32),
            pltpu.VMEM((PAIR, modes, 2, extent, extent), BF16),
            pltpu.VMEM((PAIR, modes, 2, extent, extent), BF16),
            pltpu.VMEM((PAIR, modes, 2, extent, extent), F32),
            pltpu.VMEM((PAIR, 2, extent, extent // 2), F32),
            pltpu.VMEM((PAIR, modes, 2, extent, extent), BF16),
            pltpu.SemaphoreType.DMA((4 * tiles_shape[1],)),
            pltpu.SemaphoreType.DMA((PAIR,)),
            pltpu.SemaphoreType.DMA((4 * tiles_shape[1],)),
        ],
        compiler_params=pltpu.CompilerParams(vmem_limit_bytes=44 * 1024 * 1024),
        name="slots",
    )(offsets, live, own, below, right, right_low, corner, probe, amps, mats, order)


def shifted(value, axis, steps):
    count = lax.axis_size(axis)
    first, last = (max(0, -steps), min(count, count - steps))
    return lax.ppermute(value, axis, [(source, source + steps) for source in range(first, last)])


def place_in(bits):
    linear = lax.axis_index("wide") * lax.axis_size("narrow") + lax.axis_index("narrow")
    place = 0
    for n, bit in enumerate(bits):
        place = place + ((linear // bit) % 2) * (1 << n)
    return place


def partners(bits):
    return [sum(bit for n, bit in enumerate(bits) if step >> n & 1) for step in range(1 << len(bits))]


def swapped(value, mask):
    count = lax.axis_size("wide") * lax.axis_size("narrow")
    return lax.ppermute(value, ("wide", "narrow"), [(source, source ^ mask) for source in range(count)])


def add_kernel(bits, count, scale, *refs):
    ins, outs = refs[:count], refs[count:]
    rows = outs[0].shape[0]
    place = place_in(bits)
    for step, out in enumerate(outs):
        at = pl.ds(pl.multiple_of((place ^ step) * rows, 8), rows)
        total = sum(ref[at, :] for ref in ins)
        out[...] = total if scale is None else total * scale


def add_parts(parts, bits, scale=None):
    count = 1 << len(bits)
    rows, cols = parts[0].shape
    vmem = pl.BlockSpec(memory_space=pltpu.VMEM)
    return pl.pallas_call(
        functools.partial(add_kernel, bits, len(parts), scale),
        out_shape=[jax.ShapeDtypeStruct((rows // count, cols), F32)] * count,
        in_specs=[vmem] * len(parts),
        out_specs=[vmem] * count,
        compiler_params=pltpu.CompilerParams(vmem_limit_bytes=8 * 1024 * 1024),
        name="add_parts",
    )(*parts)


def join_kernel(bits, *refs):
    ins, out = refs[:-1], refs[-1]
    rows = ins[0].shape[0]
    place = place_in(bits)
    for step, ref in enumerate(ins):
        at = pl.ds(pl.multiple_of((place ^ step) * rows, 8), rows)
        out[at, :] = ref[...]


def join_parts(parts, bits):
    rows, cols = parts[0].shape
    vmem = pl.BlockSpec(memory_space=pltpu.VMEM)
    return pl.pallas_call(
        functools.partial(join_kernel, bits),
        out_shape=jax.ShapeDtypeStruct((rows * len(parts), cols), F32),
        in_specs=[vmem] * len(parts),
        out_specs=vmem,
        compiler_params=pltpu.CompilerParams(vmem_limit_bytes=8 * 1024 * 1024),
        name="join_parts",
    )(*parts)


def place_kernel(bits, *refs):
    ins, out, sems = refs[:-2], refs[-2], refs[-1]
    rows = ins[0].shape[0]
    place = place_in(bits)
    copies = []
    for step, ref in enumerate(ins):
        at = pl.ds(pl.multiple_of((place ^ step) * rows, 8), rows)
        copies.append(pltpu.make_async_copy(ref, out.at[at, :], sems.at[step]))
    for copy in copies:
        copy.start()
    for copy in copies:
        copy.wait()


def place_parts(parts, bits):
    rows, cols = parts[0].shape
    anywhere = pl.BlockSpec(memory_space=pl.ANY)
    return pl.pallas_call(
        functools.partial(place_kernel, bits),
        out_shape=jax.ShapeDtypeStruct((rows * len(parts), cols), F32),
        in_specs=[anywhere] * len(parts),
        out_specs=anywhere,
        scratch_shapes=[pltpu.SemaphoreType.DMA((len(parts),))],
        compiler_params=pltpu.CompilerParams(vmem_limit_bytes=8 * 1024 * 1024),
        name="place_parts",
    )(*parts)


def together(*values):
    return lax.optimization_barrier(values)


def sum_everywhere(keep, send, scale, grad_low, grad_right, came_right_low):
    narrow, wide = lax.axis_size("narrow"), lax.axis_size("wide")
    bits = [1 << n for n in range((narrow * wide).bit_length() - 1)]
    rest = bits[1:]
    groups = [tuple(rest[n :: (len(rest) + 1) // 2]) for n in range((len(rest) + 1) // 2)]
    cols = grad_low.shape[2] - grad_right.shape[2]
    parts = [keep, swapped(send, bits[0])]
    for n, group in enumerate(groups):
        pieces = add_parts(parts, group)
        if n == 1:
            _, grad_low = together(pieces, grad_low)
            came_low = shifted(grad_low, "narrow", 1)
        parts = [pieces[0]] + [swapped(piece, mask) for piece, mask in zip(pieces[1:], partners(group)[1:])]
        if n == 0:
            parts, came_right_low = together(parts, came_right_low)
    value = add_parts(parts, (), scale)[0]
    for group in reversed(groups):
        if group == groups[0]:
            _, grad_right = together(value, grad_right + came_low[:, :, cols:])
            came_right = shifted(grad_right, "wide", 1)
        parts = [value] + [swapped(value, mask) for mask in partners(group)[1:]]
        if group != groups[0]:
            value = join_parts(parts, group)
    parts = parts + [swapped(part, bits[0]) for part in parts]
    return place_parts(parts, groups[0] + (bits[0],)), came_low[:, :, :cols], came_right, came_right_low


def on_device(object_field, probe, amplitudes, offsets, live):
    extent = probe.shape[2]
    top, whole = together(object_field[:, :extent], object_field)
    right = shifted(top, "wide", -1)
    below = shifted(top, "narrow", -1)
    right_low = shifted(whole[:, extent:], "wide", -1)
    corner = shifted(right, "narrow", -1)
    grad_own, grad_low, grad_right, grad_right_low, keep, send = run_slots(
        offsets, live, object_field, below, right, right_low, corner, probe, amplitudes
    )
    came_right_low = shifted(grad_right_low, "wide", 1)
    total_slots = lax.axis_size("wide") * lax.axis_size("narrow") * offsets.shape[0]
    probe_grad, came_below, came_right, came_right_low = sum_everywhere(
        keep, send, 1.0 / math.sqrt(total_slots), grad_low, grad_right, came_right_low
    )
    rims = jnp.concatenate([came_right, came_right_low], 1)
    object_grad = grad_own.at[:, :extent, :].add(came_below).at[:, :, :extent].add(rims)
    return (object_grad, probe_grad.reshape(probe.shape))


def solution(mesh):
    return jax.shard_map(
        on_device,
        mesh=mesh,
        in_specs=(
            P(None, "narrow", "wide"),
            P(),
            P(("wide", "narrow"), None, None),
            P(("wide", "narrow"), None),
            P(("wide", "narrow")),
        ),
        out_specs=(P(None, "narrow", "wide"), P()),
        check_vma=False,
    )
```

```python
import functools
import math

import jax
import jax.numpy as jnp
import ml_dtypes
import numpy as np
from jax import lax
from jax.experimental import pallas as pl
from jax.experimental.pallas import tpu as pltpu
from jax.sharding import PartitionSpec as P

F32 = jnp.float32
BF16 = jnp.bfloat16
LANES = 128
PAIR = 4


def half_dft(extent):
    half = extent // 2
    blocks = []
    for parity in range(2):
        freq = 2 * np.arange(half)[:, None] + parity
        angles = (freq * np.arange(half)[None, :] % extent) * (2.0 * math.pi / extent)
        cosine = np.cos(angles) / math.sqrt(extent)
        sine = np.sin(angles) / math.sqrt(extent)
        blocks.append(np.block([[cosine, sine], [-sine, cosine]]))
    both = np.stack(blocks)
    return np.stack([both, np.swapaxes(both, 1, 2)]).astype(ml_dtypes.bfloat16)


def parity_order(extent):
    order = np.concatenate([np.arange(0, extent, 2), np.arange(1, extent, 2)])
    matrix = np.zeros((extent, extent), np.float32)
    matrix[order, np.arange(extent)] = 1.0
    return matrix


def dot(a, b):
    return jnp.dot(a, b, preferred_element_type=F32)


def slots_kernel(
    tile_rows, tile_cols, offsets, live, own, below, right, right_low, corner, probe_in, amps, mats, order,
    grad_own, grad_low, grad_right, grad_right_low, probe_keep, probe_send,
    ext, grad, probe, probe_sum, window, part, amp, sorted_amp, waves, inner, far, power, across,
    in_sems, amp_sems, out_sems,
):
    modes = probe.shape[0]
    extent = probe.shape[2]
    half = extent // 2
    rows_step = 32
    wide_cols = extent // LANES + 1
    count = live[0]

    low_rows = slice(tile_rows, tile_rows + extent)
    whole = slice(0, tile_cols)
    rim = slice(tile_cols, tile_cols + extent)
    places = [
        (own, slice(0, tile_rows), whole),
        (below, low_rows, whole),
        (right, slice(0, extent), rim),
        (right_low, slice(extent, tile_rows), rim),
        (corner, low_rows, rim),
    ]

    def strips(array, rows, cols):
        for start in range(0, cols.stop - cols.start, LANES):
            yield array.at[:, :, start : start + LANES], ((slice(None), (cols.start + start) // LANES, rows, slice(None)))

    strip_loads = [(src, at) for array, rows, cols in places for src, at in strips(array, rows, cols)]
    loads = [pltpu.make_async_copy(src, ext.at[at], in_sems.at[n]) for n, (src, at) in enumerate(strip_loads)]
    loads.append(pltpu.make_async_copy(probe_in, probe, in_sems.at[len(loads)]))
    for load in loads:
        load.start()
    grad[...] = jnp.zeros_like(grad)
    probe_sum[...] = jnp.zeros_like(probe_sum)
    for load in loads:
        load.wait()
    lane = lax.broadcasted_iota(jnp.int32, (rows_step, LANES), 1)

    def rows_of(k, c, rows):
        start = (k * 2 + c) * extent
        return slice(start + rows.start, start + rows.stop)

    def take(q, row_at, first_tile, shift):
        back = lax.rem(LANES - shift, LANES)
        for plane in range(2):
            for row in range(0, extent, rows_step):
                rows = pl.ds(row_at + row, rows_step)
                turned = [pltpu.roll(ext[plane, first_tile + c, rows, :], back, 1) for c in range(wide_cols)]
                for c in range(wide_cols - 1):
                    window[q, plane, row : row + rows_step, c * LANES : (c + 1) * LANES] = jnp.where(
                        lane < LANES - shift, turned[c], turned[c + 1]
                    )

    def give(q, row_at, first_tile, shift):
        zero = jnp.zeros((rows_step, LANES), F32)
        for plane in range(2):
            for row in range(0, extent, rows_step):
                rows = pl.ds(row_at + row, rows_step)
                turned = [zero]
                for c in range(wide_cols - 1):
                    turned.append(pltpu.roll(part[q, plane, row : row + rows_step, c * LANES : (c + 1) * LANES], shift, 1))
                turned.append(zero)
                for c in range(wide_cols):
                    grad[plane, first_tile + c, rows, :] += jnp.where(lane >= shift, turned[c + 1], turned[c])

    def psi(k):
        for row in range(0, half, rows_step):
            spans = [slice(base, base + rows_step) for base in (row, half + row)]
            probes = [(probe[k, 0, rows, :], probe[k, 1, rows, :]) for rows in spans]
            for q in range(PAIR):
                waves_at = []
                for rows, (pr, pi) in zip(spans, probes):
                    o_re, o_im = window[q, 0, rows, :], window[q, 1, rows, :]
                    waves_at.append((pr * o_re - pi * o_im, pr * o_im + pi * o_re))
                for c in range(2):
                    rows = slice(c * half + row, c * half + row + rows_step)
                    waves[q, k, 0, rows, :] = (waves_at[0][c] + waves_at[1][c]).astype(BF16)
                    waves[q, k, 1, rows, :] = (waves_at[0][c] - waves_at[1][c]).astype(BF16)

    def left(q, k):
        for a in range(2):
            z = dot(mats[0, a], waves[q, k, a])
            left, right_half = z[:, :half], z[:, half:]
            for b, value in enumerate((left + right_half, left - right_half)):
                value = value.astype(BF16)
                inner[q, k, b, a * half : (a + 1) * half, :half] = value[:half]
                inner[q, k, b, a * half : (a + 1) * half, half:] = value[half:]

    def right(q, k):
        for b in range(2):
            f = dot(inner[q, k, b], mats[1, b])
            far[q, k, b] = f
            own_power = f[:, :half] * f[:, :half] + f[:, half:] * f[:, half:]
            power[q, b] = own_power if k == 0 else power[q, b] + own_power

    def factors(q, used):
        high = amp[q].astype(BF16)
        low = (amp[q] - high.astype(F32)).astype(BF16)
        turned = dot(high, order[...]) + dot(low, order[...])
        for b in range(2):
            sorted_amp[q, b] = turned[:, b * half : (b + 1) * half]
        for b in range(2):
            for a in range(2):
                rows = slice(a * half, (a + 1) * half)
                for_rows = sorted_amp[q, b, pl.ds(a, half, 2), :]
                factor = 2.0 - 2.0 * for_rows * lax.rsqrt(power[q, b, rows] + 0.5)
                power[q, b, rows] = factor if q == 0 else jnp.where(used, factor, 0.0)

    def back_right(q, k):
        ys = []
        for b in range(2):
            factor = power[q, b]
            g = jnp.concatenate([far[q, k, b, :, :half] * factor, far[q, k, b, :, half:] * factor], 1)
            ys.append(dot(g.astype(BF16), mats[0, b]))
        for side, y in enumerate((ys[0] + ys[1], ys[0] - ys[1])):
            y = y.astype(BF16)
            cols = slice(side * half, (side + 1) * half)
            for a in range(2):
                rows = slice(a * half, (a + 1) * half)
                across[q, k, a, :half, cols] = y[rows, :half]
                across[q, k, a, half:, cols] = y[rows, half:]

    def back_left(k):
        vs = [(dot(mats[1, 0], across[q, k, 0]), dot(mats[1, 1], across[q, k, 1])) for q in range(PAIR)]
        for side in range(2):
            rows = slice(side * half, (side + 1) * half)
            pr, pi = probe[k, 0, rows, :], probe[k, 1, rows, :]
            sum_re, sum_im = probe_sum[rows_of(k, 0, rows), :], probe_sum[rows_of(k, 1, rows), :]
            for q, (v0, v1) in enumerate(vs):
                v = v0 + v1 if side == 0 else v0 - v1
                g_re, g_im = v[:half], v[half:]
                o_re, o_im = window[q, 0, rows, :], window[q, 1, rows, :]
                add_re = pr * g_re + pi * g_im
                add_im = pr * g_im - pi * g_re
                part[q, 0, rows, :] = add_re if k == 0 else part[q, 0, rows, :] + add_re
                part[q, 1, rows, :] = add_im if k == 0 else part[q, 1, rows, :] + add_im
                sum_re = sum_re + o_re * g_re + o_im * g_im
                sum_im = sum_im + o_re * g_im - o_im * g_re
            probe_sum[rows_of(k, 0, rows), :] = sum_re
            probe_sum[rows_of(k, 1, rows), :] = sum_im

    @pl.loop(0, (count + PAIR - 1) // PAIR)
    def _(step):
        numbers = [jnp.minimum(step * PAIR + q, count - 1) for q in range(PAIR)]
        amp_loads = [pltpu.make_async_copy(amps.at[n], amp.at[q], amp_sems.at[q]) for q, n in enumerate(numbers)]
        for load in amp_loads:
            load.start()
        places = []
        for q, n in enumerate(numbers):
            col_at = lax.rem(offsets[n, 1], tile_cols)
            places.append((lax.rem(offsets[n, 0], tile_rows), col_at // LANES, lax.rem(col_at, LANES)))
            take(q, *places[q])
        every = [(q, k) for k in range(modes) for q in range(PAIR)]
        for k in range(modes):
            psi(k)
        for q, k in every:
            left(q, k)
        for q, k in every:
            right(q, k)
        for load in amp_loads:
            load.wait()
        for q in range(PAIR):
            factors(q, step * PAIR + q < count)
        for q, k in every:
            back_right(q, k)
        for k in range(modes):
            back_left(k)
        for q in range(PAIR):
            give(q, *places[q])

    own_half = (lax.axis_index("narrow") & 1) * (probe_sum.shape[0] // 2)
    other_half = probe_sum.shape[0] // 2 - own_half
    pairs = [
        (probe_sum.at[pl.ds(pl.multiple_of(start, 8), probe_sum.shape[0] // 2), :], dst)
        for start, dst in ((other_half, probe_send), (own_half, probe_keep))
    ]
    for array, rows, cols in (
        (grad_low, low_rows, slice(0, tile_cols + extent)),
        (grad_right, slice(0, extent), rim),
        (grad_right_low, slice(extent, tile_rows), rim),
        (grad_own, slice(0, tile_rows), whole),
    ):
        pairs += [(grad.at[at], dst) for dst, at in strips(array, rows, cols)]
    stores = [pltpu.make_async_copy(src, dst, out_sems.at[n]) for n, (src, dst) in enumerate(pairs)]
    for store in stores:
        store.start()
    for store in stores:
        store.wait()


def run_slots(offsets, live, own, below, right, right_low, corner, probe, amps):
    extent = probe.shape[2]
    modes = probe.shape[0]
    tile_rows, tile_cols = own.shape[1:]
    mats = jnp.asarray(half_dft(extent))
    order = jnp.asarray(parity_order(extent)).astype(BF16)
    smem = pl.BlockSpec(memory_space=pltpu.SMEM)
    vmem = pl.BlockSpec(memory_space=pltpu.VMEM)
    hbm = pl.BlockSpec(memory_space=pltpu.HBM)
    anywhere = pl.BlockSpec(memory_space=pl.ANY)
    tiles_shape = (2, (tile_cols + extent) // LANES, tile_rows + extent, LANES)
    sum_shape = (modes * 2 * extent, extent)
    half_sum = (sum_shape[0] // 2, extent)
    outs = [(2, tile_rows, tile_cols), (2, extent, tile_cols + extent), (2, extent, extent)]
    outs += [(2, tile_rows - extent, extent), half_sum, half_sum]
    return pl.pallas_call(
        functools.partial(slots_kernel, tile_rows, tile_cols),
        out_shape=[jax.ShapeDtypeStruct(shape, F32) for shape in outs],
        in_specs=[smem, smem, hbm] + [anywhere] * 4 + [hbm, hbm, vmem, vmem],
        out_specs=[anywhere] * len(outs),
        scratch_shapes=[
            pltpu.VMEM(tiles_shape, F32),
            pltpu.VMEM(tiles_shape, F32),
            pltpu.VMEM(probe.shape, F32),
            pltpu.VMEM(sum_shape, F32),
            pltpu.VMEM((PAIR, 2, extent, extent), F32),
            pltpu.VMEM((PAIR, 2, extent, extent), F32),
            pltpu.VMEM((PAIR, extent, extent), F32),
            pltpu.VMEM((PAIR, 2, extent, extent // 2), F32),
            pltpu.VMEM((PAIR, modes, 2, extent, extent), BF16),
            pltpu.VMEM((PAIR, modes, 2, extent, extent), BF16),
            pltpu.VMEM((PAIR, modes, 2, extent, extent), F32),
            pltpu.VMEM((PAIR, 2, extent, extent // 2), F32),
            pltpu.VMEM((PAIR, modes, 2, extent, extent), BF16),
            pltpu.SemaphoreType.DMA((4 * tiles_shape[1],)),
            pltpu.SemaphoreType.DMA((PAIR,)),
            pltpu.SemaphoreType.DMA((4 * tiles_shape[1],)),
        ],
        compiler_params=pltpu.CompilerParams(vmem_limit_bytes=44 * 1024 * 1024),
        name="slots",
    )(offsets, live, own, below, right, right_low, corner, probe, amps, mats, order)


def shifted(value, axis, steps):
    count = lax.axis_size(axis)
    first, last = (max(0, -steps), min(count, count - steps))
    return lax.ppermute(value, axis, [(source, source + steps) for source in range(first, last)])


def place_in(bits):
    linear = lax.axis_index("wide") * lax.axis_size("narrow") + lax.axis_index("narrow")
    place = 0
    for n, bit in enumerate(bits):
        place = place + ((linear // bit) % 2) * (1 << n)
    return place


def partners(bits):
    return [sum(bit for n, bit in enumerate(bits) if step >> n & 1) for step in range(1 << len(bits))]


def swapped(value, mask):
    count = lax.axis_size("wide") * lax.axis_size("narrow")
    return lax.ppermute(value, ("wide", "narrow"), [(source, source ^ mask) for source in range(count)])


def add_kernel(bits, count, scale, *refs):
    ins, outs = refs[:count], refs[count:]
    rows = outs[0].shape[0]
    place = place_in(bits)
    for step, out in enumerate(outs):
        at = pl.ds(pl.multiple_of((place ^ step) * rows, 8), rows)
        total = sum(ref[at, :] for ref in ins)
        out[...] = total if scale is None else total * scale


def add_parts(parts, bits, scale=None):
    count = 1 << len(bits)
    rows, cols = parts[0].shape
    vmem = pl.BlockSpec(memory_space=pltpu.VMEM)
    return pl.pallas_call(
        functools.partial(add_kernel, bits, len(parts), scale),
        out_shape=[jax.ShapeDtypeStruct((rows // count, cols), F32)] * count,
        in_specs=[vmem] * len(parts),
        out_specs=[vmem] * count,
        compiler_params=pltpu.CompilerParams(vmem_limit_bytes=8 * 1024 * 1024),
        name="add_parts",
    )(*parts)


def join_kernel(bits, *refs):
    ins, out = refs[:-1], refs[-1]
    rows = ins[0].shape[0]
    place = place_in(bits)
    for step, ref in enumerate(ins):
        at = pl.ds(pl.multiple_of((place ^ step) * rows, 8), rows)
        out[at, :] = ref[...]


def join_parts(parts, bits):
    rows, cols = parts[0].shape
    vmem = pl.BlockSpec(memory_space=pltpu.VMEM)
    return pl.pallas_call(
        functools.partial(join_kernel, bits),
        out_shape=jax.ShapeDtypeStruct((rows * len(parts), cols), F32),
        in_specs=[vmem] * len(parts),
        out_specs=vmem,
        compiler_params=pltpu.CompilerParams(vmem_limit_bytes=8 * 1024 * 1024),
        name="join_parts",
    )(*parts)


def place_kernel(bits, *refs):
    ins, out, sems = refs[:-2], refs[-2], refs[-1]
    rows = ins[0].shape[0]
    place = place_in(bits)
    copies = []
    for step, ref in enumerate(ins):
        at = pl.ds(pl.multiple_of((place ^ step) * rows, 8), rows)
        copies.append(pltpu.make_async_copy(ref, out.at[at, :], sems.at[step]))
    for copy in copies:
        copy.start()
    for copy in copies:
        copy.wait()


def place_parts(parts, bits):
    rows, cols = parts[0].shape
    anywhere = pl.BlockSpec(memory_space=pl.ANY)
    return pl.pallas_call(
        functools.partial(place_kernel, bits),
        out_shape=jax.ShapeDtypeStruct((rows * len(parts), cols), F32),
        in_specs=[anywhere] * len(parts),
        out_specs=anywhere,
        scratch_shapes=[pltpu.SemaphoreType.DMA((len(parts),))],
        compiler_params=pltpu.CompilerParams(vmem_limit_bytes=8 * 1024 * 1024),
        name="place_parts",
    )(*parts)


def together(*values):
    return lax.optimization_barrier(values)


def sum_everywhere(keep, send, scale, grad_low, grad_right, came_right_low):
    narrow, wide = lax.axis_size("narrow"), lax.axis_size("wide")
    bits = [1 << n for n in range((narrow * wide).bit_length() - 1)]
    rest = bits[1:]
    groups = [tuple(rest[n :: (len(rest) + 1) // 2]) for n in range((len(rest) + 1) // 2)]
    cols = grad_low.shape[2] - grad_right.shape[2]
    parts = [keep, swapped(send, bits[0])]
    for n, group in enumerate(groups):
        pieces = add_parts(parts, group)
        if n == 1:
            _, grad_low = together(pieces, grad_low)
            came_low = shifted(grad_low, "narrow", 1)
        parts = [pieces[0]] + [swapped(piece, mask) for piece, mask in zip(pieces[1:], partners(group)[1:])]
        if n == 0:
            parts, came_right_low = together(parts, came_right_low)
    value = add_parts(parts, (), scale)[0]
    for group in reversed(groups):
        if group == groups[0]:
            _, grad_right = together(value, grad_right + came_low[:, :, cols:])
            came_right = shifted(grad_right, "wide", 1)
        parts = [value] + [swapped(value, mask) for mask in partners(group)[1:]]
        if group != groups[0]:
            value = join_parts(parts, group)
    parts = parts + [swapped(part, bits[0]) for part in parts]
    return place_parts(parts, groups[0] + (bits[0],)), came_low[:, :, :cols], came_right, came_right_low


def on_device(object_field, probe, amplitudes, offsets, live):
    extent = probe.shape[2]
    top, whole = together(object_field[:, :extent], object_field)
    right = shifted(top, "wide", -1)
    below = shifted(top, "narrow", -1)
    right_low = shifted(whole[:, extent:], "wide", -1)
    corner = shifted(right, "narrow", -1)
    grad_own, grad_low, grad_right, grad_right_low, keep, send = run_slots(
        offsets, live, object_field, below, right, right_low, corner, probe, amplitudes
    )
    came_right_low = shifted(grad_right_low, "wide", 1)
    total_slots = lax.axis_size("wide") * lax.axis_size("narrow") * offsets.shape[0]
    probe_grad, came_below, came_right, came_right_low = sum_everywhere(
        keep, send, 1.0 / math.sqrt(total_slots), grad_low, grad_right, came_right_low
    )
    rims = jnp.concatenate([came_right, came_right_low], 1)
    object_grad = grad_own.at[:, :extent, :].add(came_below).at[:, :, :extent].add(rims)
    return (object_grad, probe_grad.reshape(probe.shape))


def solution(mesh):
    return jax.shard_map(
        on_device,
        mesh=mesh,
        in_specs=(
            P(None, "narrow", "wide"),
            P(),
            P(("wide", "narrow"), None, None),
            P(("wide", "narrow"), None),
            P(("wide", "narrow")),
        ),
        out_specs=(P(None, "narrow", "wide"), P()),
        check_vma=False,
    )
```

```python
import functools
import math

import jax
import jax.numpy as jnp
import ml_dtypes
import numpy as np
from jax import lax
from jax.experimental import pallas as pl
from jax.experimental.pallas import tpu as pltpu
from jax.sharding import PartitionSpec as P

F32 = jnp.float32
BF16 = jnp.bfloat16
LANES = 128
PAIR = 2


def half_dft(extent):
    half = extent // 2
    blocks = []
    for parity in range(2):
        freq = 2 * np.arange(half)[:, None] + parity
        angles = (freq * np.arange(half)[None, :] % extent) * (2.0 * math.pi / extent)
        cosine = np.cos(angles) / math.sqrt(extent)
        sine = np.sin(angles) / math.sqrt(extent)
        blocks.append(np.block([[cosine, sine], [-sine, cosine]]))
    both = np.stack(blocks)
    return np.stack([both, np.swapaxes(both, 1, 2)]).astype(ml_dtypes.bfloat16)


def parity_order(extent):
    order = np.concatenate([np.arange(0, extent, 2), np.arange(1, extent, 2)])
    matrix = np.zeros((extent, extent), np.float32)
    matrix[order, np.arange(extent)] = 1.0
    return matrix


def dot(a, b):
    return jnp.dot(a, b, preferred_element_type=F32)


def slots_kernel(
    tile_rows, tile_cols, offsets, live, own, below, right, right_low, corner, probe_in, amps, mats, order,
    grad_own, grad_below, grad_corner, grad_right, grad_right_low, probe_keep, probe_send,
    ext, grad, probe, probe_sum, window, part, amp, sorted_amp, waves, inner, far, power, across,
    in_sems, amp_sems, out_sems,
):
    modes = probe.shape[0]
    extent = probe.shape[2]
    half = extent // 2
    rows_step = 32
    wide_cols = extent // LANES + 1
    count = live[0]

    low_rows = slice(tile_rows, tile_rows + extent)
    whole = slice(0, tile_cols)
    rim = slice(tile_cols, tile_cols + extent)
    places = [
        (own, slice(0, tile_rows), whole),
        (below, low_rows, whole),
        (right, slice(0, extent), rim),
        (right_low, slice(extent, tile_rows), rim),
        (corner, low_rows, rim),
    ]

    def strips(array, rows, cols):
        for start in range(0, cols.stop - cols.start, LANES):
            yield array.at[:, :, start : start + LANES], ((slice(None), (cols.start + start) // LANES, rows, slice(None)))

    strip_loads = [(src, at) for array, rows, cols in places for src, at in strips(array, rows, cols)]
    loads = [pltpu.make_async_copy(src, ext.at[at], in_sems.at[n]) for n, (src, at) in enumerate(strip_loads)]
    loads.append(pltpu.make_async_copy(probe_in, probe, in_sems.at[len(loads)]))
    for load in loads:
        load.start()
    grad[...] = jnp.zeros_like(grad)
    probe_sum[...] = jnp.zeros_like(probe_sum)
    for load in loads:
        load.wait()
    lane = lax.broadcasted_iota(jnp.int32, (rows_step, LANES), 1)

    def rows_of(k, c, rows):
        start = (k * 2 + c) * extent
        return slice(start + rows.start, start + rows.stop)

    def take(q, row_at, first_tile, shift):
        back = lax.rem(LANES - shift, LANES)
        for plane in range(2):
            for row in range(0, extent, rows_step):
                rows = pl.ds(row_at + row, rows_step)
                turned = [pltpu.roll(ext[plane, first_tile + c, rows, :], back, 1) for c in range(wide_cols)]
                for c in range(wide_cols - 1):
                    window[q, plane, row : row + rows_step, c * LANES : (c + 1) * LANES] = jnp.where(
                        lane < LANES - shift, turned[c], turned[c + 1]
                    )

    def give(q, row_at, first_tile, shift):
        zero = jnp.zeros((rows_step, LANES), F32)
        for plane in range(2):
            for row in range(0, extent, rows_step):
                rows = pl.ds(row_at + row, rows_step)
                turned = [zero]
                for c in range(wide_cols - 1):
                    turned.append(pltpu.roll(part[q, plane, row : row + rows_step, c * LANES : (c + 1) * LANES], shift, 1))
                turned.append(zero)
                for c in range(wide_cols):
                    grad[plane, first_tile + c, rows, :] += jnp.where(lane >= shift, turned[c + 1], turned[c])

    def psi(k):
        for row in range(0, half, rows_step):
            spans = [slice(base, base + rows_step) for base in (row, half + row)]
            probes = [(probe[k, 0, rows, :], probe[k, 1, rows, :]) for rows in spans]
            for q in range(PAIR):
                waves_at = []
                for rows, (pr, pi) in zip(spans, probes):
                    o_re, o_im = window[q, 0, rows, :], window[q, 1, rows, :]
                    waves_at.append((pr * o_re - pi * o_im, pr * o_im + pi * o_re))
                for c in range(2):
                    rows = slice(c * half + row, c * half + row + rows_step)
                    waves[q, k, 0, rows, :] = (waves_at[0][c] + waves_at[1][c]).astype(BF16)
                    waves[q, k, 1, rows, :] = (waves_at[0][c] - waves_at[1][c]).astype(BF16)

    def left(q, k):
        for a in range(2):
            z = dot(mats[0, a], waves[q, k, a])
            left, right_half = z[:, :half], z[:, half:]
            for b, value in enumerate((left + right_half, left - right_half)):
                value = value.astype(BF16)
                inner[q, k, b, a * half : (a + 1) * half, :half] = value[:half]
                inner[q, k, b, a * half : (a + 1) * half, half:] = value[half:]

    def right(q, k):
        for b in range(2):
            f = dot(inner[q, k, b], mats[1, b])
            far[q, k, b] = f
            own_power = f[:, :half] * f[:, :half] + f[:, half:] * f[:, half:]
            power[q, b] = own_power if k == 0 else power[q, b] + own_power

    def factors(q, used):
        high = amp[q].astype(BF16)
        low = (amp[q] - high.astype(F32)).astype(BF16)
        turned = dot(high, order[...]) + dot(low, order[...])
        for b in range(2):
            sorted_amp[q, b] = turned[:, b * half : (b + 1) * half]
        for b in range(2):
            for a in range(2):
                rows = slice(a * half, (a + 1) * half)
                for_rows = sorted_amp[q, b, pl.ds(a, half, 2), :]
                factor = 2.0 - 2.0 * for_rows * lax.rsqrt(power[q, b, rows] + 0.5)
                power[q, b, rows] = factor if q == 0 else jnp.where(used, factor, 0.0)

    def back_right(q, k):
        ys = []
        for b in range(2):
            factor = power[q, b]
            g = jnp.concatenate([far[q, k, b, :, :half] * factor, far[q, k, b, :, half:] * factor], 1)
            ys.append(dot(g.astype(BF16), mats[0, b]))
        for side, y in enumerate((ys[0] + ys[1], ys[0] - ys[1])):
            y = y.astype(BF16)
            cols = slice(side * half, (side + 1) * half)
            for a in range(2):
                rows = slice(a * half, (a + 1) * half)
                across[q, k, a, :half, cols] = y[rows, :half]
                across[q, k, a, half:, cols] = y[rows, half:]

    def back_left(k):
        vs = [(dot(mats[1, 0], across[q, k, 0]), dot(mats[1, 1], across[q, k, 1])) for q in range(PAIR)]
        for side in range(2):
            rows = slice(side * half, (side + 1) * half)
            pr, pi = probe[k, 0, rows, :], probe[k, 1, rows, :]
            sum_re, sum_im = probe_sum[rows_of(k, 0, rows), :], probe_sum[rows_of(k, 1, rows), :]
            for q, (v0, v1) in enumerate(vs):
                v = v0 + v1 if side == 0 else v0 - v1
                g_re, g_im = v[:half], v[half:]
                o_re, o_im = window[q, 0, rows, :], window[q, 1, rows, :]
                add_re = pr * g_re + pi * g_im
                add_im = pr * g_im - pi * g_re
                part[q, 0, rows, :] = add_re if k == 0 else part[q, 0, rows, :] + add_re
                part[q, 1, rows, :] = add_im if k == 0 else part[q, 1, rows, :] + add_im
                sum_re = sum_re + o_re * g_re + o_im * g_im
                sum_im = sum_im + o_re * g_im - o_im * g_re
            probe_sum[rows_of(k, 0, rows), :] = sum_re
            probe_sum[rows_of(k, 1, rows), :] = sum_im

    @pl.loop(0, (count + PAIR - 1) // PAIR)
    def _(step):
        numbers = [jnp.minimum(step * PAIR + q, count - 1) for q in range(PAIR)]
        amp_loads = [pltpu.make_async_copy(amps.at[n], amp.at[q], amp_sems.at[q]) for q, n in enumerate(numbers)]
        for load in amp_loads:
            load.start()
        places = []
        for q, n in enumerate(numbers):
            col_at = lax.rem(offsets[n, 1], tile_cols)
            places.append((lax.rem(offsets[n, 0], tile_rows), col_at // LANES, lax.rem(col_at, LANES)))
            take(q, *places[q])
        every = [(q, k) for k in range(modes) for q in range(PAIR)]
        for k in range(modes):
            psi(k)
        for q, k in every:
            left(q, k)
        for q, k in every:
            right(q, k)
        for load in amp_loads:
            load.wait()
        for q in range(PAIR):
            factors(q, step * PAIR + q < count)
        for q, k in every:
            back_right(q, k)
        for k in range(modes):
            back_left(k)
        for q in range(PAIR):
            give(q, *places[q])

    own_half = (lax.axis_index("narrow") & 1) * (probe_sum.shape[0] // 2)
    other_half = probe_sum.shape[0] // 2 - own_half
    pairs = [
        (probe_sum.at[pl.ds(pl.multiple_of(start, 8), probe_sum.shape[0] // 2), :], dst)
        for start, dst in ((other_half, probe_send), (own_half, probe_keep))
    ]
    for array, rows, cols in (
        (grad_corner, low_rows, rim),
        (grad_below, low_rows, whole),
        (grad_right, slice(0, extent), rim),
        (grad_right_low, slice(extent, tile_rows), rim),
        (grad_own, slice(0, tile_rows), whole),
    ):
        pairs += [(grad.at[at], dst) for dst, at in strips(array, rows, cols)]
    stores = [pltpu.make_async_copy(src, dst, out_sems.at[n]) for n, (src, dst) in enumerate(pairs)]
    for store in stores:
        store.start()
    for store in stores:
        store.wait()


def run_slots(offsets, live, own, below, right, right_low, corner, probe, amps):
    extent = probe.shape[2]
    modes = probe.shape[0]
    tile_rows, tile_cols = own.shape[1:]
    mats = jnp.asarray(half_dft(extent))
    order = jnp.asarray(parity_order(extent)).astype(BF16)
    smem = pl.BlockSpec(memory_space=pltpu.SMEM)
    vmem = pl.BlockSpec(memory_space=pltpu.VMEM)
    hbm = pl.BlockSpec(memory_space=pltpu.HBM)
    anywhere = pl.BlockSpec(memory_space=pl.ANY)
    tiles_shape = (2, (tile_cols + extent) // LANES, tile_rows + extent, LANES)
    sum_shape = (modes * 2 * extent, extent)
    half_sum = (sum_shape[0] // 2, extent)
    outs = [(2, tile_rows, tile_cols), (2, extent, tile_cols), (2, extent, extent), (2, extent, extent)]
    outs += [(2, tile_rows - extent, extent), half_sum, half_sum]
    return pl.pallas_call(
        functools.partial(slots_kernel, tile_rows, tile_cols),
        out_shape=[jax.ShapeDtypeStruct(shape, F32) for shape in outs],
        in_specs=[smem, smem, hbm] + [anywhere] * 4 + [hbm, hbm, vmem, vmem],
        out_specs=[anywhere] * len(outs),
        scratch_shapes=[
            pltpu.VMEM(tiles_shape, F32),
            pltpu.VMEM(tiles_shape, F32),
            pltpu.VMEM(probe.shape, F32),
            pltpu.VMEM(sum_shape, F32),
            pltpu.VMEM((PAIR, 2, extent, extent), F32),
            pltpu.VMEM((PAIR, 2, extent, extent), F32),
            pltpu.VMEM((PAIR, extent, extent), F32),
            pltpu.VMEM((PAIR, 2, extent, extent // 2), F32),
            pltpu.VMEM((PAIR, modes, 2, extent, extent), BF16),
            pltpu.VMEM((PAIR, modes, 2, extent, extent), BF16),
            pltpu.VMEM((PAIR, modes, 2, extent, extent), F32),
            pltpu.VMEM((PAIR, 2, extent, extent // 2), F32),
            pltpu.VMEM((PAIR, modes, 2, extent, extent), BF16),
            pltpu.SemaphoreType.DMA((4 * tiles_shape[1],)),
            pltpu.SemaphoreType.DMA((PAIR,)),
            pltpu.SemaphoreType.DMA((4 * tiles_shape[1],)),
        ],
        compiler_params=pltpu.CompilerParams(vmem_limit_bytes=44 * 1024 * 1024),
        name="slots",
    )(offsets, live, own, below, right, right_low, corner, probe, amps, mats, order)


def shifted(value, axis, steps):
    count = lax.axis_size(axis)
    first, last = (max(0, -steps), min(count, count - steps))
    return lax.ppermute(value, axis, [(source, source + steps) for source in range(first, last)])


def place_in(bits):
    linear = lax.axis_index("wide") * lax.axis_size("narrow") + lax.axis_index("narrow")
    place = 0
    for n, bit in enumerate(bits):
        place = place + ((linear // bit) % 2) * (1 << n)
    return place


def partners(bits):
    return [sum(bit for n, bit in enumerate(bits) if step >> n & 1) for step in range(1 << len(bits))]


def swapped(value, mask):
    count = lax.axis_size("wide") * lax.axis_size("narrow")
    return lax.ppermute(value, ("wide", "narrow"), [(source, source ^ mask) for source in range(count)])


def add_kernel(bits, count, scale, *refs):
    ins, outs = refs[:count], refs[count:]
    rows = outs[0].shape[0]
    place = place_in(bits)
    for step, out in enumerate(outs):
        at = pl.ds(pl.multiple_of((place ^ step) * rows, 8), rows)
        total = sum(ref[at, :] for ref in ins)
        out[...] = total if scale is None else total * scale


def add_parts(parts, bits, scale=None):
    count = 1 << len(bits)
    rows, cols = parts[0].shape
    vmem = pl.BlockSpec(memory_space=pltpu.VMEM)
    return pl.pallas_call(
        functools.partial(add_kernel, bits, len(parts), scale),
        out_shape=[jax.ShapeDtypeStruct((rows // count, cols), F32)] * count,
        in_specs=[vmem] * len(parts),
        out_specs=[vmem] * count,
        compiler_params=pltpu.CompilerParams(vmem_limit_bytes=8 * 1024 * 1024),
        name="add_parts",
    )(*parts)


def join_kernel(bits, *refs):
    ins, out = refs[:-1], refs[-1]
    rows = ins[0].shape[0]
    place = place_in(bits)
    for step, ref in enumerate(ins):
        at = pl.ds(pl.multiple_of((place ^ step) * rows, 8), rows)
        out[at, :] = ref[...]


def join_parts(parts, bits):
    rows, cols = parts[0].shape
    vmem = pl.BlockSpec(memory_space=pltpu.VMEM)
    return pl.pallas_call(
        functools.partial(join_kernel, bits),
        out_shape=jax.ShapeDtypeStruct((rows * len(parts), cols), F32),
        in_specs=[vmem] * len(parts),
        out_specs=vmem,
        compiler_params=pltpu.CompilerParams(vmem_limit_bytes=8 * 1024 * 1024),
        name="join_parts",
    )(*parts)


def place_kernel(bits, *refs):
    ins, out, sems = refs[:-2], refs[-2], refs[-1]
    rows = ins[0].shape[0]
    place = place_in(bits)
    copies = []
    for step, ref in enumerate(ins):
        at = pl.ds(pl.multiple_of((place ^ step) * rows, 8), rows)
        copies.append(pltpu.make_async_copy(ref, out.at[at, :], sems.at[step]))
    for copy in copies:
        copy.start()
    for copy in copies:
        copy.wait()


def place_parts(parts, bits):
    rows, cols = parts[0].shape
    anywhere = pl.BlockSpec(memory_space=pl.ANY)
    return pl.pallas_call(
        functools.partial(place_kernel, bits),
        out_shape=jax.ShapeDtypeStruct((rows * len(parts), cols), F32),
        in_specs=[anywhere] * len(parts),
        out_specs=anywhere,
        scratch_shapes=[pltpu.SemaphoreType.DMA((len(parts),))],
        compiler_params=pltpu.CompilerParams(vmem_limit_bytes=8 * 1024 * 1024),
        name="place_parts",
    )(*parts)


def together(*values):
    return lax.optimization_barrier(values)


def sum_everywhere(keep, send, scale, grad_right, came_corner, came_right_low, grad_below):
    narrow, wide = lax.axis_size("narrow"), lax.axis_size("wide")
    bits = [1 << n for n in range((narrow * wide).bit_length() - 1)]
    rest = bits[1:]
    groups = [tuple(rest[n :: (len(rest) + 1) // 2]) for n in range((len(rest) + 1) // 2)]
    parts = [keep, swapped(send, bits[0])]
    for n, group in enumerate(groups):
        pieces = add_parts(parts, group)
        if n == 0:
            _, grad_right = together(pieces, grad_right)
            came_right = shifted(grad_right + came_corner, "wide", 1)
        if n == 1:
            _, grad_below = together(pieces, grad_below)
            came_below = shifted(grad_below, "narrow", 1)
        parts = [pieces[0]] + [swapped(piece, mask) for piece, mask in zip(pieces[1:], partners(group)[1:])]
        if n == 0:
            parts, came_right_low = together(parts, came_right_low)
    value = add_parts(parts, (), scale)[0]
    for group in reversed(groups):
        if group == groups[0]:
            value, came_right, came_below = together(value, came_right, came_below)
        parts = [value] + [swapped(value, mask) for mask in partners(group)[1:]]
        if group != groups[0]:
            value = join_parts(parts, group)
    parts = parts + [swapped(part, bits[0]) for part in parts]
    return place_parts(parts, groups[0] + (bits[0],)), came_below, came_right, came_right_low


def on_device(object_field, probe, amplitudes, offsets, live):
    extent = probe.shape[2]
    top, whole = together(object_field[:, :extent], object_field)
    right = shifted(top, "wide", -1)
    below = shifted(top, "narrow", -1)
    right_low = shifted(whole[:, extent:], "wide", -1)
    corner = shifted(right, "narrow", -1)
    grad_own, grad_below, grad_corner, grad_right, grad_right_low, keep, send = run_slots(
        offsets, live, object_field, below, right, right_low, corner, probe, amplitudes
    )
    came_right_low = shifted(grad_right_low, "wide", 1)
    came_corner = shifted(grad_corner, "narrow", 1)
    total_slots = lax.axis_size("wide") * lax.axis_size("narrow") * offsets.shape[0]
    probe_grad, came_below, came_right, came_right_low = sum_everywhere(
        keep, send, 1.0 / math.sqrt(total_slots), grad_right, came_corner, came_right_low, grad_below
    )
    rims = jnp.concatenate([came_right, came_right_low], 1)
    object_grad = grad_own.at[:, :extent, :].add(came_below).at[:, :, :extent].add(rims)
    return (object_grad, probe_grad.reshape(probe.shape))


def solution(mesh):
    return jax.shard_map(
        on_device,
        mesh=mesh,
        in_specs=(
            P(None, "narrow", "wide"),
            P(),
            P(("wide", "narrow"), None, None),
            P(("wide", "narrow"), None),
            P(("wide", "narrow")),
        ),
        out_specs=(P(None, "narrow", "wide"), P()),
        check_vma=False,
    )
```
